32 devices in a mesh: dp: 8 (over z, x), tensor: 4 (over y, core).
Axes of the slice: x: 2, y: 2, z: 4, core: 2. Of those that a mesh axis runs over, the one named last changes fastest.
Arguments:
- inputs: bfloat16 [8, 1024, 768], P('dp'), may hold values from -6 to 6
- segments: int32 [8, 1024], P('dp'), may hold values from 0 to 3, never falling along the last dimension, each value on 1 to 512 neighbouring positions
- cotangent: bfloat16 [8, 1024, 768], P('dp'), may hold values from -6 to 6
- owner: int32 [768], replicated, may hold values from 0 to 7, as said below
- masters: float32 [4, 768, 48, 48], P('tensor', 'dp')
- first_moment: float32 [4, 768, 48, 48], P('tensor', 'dp')
- second_moment: float32 [4, 768, 48, 48], P('tensor', 'dp'), as said below
- left_stats: float32 [4, 768, 48, 48], P('tensor', 'dp'), as said below
- right_stats: float32 [4, 768, 48, 48], P('tensor', 'dp'), as said below
- left_basis: float32 [4, 768, 48, 48], P('tensor', 'dp'), as said below
- right_basis: float32 [4, 768, 48, 48], P('tensor', 'dp'), as said below
- norm_master: float32 [3072], P('dp')
- norm_first: float32 [3072], P('dp')
- norm_second: float32 [3072], P('dp'), as said below
Outputs:
- output: bfloat16 [8, 1024, 768], P('dp')
- input_grad: float32 [8, 1024, 768], P('dp')
- new_first: float32 [4, 768, 48, 48], P('tensor', 'dp')
- new_second: float32 [4, 768, 48, 48], P('tensor', 'dp')
- new_master: float32 [4, 768, 48, 48], P('tensor', 'dp')
- new_left_stats: float32 [4, 768, 48, 48], P('tensor', 'dp')
- new_right_stats: float32 [4, 768, 48, 48], P('tensor', 'dp')
- new_left_basis: float32 [4, 768, 48, 48], P('tensor', 'dp')
- renewed_right_rotation: float32 [4, 768, 48, 48], P('tensor', 'dp')
- new_norm_first: float32 [3072], P('dp')
- new_norm_second: float32 [3072], P('dp')
- new_norm: float32 [3072], P('dp')
The draws below stay inside these ranges and needn't reach their ends.
Inputs may be any that keep to these rules, and one draw needn't show every extreme that they name: `owner`: every data index owns exactly 96 blocks. `segments`: ids never fall along a row; a row holds 4 documents of at most 512 tokens, one of exactly that many. `left_basis`: each block is orthogonal. `right_basis`: each block is orthogonal. `left_stats`: each block is symmetric positive definite. `right_stats`: each block is symmetric positive definite. `second_moment`: Positive. `norm_second`: Positive.
All inputs are finite; a program needn't handle non-finite values.
Results may differ from the reference program's by a relative error of at most 0.012.
Values may be sent and summed in bfloat16 or wider, within the bound.
A program may use at most 192 MiB of HBM per device.

```python
import math
import jax
import jax.numpy as jnp
import numpy as np
from jax import lax

D = 768
HEADS = 12
HD = 64
FF = 3072
SEQ = 1024
DOCS = 4
BS = 48
STEP = 10
ROWS = 8
NBLK = 768
BLK_DEV = 96
N_DP = 8
N_TENSOR = 4


def shared_owner(key):
    spread = jnp.arange(NBLK, dtype=jnp.int32) % N_DP
    return jax.random.permutation(jax.random.fold_in(key, 7), spread)


def slot_kinds(key):
    owner = shared_owner(key)
    index = jnp.arange(NBLK, dtype=jnp.int32)
    earlier = (owner[:, None] == owner[None, :]) & (index[None, :] < index[:, None])
    rank = jnp.sum(earlier.astype(jnp.int32), axis=1).astype(jnp.int32)
    slots = (owner * BLK_DEV + rank).astype(jnp.int32)
    inverse = jnp.sum(jnp.where(slots[None, :] == index[:, None], index[None, :], 0), axis=1).astype(jnp.int32)
    columns = inverse % (NBLK // (D // BS)) * BS
    attn = D // N_TENSOR
    mlp = FF // N_TENSOR
    kind = (columns >= 3 * attn).astype(jnp.int32) + (columns >= 3 * attn + mlp).astype(jnp.int32) + (columns >= 4 * attn + mlp).astype(jnp.int32)
    return kind


def pick(kind, table):
    return jnp.where(kind == 0, table[0], jnp.where(kind == 1, table[1], jnp.where(kind == 2, table[2], table[3]))).astype(jnp.float32)


def grad_size(kind):
    return math.sqrt(ROWS * SEQ) * pick(kind, (0.5, 0.3, 0.15, 0.65))[None, :, None, None]


def stats_blocks(key, kind):
    first_key, second_key = jax.random.split(key)
    size = 0.0526 * BS * grad_size(kind) ** 2
    diagonal = jnp.exp(jax.random.uniform(first_key, (N_TENSOR, NBLK, BS), jnp.float32, math.log(2.0), math.log(8.0)))
    noise = jax.random.uniform(second_key, (N_TENSOR, NBLK, BS, BS), jnp.float32, -1.0, 1.0)
    symmetric = (noise + jnp.swapaxes(noise, -1, -2)) * 0.5 * (1.8 / BS)
    identity = jnp.eye(BS, dtype=jnp.float32)
    return size * (symmetric * (1.0 - identity) + diagonal[..., None] * identity)


def basis_blocks(key):
    keys = jax.random.split(key, 4)
    shape = (N_TENSOR, NBLK, BS)
    first_vec = jax.random.normal(keys[0], shape, jnp.float32)
    second_vec = jax.random.normal(keys[1], shape, jnp.float32)
    first_len = jnp.sum(first_vec * first_vec, axis=-1)[..., None, None]
    second_len = jnp.sum(second_vec * second_vec, axis=-1)[..., None, None]
    cross = jnp.sum(first_vec * second_vec, axis=-1)[..., None, None]
    identity = jnp.eye(BS, dtype=jnp.float32)
    reflect = identity - 2.0 * first_vec[..., :, None] * first_vec[..., None, :] / first_len
    reflect = reflect - 2.0 * second_vec[..., :, None] * second_vec[..., None, :] / second_len
    reflect = reflect + 4.0 * cross * first_vec[..., :, None] * second_vec[..., None, :] / (first_len * second_len)
    scores = jax.random.randint(keys[2], shape, 0, BS) * BS + jnp.arange(BS, dtype=jnp.int32)
    order = jnp.argsort(scores, axis=-1)
    rows = jnp.take_along_axis(reflect, jnp.broadcast_to(order[..., None], reflect.shape), axis=-2)
    signs = (jax.random.randint(keys[3], shape, 0, 2) * 2 - 1).astype(jnp.float32)
    return rows * signs[..., None]


def draw_owner(key, part):
    return shared_owner(key)


def draw_masters(key, part):
    kind = slot_kinds(key)
    key = jax.random.fold_in(key, 11)
    scale = pick(kind, (D ** (-0.5), D ** (-0.5), 4.0 * D ** (-0.5), FF ** (-0.5)))[None, :, None, None]
    return jnp.clip(jax.random.normal(key, (N_TENSOR, NBLK, BS, BS), jnp.float32), -4.0, 4.0) * scale


def draw_first_moment(key, part):
    kind = slot_kinds(key)
    key = jax.random.fold_in(key, 12)
    return jnp.clip(jax.random.normal(key, (N_TENSOR, NBLK, BS, BS), jnp.float32), -4.0, 4.0) * 0.111 * grad_size(kind)


def draw_second_moment(key, part):
    kind = slot_kinds(key)
    key = jax.random.fold_in(key, 13)
    factor = jnp.exp(jax.random.uniform(key, (N_TENSOR, NBLK, BS, BS), jnp.float32, 0.0, math.log(4.0)))
    return factor * 0.0526 * grad_size(kind) ** 2


def draw_left_stats(key, part):
    kind = slot_kinds(key)
    key = jax.random.fold_in(key, 14)
    return stats_blocks(key, kind)


def draw_right_stats(key, part):
    kind = slot_kinds(key)
    key = jax.random.fold_in(key, 15)
    return stats_blocks(key, kind)


def draw_left_basis(key, part):
    key = jax.random.fold_in(key, 16)
    return basis_blocks(key)


def draw_right_basis(key, part):
    key = jax.random.fold_in(key, 17)
    return basis_blocks(key)


def draw_norm_master(key, part):
    key = jax.random.fold_in(key, 18)
    first_key, second_key = jax.random.split(key)
    quarter = jnp.arange(4 * D, dtype=jnp.int32) // D
    gains = 1.0 + jax.random.uniform(first_key, (4 * D,), jnp.float32, -0.3, 0.3)
    biases = 0.2 * jnp.clip(jax.random.normal(second_key, (4 * D,), jnp.float32), -4.0, 4.0)
    return jnp.where(quarter % 2 == 0, gains, biases)


def draw_norm_first(key, part):
    key = jax.random.fold_in(key, 19)
    return jnp.clip(jax.random.normal(key, (4 * D,), jnp.float32), -4.0, 4.0) * 0.111 * math.sqrt(ROWS * SEQ)


def draw_norm_second(key, part):
    key = jax.random.fold_in(key, 20)
    factor = jnp.exp(jax.random.uniform(key, (4 * D,), jnp.float32, 0.0, math.log(4.0)))
    return factor * 0.0526 * ROWS * SEQ


def strengthened(array, own_key, source, target, blocks, factor):
    def block_of(dim):
        return (jnp.arange(array.shape[dim]) // (array.shape[dim] // blocks)).reshape((-1,) + (1,) * (array.ndim - 1 - dim))

    near = jax.random.permutation(own_key, blocks)[block_of(target)]
    second = (block_of(target) + blocks // 2) % blocks
    return jnp.where((block_of(source) == near) | (block_of(source) == second), factor * array, array)


def block_levels(key, dims, shards, low, high):
    def one(dim, shards_of):
        heights = jax.random.uniform(jax.random.fold_in(jax.random.fold_in(key, 6), dim), (shards_of,), jnp.float32, low / len(shards), high / len(shards))
        return jnp.repeat(jnp.exp(heights), dims[dim] // shards_of).reshape((-1,) + (1,) * (len(dims) - dim - 1))

    factor_of = one(*shards[0])
    for cut in shards[1:]:
        factor_of = factor_of * one(*cut)
    return factor_of


def profile(count, total, reach, skew):
    portions = [(1 << 20) // math.isqrt(standing ** skew) + 1 for standing in range(2, count + 1)]
    rest, holding = total - reach - (count - 1), [1] * (count - 1)
    while rest > 0:
        movable = [i for i in range(count - 1) if holding[i] < reach]
        mass, remaining = sum([portions[i] for i in movable]), rest
        for i in movable:
            addition = min(reach - holding[i], max(1, remaining * portions[i] // mass), rest)
            holding[i] = holding[i] + addition
            rest = rest - addition
    return np.array([reach] + holding)


def uneven(stream_key, amount, total, reach, lean):
    if amount == 2:
        one = jax.random.randint(stream_key, (), max(1, total - reach), min(reach, total - 1) + 1)
        return jnp.stack([one, total - one])
    lengths = jnp.asarray(profile(amount, total, reach, lean), jnp.int32)
    couples = (amount - 1) // 2
    donor, taker = lengths[1:1 + 2 * couples:2], lengths[2:2 + 2 * couples:2]
    slack = jnp.minimum(donor - 1, reach - taker)
    shifted = jax.random.randint(jax.random.fold_in(stream_key, 1), (couples,), 0, 1 << 20) % (slack + 1)
    lengths = lengths.at[1:1 + 2 * couples:2].set(donor - shifted).at[2:2 + 2 * couples:2].set(taker + shifted)
    return lengths[jax.random.permutation(jax.random.fold_in(stream_key, 2), amount)]


def gaussian(rng, extent, deviation, limit, cuts=(), kind=jnp.bfloat16):
    factor_of = block_levels(rng, extent, cuts, -0.22, 0.18) if cuts else 1.0
    drawn = jax.random.normal(rng, extent, jnp.float32) * deviation * factor_of
    return jnp.minimum(jnp.maximum(drawn, -limit), limit).astype(kind)


def noise_with(key, dims, scale, most, cuts, heavy, kind=jnp.bfloat16):
    array = scale * jax.random.normal(key, dims, jnp.float32)
    if cuts:
        array = array * block_levels(key, dims, cuts, -0.22, 0.18)
    return jnp.clip(strengthened(array, jax.random.fold_in(key, 3), *heavy), -most, most).astype(kind)


def setup_inputs(seed: int = 0) -> dict:
    key_of = jax.random.split(jax.random.key(seed), 15)
    inputs = gaussian(key_of[0], (ROWS, SEQ, D), 1.0, 6.0, ((0, 8),))
    segments = jax.vmap(lambda own: jnp.searchsorted(jnp.cumsum(uneven(own, DOCS, SEQ, SEQ // 2, 0)), jnp.arange(SEQ), side="right"))(jax.random.split(key_of[1], ROWS)).reshape((ROWS, SEQ)).astype(jnp.int32)
    cotangent = noise_with(key_of[2], (ROWS, SEQ, D), 1.0, 6.0, ((0, 8),), (0, 2, 8, 2.0))
    owner = draw_owner(jax.random.fold_in(key_of[14], 71), 0)
    masters = draw_masters(jax.random.fold_in(key_of[14], 71), 0)
    first_moment = draw_first_moment(jax.random.fold_in(key_of[14], 71), 0)
    second_moment = draw_second_moment(jax.random.fold_in(key_of[14], 71), 0)
    left_stats = draw_left_stats(jax.random.fold_in(key_of[14], 71), 0)
    right_stats = draw_right_stats(jax.random.fold_in(key_of[14], 71), 0)
    left_basis = draw_left_basis(jax.random.fold_in(key_of[14], 71), 0)
    right_basis = draw_right_basis(jax.random.fold_in(key_of[14], 71), 0)
    norm_master = draw_norm_master(jax.random.fold_in(key_of[14], 71), 0)
    norm_first = draw_norm_first(jax.random.fold_in(key_of[14], 71), 0)
    norm_second = draw_norm_second(jax.random.fold_in(key_of[14], 71), 0)
    return {"inputs": inputs, "segments": segments, "cotangent": cotangent, "owner": owner, "masters": masters, "first_moment": first_moment, "second_moment": second_moment, "left_stats": left_stats, "right_stats": right_stats, "left_basis": left_basis, "right_basis": right_basis, "norm_master": norm_master, "norm_first": norm_first, "norm_second": norm_second}


@jax.custom_vjp
def low(v):
    return lax.optimization_barrier(v.astype(jnp.bfloat16)).astype(jnp.float32)

@jax.custom_vjp
def low_back(v):
    return v

def low_keep(v):
    return (low(v), None)

def low_pass(kept, grad):
    return (grad,)

def back_keep(v):
    return (v, None)

def back_low(kept, grad):
    return (low(grad),)
low.defvjp(low_keep, low_pass)
low_back.defvjp(back_keep, back_low)
highest = lax.Precision.HIGHEST
norm_eps = 1e-05
beta_one = 0.9
beta_two = 0.95
beta_stats = 0.95
learn_rate = 0.03
norm_rate = 0.4
weight_decay = 0.01
adam_eps = 1e-08

def shift_for(length):
    return math.log(length / 8.0)

def block_slots(owner, per_dev):
    count = owner.shape[0]
    index = jnp.arange(count, dtype=jnp.int32)
    earlier = (owner[:, None] == owner[None, :]) & (index[None, :] < index[:, None])
    rank = lax.optimization_barrier(jnp.sum(earlier.astype(jnp.int32), axis=1)).astype(jnp.int32)
    slots = (owner * per_dev + rank).astype(jnp.int32)
    inverse = lax.optimization_barrier(jnp.sum(jnp.where(slots[None, :] == index[:, None], index[None, :], 0), axis=1)).astype(jnp.int32)
    return (slots, inverse)

def blocks_to_matrix(blocks, grid_rows):
    block = blocks.shape[-1]
    grid_cols = blocks.shape[0] // grid_rows
    return blocks.reshape(grid_rows, grid_cols, block, block).transpose(0, 2, 1, 3).reshape(grid_rows * block, grid_cols * block)

def matrix_to_blocks(weight_matrix, block):
    grid_rows = weight_matrix.shape[0] // block
    grid_cols = weight_matrix.shape[1] // block
    return weight_matrix.reshape(grid_rows, block, grid_cols, block).transpose(0, 2, 1, 3).reshape(grid_rows * grid_cols, block, block)

def normalize(rows):
    centered = rows - lax.optimization_barrier(jnp.mean(rows, axis=-1, keepdims=True))
    spread = lax.optimization_barrier(jnp.mean(centered * centered, axis=-1, keepdims=True))
    return centered * lax.rsqrt(spread + norm_eps)

def matmul(left, right):
    return jnp.dot(left, right, precision=highest)

def row_masks(row_seg):
    position = jnp.arange(row_seg.shape[0], dtype=jnp.int32)
    same = row_seg[:, None] == row_seg[None, :]
    return (same & (position[None, :] <= position[:, None]), same & (position[None, :] < position[:, None]))

def penalty_from(first_raw, strict):
    picks = jnp.where(strict, jax.nn.softplus(first_raw - shift_for(first_raw.shape[0])), 0.0)
    running = jnp.cumsum(picks, axis=0)
    return jnp.concatenate([jnp.zeros((1, picks.shape[1]), picks.dtype), running[:-1]], axis=0)

def row_forward(row, row_seg, w_query, w_key, w_value, w_out, w_up, w_down, norms):
    length = row.shape[0]
    normed_one = low(normalize(row) * norms[0] + norms[1])
    queries = low_back(low(matmul(normed_one, w_query)))
    keys = low_back(low(matmul(normed_one, w_key)))
    values = low_back(low(matmul(normed_one, w_value)))

    def heads_of(piece):
        return piece.reshape(length, HEADS, HD).transpose(1, 0, 2)
    raw = low_back(jnp.einsum('hqd,hkd->hqk', heads_of(queries), heads_of(keys), precision=highest) * HD ** (-0.5))
    allowed, strict = row_masks(row_seg)
    penalty = low(penalty_from(raw[0], strict))
    logits = jnp.where(allowed[None], raw - penalty[None], -1e+30)
    top = lax.optimization_barrier(jnp.max(logits, axis=-1, keepdims=True))
    weights = jnp.exp(logits - top)
    probs = weights / lax.optimization_barrier(jnp.sum(weights, axis=-1, keepdims=True))
    mixed = jnp.einsum('hqk,hkd->hqd', low(probs), heads_of(values), precision=highest)
    attention_output = low_back(low(mixed.transpose(1, 0, 2).reshape(length, HEADS * HD)))
    resid = row + low_back(matmul(attention_output, w_out))
    normed_two = low(normalize(resid) * norms[2] + norms[3])
    up_pre = low_back(matmul(normed_two, w_up))
    activated = low(jax.nn.gelu(up_pre, approximate=True))
    return resid + low_back(matmul(activated, w_down))

def batch_prod(left, right):
    return jnp.einsum('nij,njk->nik', left, right, precision=highest)

def swap_last(weight_matrix):
    return jnp.swapaxes(weight_matrix, -1, -2)

def orthonormal(weight_matrix):
    gram = batch_prod(swap_last(weight_matrix), weight_matrix)
    factor = jnp.linalg.cholesky(gram)
    solved = jax.scipy.linalg.solve_triangular(factor, swap_last(weight_matrix), lower=True)
    return swap_last(solved)

def soap_update(grad, master, first, second, left_stats, right_stats, left_basis, right_basis):
    shape = grad.shape
    block = shape[-1]
    flat = [item.reshape(-1, block, block) for item in (grad, master, first, second, left_stats, right_stats, left_basis, right_basis)]
    grad, master, first, second, left_stats, right_stats, left_basis, right_basis = flat
    new_left = beta_stats * left_stats + (1.0 - beta_stats) * batch_prod(grad, swap_last(grad))
    new_right = beta_stats * right_stats + (1.0 - beta_stats) * batch_prod(swap_last(grad), grad)
    rotated = batch_prod(batch_prod(swap_last(left_basis), grad), right_basis)
    new_first = beta_one * first + (1.0 - beta_one) * rotated
    new_second = beta_two * second + (1.0 - beta_two) * rotated * rotated
    direction = new_first / (1.0 - beta_one ** STEP) / (jnp.sqrt(new_second / (1.0 - beta_two ** STEP)) + adam_eps)
    moved = batch_prod(batch_prod(left_basis, direction), swap_last(right_basis))
    new_master = master - learn_rate * (moved + weight_decay * master)
    left_next = orthonormal(batch_prod(new_left, left_basis))
    right_next = orthonormal(batch_prod(new_right, right_basis))
    results = (new_first, new_second, new_master, new_left, new_right, left_next, right_next)
    return tuple((item.reshape(shape) for item in results))

def norm_update(grad, master, first, second):
    new_first = beta_one * first + (1.0 - beta_one) * grad
    new_second = beta_two * second + (1.0 - beta_two) * grad * grad
    direction = new_first / (1.0 - beta_one ** STEP) / (jnp.sqrt(new_second / (1.0 - beta_two ** STEP)) + adam_eps)
    return (new_first, new_second, master - norm_rate * direction)

def reference(inputs, segments, cotangent, owner, masters, first_moment, second_moment, left_stats, right_stats, left_basis, right_basis, norm_master, norm_first, norm_second):
    slots, inverse = block_slots(owner, BLK_DEV)
    grid_rows = D // BS
    rank_attn = D // N_TENSOR
    rank_mlp = FF // N_TENSOR
    edges = [0, rank_attn, 2 * rank_attn, 3 * rank_attn, 3 * rank_attn + rank_mlp, 4 * rank_attn + rank_mlp, 4 * rank_attn + 2 * rank_mlp]
    matrices = []
    for rank in range(N_TENSOR):
        stored = masters[rank].astype(jnp.bfloat16).astype(jnp.float32)
        matrices.append(blocks_to_matrix(jnp.take(stored, slots, axis=0), grid_rows))
    pieces = [[weight_matrix[:, edges[place]:edges[place + 1]] for weight_matrix in matrices] for place in range(6)]
    w_query = jnp.concatenate(pieces[0], axis=1)
    w_key = jnp.concatenate(pieces[1], axis=1)
    w_value = jnp.concatenate(pieces[2], axis=1)
    w_up = jnp.concatenate(pieces[3], axis=1)
    w_out = jnp.concatenate([piece.T for piece in pieces[4]], axis=0)
    w_down = jnp.concatenate([piece.T for piece in pieces[5]], axis=0)
    norms = norm_master.astype(jnp.bfloat16).astype(jnp.float32).reshape(4, D)
    params = (w_query, w_key, w_value, w_out, w_up, w_down, norms)
    zeros = tuple((jnp.zeros_like(item) for item in params))

    def step(totals, packed):
        row_in, row_seg, row_back = packed

        def forward(row, *weights):
            return row_forward(row, row_seg, *weights)
        result, pull = jax.vjp(forward, row_in.astype(jnp.float32), *params)
        grads = pull(row_back.astype(jnp.float32))
        totals = tuple((total + grad for total, grad in zip(totals, grads[1:])))
        return (totals, (result.astype(jnp.bfloat16), grads[0]))
    totals, (output, input_grad) = lax.scan(step, zeros, (inputs, segments, cotangent))
    grad_query, grad_key, grad_value, grad_out, grad_up, grad_down, grad_norms = totals
    stored_grads = []
    for rank in range(N_TENSOR):
        attn_cols = slice(rank * rank_attn, (rank + 1) * rank_attn)
        mlp_cols = slice(rank * rank_mlp, (rank + 1) * rank_mlp)
        weight_matrix = jnp.concatenate([grad_query[:, attn_cols], grad_key[:, attn_cols], grad_value[:, attn_cols], grad_up[:, mlp_cols], grad_out[attn_cols, :].T, grad_down[mlp_cols, :].T], axis=1)
        stored_grads.append(jnp.take(matrix_to_blocks(weight_matrix, BS), inverse, axis=0))
    grads = jnp.stack(stored_grads)
    new_first, new_second, new_master, new_left, new_right, left_next, right_next = soap_update(grads, masters, first_moment, second_moment, left_stats, right_stats, left_basis, right_basis)
    norm_first_new, norm_second_new, norm_new = norm_update(grad_norms.reshape(-1), norm_master, norm_first, norm_second)
    return (output, input_grad, new_first, new_second, new_master, new_left, new_right, left_next, right_next, norm_first_new, norm_second_new, norm_new)
```

```python
import functools
import math

import jax
import jax.numpy as jnp
from jax import lax
from jax.experimental import pallas as pl
from jax.experimental.pallas import tpu as pltpu
from jax.sharding import PartitionSpec as P

HD = 64
STEP = 10
F32 = jnp.float32
BF16 = jnp.bfloat16


highest = lax.Precision.HIGHEST
norm_eps = 1e-05
beta_one = 0.9
beta_two = 0.95
beta_stats = 0.95
learn_rate = 0.03
norm_rate = 0.4
weight_decay = 0.01
adam_eps = 1e-08


def spread(shard, axis, root):
    mine = lax.axis_index(axis) == root
    return lax.psum(jnp.where(mine, shard, jnp.zeros_like(shard)), axis)


def entering(part, axis, combine, identity):
    count = lax.axis_size(axis)
    place = lax.axis_index(axis)
    ahead = count - 1 - place
    gathered = lax.all_gather(part, axis)
    state = jnp.zeros_like(part) + jnp.asarray(identity, part.dtype)

    def one(lap, state):
        source = count - 1 - lap
        return combine(state, lax.dynamic_index_in_dim(gathered, source, 0, False))

    return lax.fori_loop(0, ahead, one, state)


def shift_for(length):
    return math.log(length / 8.0)


def block_slots(owner, per_dev):
    count = owner.shape[0]
    index = jnp.arange(count, dtype=jnp.int32)
    earlier = (owner[:, None] == owner[None, :]) & (index[None, :] < index[:, None])
    rank = jnp.sum(earlier.astype(jnp.int32), axis=1)
    slots = owner * per_dev + rank
    inverse = jnp.sum(jnp.where(slots[None, :] == index[:, None], index[None, :], 0), axis=1)
    return (slots, inverse)


def blocks_to_matrix(blocks, grid_rows):
    block = blocks.shape[-1]
    grid_cols = blocks.shape[0] // grid_rows
    return (
        blocks.reshape(grid_rows, grid_cols, block, block)
        .transpose(0, 2, 1, 3)
        .reshape(grid_rows * block, grid_cols * block)
    )


def matrix_to_blocks(weight_matrix, block):
    grid_rows = weight_matrix.shape[0] // block
    grid_cols = weight_matrix.shape[1] // block
    return (
        weight_matrix.reshape(grid_rows, block, grid_cols, block)
        .transpose(0, 2, 1, 3)
        .reshape(grid_rows * grid_cols, block, block)
    )


def normalize(rows):
    centered = rows - jnp.mean(rows, axis=-1, keepdims=True)
    inverse_std = lax.rsqrt(jnp.mean(centered * centered, axis=-1, keepdims=True) + norm_eps)
    return (centered * inverse_std, inverse_std)


def norm_back(plain, inverse_std, grad):
    return inverse_std * (
        grad
        - jnp.mean(grad, axis=-1, keepdims=True)
        - plain * jnp.mean(grad * plain, axis=-1, keepdims=True)
    )


def contract_rows(left, right):
    return lax.dot_general(
        left, right, (((0,), (0,)), ((), ())), preferred_element_type=jnp.float32
    )


def contract_cols(left, right):
    return lax.dot_general(
        left, right, (((1,), (1,)), ((), ())), preferred_element_type=jnp.float32
    )


def row_masks(row_seg):
    position = jnp.arange(row_seg.shape[0], dtype=jnp.int32)
    same = row_seg[:, None] == row_seg[None, :]
    return (
        same & (position[None, :] <= position[:, None]),
        same & (position[None, :] < position[:, None]),
    )


def penalty_from(first_raw, strict):
    picks = jnp.where(strict, jax.nn.softplus(first_raw - shift_for(first_raw.shape[0])), 0.0)
    running = jnp.cumsum(picks, axis=0)
    return jnp.concatenate([jnp.zeros((1, picks.shape[1]), picks.dtype), running[:-1]], axis=0)


def later_sums(grads):
    suffix = jnp.cumsum(grads[::-1], axis=0)[::-1]
    return jnp.concatenate([suffix[1:], jnp.zeros((1, suffix.shape[1]), suffix.dtype)], axis=0)


def append_column_block(earlier, latter):
    return earlier + latter


def split_heads(row_proj, rank_attn):
    length = row_proj.shape[0]

    def heads_of(piece):
        return piece.reshape(length, -1, HD).transpose(1, 0, 2)

    return (
        heads_of(row_proj[:, :rank_attn]),
        heads_of(row_proj[:, rank_attn : 2 * rank_attn]),
        heads_of(row_proj[:, 2 * rank_attn :]),
    )


def merge_heads(heads):
    return heads.transpose(1, 0, 2).reshape(heads.shape[1], -1)


def split3(v):
    hi = v.astype(BF16)
    return hi, (v - hi.astype(F32)).astype(BF16)

def prod(left, right, dims):
    lh, ll = left
    rh, rl = right
    spec = (dims, ((), ()))
    def one(a, b):
        return lax.dot_general(a, b, spec, preferred_element_type=F32)
    return one(lh, rh) + (one(lh, rl) + one(ll, rh))

NN = ((1,), (0,))
NT = ((1,), (1,))
TN = ((0,), (0,))

def soap_kernel(count, chunk, block, g_ref, m_ref, f_ref, s_ref, l_ref, r_ref, ql_ref, qr_ref,
                nf_ref, ns_ref, nm_ref, nl_ref, nr_ref, bl_ref, br_ref, a_scr, t_scr):
    step = pl.program_id(0)
    tiles = block // 8
    for c in range(chunk):
        g = g_ref[c]
        ql, qr = split3(ql_ref[c]), split3(qr_ref[c])
        gs = split3(g)
        gt = split3(g.T)
        new_left = beta_stats * l_ref[c] + (1.0 - beta_stats) * prod(gs, gs, NT)
        new_right = beta_stats * r_ref[c] + (1.0 - beta_stats) * prod(gt, gt, NT)
        nl_ref[c] = new_left
        nr_ref[c] = new_right
        half = prod(gt, ql, NN)
        rot = prod(split3(half.T), qr, NN)
        first = beta_one * f_ref[c] + (1.0 - beta_one) * rot
        second = beta_two * s_ref[c] + (1.0 - beta_two) * rot * rot
        nf_ref[c] = first
        ns_ref[c] = second
        direction = first / (1.0 - beta_one**STEP) / (
            jnp.sqrt(second / (1.0 - beta_two**STEP)) + adam_eps)
        moved = prod(split3(prod(ql, split3(direction), NN)), qr, NT)
        master = m_ref[c]
        nm_ref[c] = master - learn_rate * (moved + weight_decay * master)
        a_scr[0, step * chunk + c] = prod(split3(new_left), ql, NN)
        a_scr[1, step * chunk + c] = prod(split3(new_right), qr, NN)

    @pl.when(step == pl.num_programs(0) - 1)
    def _():
        def bring(i, _):
            for s in range(2):
                slab = a_scr[s, :, pl.ds(i, 1), :].reshape(128, block)
                t_scr[s, i] = slab.T
            return 0
        lax.fori_loop(0, block, bring, 0, unroll=4)
        sub = lax.broadcasted_iota(jnp.int32, (8, 128), 0)
        norms = [[None] * tiles, [None] * tiles]
        for kt in range(tiles):
            def one(kk, carry):
                k = kt * 8 + kk
                acc = [[jnp.zeros((8, 128), F32) for _ in range(kt, tiles)] for _ in range(2)]
                for i in range(block):
                    for s in range(2):
                        row = jnp.broadcast_to(t_scr[s, i, pl.ds(k, 1), :], (8, 128))
                        for j in range(kt, tiles):
                            acc[s][j - kt] += row * t_scr[s, i, 8 * j : 8 * j + 8, :]
                out = []
                for s in range(2):
                    here = sub == kk
                    size = jnp.sum(jnp.where(here, acc[s][0], 0.0), axis=0, keepdims=True)
                    size = jnp.broadcast_to(size, (8, 128))
                    inv = 1.0 / size
                    acc[s] = [v * inv for v in acc[s]]
                    acc[s][0] = jnp.where(sub > kk, acc[s][0], 0.0)
                    out.append(jnp.where(here, size, carry[s]))
                for i in range(block):
                    for s in range(2):
                        row = jnp.broadcast_to(t_scr[s, i, pl.ds(k, 1), :], (8, 128))
                        for j in range(kt, tiles):
                            t_scr[s, i, 8 * j : 8 * j + 8, :] -= row * acc[s][j - kt]
                return tuple(out)
            res = lax.fori_loop(0, 8, one, (jnp.ones((8, 128), F32),) * 2)
            for s in range(2):
                norms[s][kt] = lax.rsqrt(res[s])
        scale = [jnp.concatenate(norms[s], axis=0) for s in range(2)]
        def back(i, _):
            for s, ref in ((0, bl_ref), (1, br_ref)):
                done = (t_scr[s, i] * scale[s]).T
                ref[:, pl.ds(i, 1), :] = done[:count].reshape(count, 1, block)
            return 0
        lax.fori_loop(0, block, back, 0, unroll=4)

def soap(g, m, f, s, l, r, ql, qr):
    count, block = g.shape[0], g.shape[-1]
    chunk = math.gcd(count, 8)
    spec = pl.BlockSpec((chunk, block, block), lambda i: (i, 0, 0))
    whole = pl.BlockSpec((count, block, block), lambda i: (0, 0, 0))
    shape = jax.ShapeDtypeStruct(g.shape, F32)
    return pl.pallas_call(
        functools.partial(soap_kernel, count, chunk, block),
        grid=(count // chunk,),
        in_specs=[spec] * 8,
        out_specs=[spec] * 5 + [whole] * 2,
        out_shape=[shape] * 7,
        scratch_shapes=[pltpu.VMEM((2, 128, block, block), F32), pltpu.VMEM((2, block, block, 128), F32)],
        compiler_params=pltpu.CompilerParams(vmem_limit_bytes=48 * 2**20),
        name="soap",
    )(g, m, f, s, l, r, ql, qr)


def norm_update(grad, master, first, second):
    new_first = beta_one * first + (1.0 - beta_one) * grad
    new_second = beta_two * second + (1.0 - beta_two) * grad * grad
    direction = (
        new_first
        / (1.0 - beta_one**STEP)
        / (jnp.sqrt(new_second / (1.0 - beta_two**STEP)) + adam_eps)
    )
    return (new_first, new_second, master - norm_rate * direction)


def body(
    inputs,
    segments,
    cotangent,
    owner,
    masters,
    first_moment,
    second_moment,
    left_stats,
    right_stats,
    left_basis,
    right_basis,
    norm_master,
    norm_first,
    norm_second,
):
    rows_here = inputs.shape[0]
    length = inputs.shape[1]
    width = inputs.shape[2]
    tensor_count = lax.axis_size("tensor")
    rank_attn = width // tensor_count
    per_dev = masters.shape[1]
    block = masters.shape[-1]
    scale = HD ** (-0.5)
    sel_shift = shift_for(length)
    tensor_index = lax.axis_index("tensor")
    shared_blocks, shared_norms = (
        lax.all_gather(masters[0].astype(jnp.bfloat16), "dp", axis=0, tiled=True),
        lax.all_gather(norm_master.astype(jnp.bfloat16), "dp", axis=0, tiled=True),
    )
    slots, inverse = block_slots(owner, per_dev)
    weight_matrix = blocks_to_matrix(jnp.take(shared_blocks, slots, axis=0), width // block)
    rank_mlp = (weight_matrix.shape[1] - 4 * rank_attn) // 2
    w_project = weight_matrix[:, : 3 * rank_attn]
    w_up = weight_matrix[:, 3 * rank_attn : 3 * rank_attn + rank_mlp]
    w_out_side = weight_matrix[:, 3 * rank_attn + rank_mlp : 4 * rank_attn + rank_mlp]
    w_down_side = weight_matrix[:, 4 * rank_attn + rank_mlp :]
    norms = shared_norms.astype(jnp.float32).reshape(4, width)
    tokens = inputs.reshape(rows_here * length, width).astype(jnp.float32)
    plain_one, inverse_one = normalize(tokens)
    normed_one = (plain_one * norms[0] + norms[1]).astype(jnp.bfloat16)
    projected = jnp.dot(normed_one, w_project, preferred_element_type=jnp.float32).astype(
        jnp.bfloat16
    )
    projection_rows = projected.reshape(rows_here, length, 3 * rank_attn)

    def attention_single_row(packed):
        row_proj, row_seg = packed
        queries, keys, values = split_heads(row_proj, rank_attn)
        raw = jnp.einsum("hqd,hkd->hqk", queries, keys, preferred_element_type=jnp.float32) * scale
        allowed, strict = row_masks(row_seg)

        def make_penalty(first_raw):
            return penalty_from(first_raw, strict).astype(jnp.bfloat16)

        def blank_penalty(first_raw):
            return jnp.zeros(first_raw.shape, jnp.bfloat16)

        local = lax.cond(tensor_index == 0, make_penalty, blank_penalty, raw[0])
        penalty = spread(local, "tensor", 0)
        logits = jnp.where(allowed[None], raw - penalty.astype(jnp.float32)[None], -1e30)
        top = jnp.max(logits, axis=-1, keepdims=True)
        weights = jnp.exp(logits - top)
        total = jnp.sum(weights, axis=-1, keepdims=True)
        probs = weights / total
        mixed = jnp.einsum(
            "hqk,hkd->hqd", probs.astype(jnp.bfloat16), values, preferred_element_type=jnp.float32
        )
        return (
            merge_heads(mixed).astype(jnp.bfloat16),
            top[..., 0] + jnp.log(total[..., 0]),
            penalty,
        )

    attention_output, logarithm_row_totals, selection_penalty = lax.map(
        attention_single_row, (projection_rows, segments)
    )
    attended_flat = attention_output.reshape(rows_here * length, rank_attn)
    attn_total = lax.psum(contract_cols(attended_flat, w_out_side), "tensor")
    resid = tokens + attn_total
    plain_two, inverse_two = normalize(resid)
    normed_two = (plain_two * norms[2] + norms[3]).astype(jnp.bfloat16)
    up_pre = jnp.dot(normed_two, w_up, preferred_element_type=jnp.float32)
    activated = jax.nn.gelu(up_pre, approximate=True).astype(jnp.bfloat16)
    mlp_total = lax.psum(contract_cols(activated, w_down_side), "tensor")
    output = (resid + mlp_total).astype(jnp.bfloat16).reshape(inputs.shape)
    back_out = cotangent.reshape(rows_here * length, width)
    d_act = jnp.dot(back_out, w_down_side, preferred_element_type=jnp.float32)
    grad_down_side = contract_rows(back_out, activated)

    def gelu_tanh(values):
        return jax.nn.gelu(values, approximate=True)

    gelu_pull = jax.vjp(gelu_tanh, up_pre)[1]
    d_up = gelu_pull(d_act)[0].astype(jnp.bfloat16)
    grad_up = contract_rows(normed_two, d_up)
    d_two = lax.psum(contract_cols(d_up, w_up), "tensor")
    grad_gain_two = jnp.sum(d_two * plain_two, axis=0)
    grad_bias_two = jnp.sum(d_two, axis=0)
    d_resid = back_out.astype(jnp.float32) + norm_back(plain_two, inverse_two, d_two * norms[2])
    d_resid_low = d_resid.astype(jnp.bfloat16)
    d_attended = jnp.dot(d_resid_low, w_out_side, preferred_element_type=jnp.float32).astype(
        jnp.bfloat16
    )
    grad_out_side = contract_rows(d_resid_low, attended_flat)

    def attend_back(packed):
        row_proj, row_seg, row_back, row_log, row_pen = packed
        queries, keys, values = split_heads(row_proj, rank_attn)
        back_heads = row_back.reshape(length, -1, HD).transpose(1, 0, 2)
        raw = jnp.einsum("hqd,hkd->hqk", queries, keys, preferred_element_type=jnp.float32) * scale
        allowed, strict = row_masks(row_seg)
        logits = jnp.where(allowed[None], raw - row_pen.astype(jnp.float32)[None], -1e30)
        probs = jnp.exp(logits - row_log[..., None])
        d_probs = jnp.einsum("hqd,hkd->hqk", back_heads, values, preferred_element_type=jnp.float32)
        inner = jnp.sum(d_probs * probs, axis=-1, keepdims=True)
        d_logits = probs * (d_probs - inner)
        pen_terms = -jnp.sum(d_logits, axis=0)
        share = lax.psum_scatter(pen_terms, "tensor", scatter_dimension=0, tiled=True)
        carried = entering(
            jnp.sum(share, axis=0),
            "tensor",
            append_column_block,
            jnp.zeros((share.shape[1],), jnp.float32),
        )
        later = lax.all_gather(later_sums(share) + carried[None], "tensor", axis=0, tiled=True)

        def with_selection(first):
            return first + jnp.where(strict, jax.nn.sigmoid(raw[0] - sel_shift) * later, 0.0)

        def without_selection(first):
            return first

        first_head = lax.cond(tensor_index == 0, with_selection, without_selection, d_logits[0])
        d_raw = jnp.concatenate([first_head[None], d_logits[1:]], axis=0).astype(jnp.bfloat16)
        d_query = (
            jnp.einsum("hqk,hkd->hqd", d_raw, keys, preferred_element_type=jnp.float32) * scale
        )
        d_key = (
            jnp.einsum("hqk,hqd->hkd", d_raw, queries, preferred_element_type=jnp.float32) * scale
        )
        d_value = jnp.einsum(
            "hqk,hqd->hkd",
            probs.astype(jnp.bfloat16),
            back_heads,
            preferred_element_type=jnp.float32,
        )
        return jnp.concatenate(
            [merge_heads(d_query), merge_heads(d_key), merge_heads(d_value)], axis=1
        ).astype(jnp.bfloat16)

    d_projected = lax.map(
        attend_back,
        (
            projection_rows,
            segments,
            d_attended.reshape(rows_here, length, rank_attn),
            logarithm_row_totals,
            selection_penalty,
        ),
    )
    d_projected = d_projected.reshape(rows_here * length, 3 * rank_attn)
    d_one = lax.psum(contract_cols(d_projected, w_project), "tensor")
    grad_project = contract_rows(normed_one, d_projected)
    grad_gain_one = jnp.sum(d_one * plain_one, axis=0)
    grad_bias_one = jnp.sum(d_one, axis=0)
    input_grad = (d_resid + norm_back(plain_one, inverse_one, d_one * norms[0])).reshape(
        inputs.shape
    )
    grad_matrix = jnp.concatenate([grad_project, grad_up, grad_out_side, grad_down_side], axis=1)
    stored_grads = jnp.take(matrix_to_blocks(grad_matrix, block), inverse, axis=0)
    norm_grads = jnp.concatenate(
        [grad_gain_one, grad_bias_one, grad_gain_two, grad_bias_two], axis=0
    )
    own_grads, own_norm_grads = (
        lax.psum_scatter(stored_grads, "dp", scatter_dimension=0, tiled=True),
        lax.psum_scatter(norm_grads, "dp", scatter_dimension=0, tiled=True),
    )
    new_first, new_second, new_master, new_left, new_right, left_next, right_next = soap(
        own_grads,
        masters[0],
        first_moment[0],
        second_moment[0],
        left_stats[0],
        right_stats[0],
        left_basis[0],
        right_basis[0],
    )
    norm_first_new, norm_second_new, norm_new = norm_update(
        own_norm_grads, norm_master, norm_first, norm_second
    )
    return (
        output,
        input_grad,
        new_first[None],
        new_second[None],
        new_master[None],
        new_left[None],
        new_right[None],
        left_next[None],
        right_next[None],
        norm_first_new,
        norm_second_new,
        norm_new,
    )


def solution(mesh):
    in_specs = (
        P("dp", None, None),
        P("dp", None),
        P("dp", None, None),
        P(),
        P("tensor", "dp", None, None),
        P("tensor", "dp", None, None),
        P("tensor", "dp", None, None),
        P("tensor", "dp", None, None),
        P("tensor", "dp", None, None),
        P("tensor", "dp", None, None),
        P("tensor", "dp", None, None),
        P("dp"),
        P("dp"),
        P("dp"),
    )
    out_specs = (
        P("dp", None, None),
        P("dp", None, None),
        P("tensor", "dp", None, None),
        P("tensor", "dp", None, None),
        P("tensor", "dp", None, None),
        P("tensor", "dp", None, None),
        P("tensor", "dp", None, None),
        P("tensor", "dp", None, None),
        P("tensor", "dp", None, None),
        P("dp"),
        P("dp"),
        P("dp"),
    )
    return jax.shard_map(body, mesh=mesh, in_specs=in_specs, out_specs=out_specs, check_vma=False)
```

```python
import functools
import math

import jax
import jax.numpy as jnp
from jax import lax
from jax.experimental import pallas as pl
from jax.experimental.pallas import tpu as pltpu
from jax.sharding import PartitionSpec as P

HD = 64
STEP = 10
F32 = jnp.float32
BF16 = jnp.bfloat16


highest = lax.Precision.HIGHEST
norm_eps = 1e-05
beta_one = 0.9
beta_two = 0.95
beta_stats = 0.95
learn_rate = 0.03
norm_rate = 0.4
weight_decay = 0.01
adam_eps = 1e-08


def shift_for(length):
    return math.log(length / 8.0)


def block_slots(owner, per_dev):
    count = owner.shape[0]
    index = jnp.arange(count, dtype=jnp.int32)
    earlier = (owner[:, None] == owner[None, :]) & (index[None, :] < index[:, None])
    rank = jnp.sum(earlier.astype(jnp.int32), axis=1)
    slots = owner * per_dev + rank
    inverse = jnp.sum(jnp.where(slots[None, :] == index[:, None], index[None, :], 0), axis=1)
    return (slots, inverse)


MESH = pl.DeviceIdType.MESH
VM = pl.BlockSpec(memory_space=pltpu.VMEM)
MIB = 2**20


def tiles_up(value):
    return -(-value // 128) * 128


def remote(src, dst, send, recv, where):
    return pltpu.make_async_remote_copy(
        src_ref=src, dst_ref=dst, send_sem=send, recv_sem=recv, device_id=where, device_id_type=MESH
    )


def greet(devices):
    barrier = pltpu.get_barrier_semaphore()
    for device in devices:
        pl.semaphore_signal(barrier, inc=1, device_id=device, device_id_type=MESH)
    pl.semaphore_wait(barrier, len(devices))


def line_greet(dp, t, m):
    place, side = dp // 2, lax.rem(dp, 2)
    barrier = pltpu.get_barrier_semaphore()
    pl.semaphore_signal(barrier, inc=1, device_id=(place * 2 + 1 - side, t), device_id_type=MESH)

    @pl.when(place > 0)
    def _():
        pl.semaphore_signal(barrier, inc=1, device_id=(dp - 2, t), device_id_type=MESH)

    @pl.when(place < m - 1)
    def _():
        pl.semaphore_signal(barrier, inc=1, device_id=(dp + 2, t), device_id_type=MESH)

    ends = (place == 0).astype(jnp.int32) + (place == m - 1).astype(jnp.int32)
    pl.semaphore_wait(barrier, 3 - ends)


def gather_kernel(n, count, block, wide, norm_rows, m_ref, norm_ref, u_ref, nout_ref, held, send_sem, recv_sem):
    m = n // 2
    dp, t = lax.axis_index("dp"), lax.axis_index("tensor")
    place, side = dp // 2, lax.rem(dp, 2)
    pair = (place * 2 + 1 - side, t)
    for k in range(count):
        held[dp, :, k * block : (k + 1) * block] = m_ref[k].astype(BF16)
    if wide > count * block:
        held[dp, :, count * block : wide] = jnp.zeros((block, wide - count * block), BF16)
    held[dp, :, wide : wide + 128] = jnp.concatenate(
        [norm_ref[...], jnp.zeros((block - norm_rows, 128), F32)], axis=0
    ).astype(BF16)
    line_greet(dp, t, m)

    def send(source, way, where):
        return remote(held.at[source], held.at[source], send_sem.at[source, way], recv_sem.at[source], where)

    def unpack(source):
        for k in range(count):
            u_ref[source * count + k] = held[source, :, k * block : (k + 1) * block]
        nout_ref[source] = held[source, :16, wide : wide + 128]

    def spread(source, left, right):
        send(source, 2, pair).start()

        @pl.when(left)
        def _():
            send(source, 0, (dp - 2, t)).start()

        @pl.when(right)
        def _():
            send(source, 1, (dp + 2, t)).start()

    def spread_done(source, left, right):
        send(source, 2, pair).wait_send()

        @pl.when(left)
        def _():
            send(source, 0, (dp - 2, t)).wait_send()

        @pl.when(right)
        def _():
            send(source, 1, (dp + 2, t)).wait_send()

    spread(dp, place > 0, place < m - 1)
    unpack(dp)

    def one(hop, _):
        @pl.when(place - hop >= 0)
        def _():
            source = dp - 2 * hop
            send(source, 2, pair).wait_recv()
            spread(source, False, place < m - 1)

        @pl.when(place + hop < m)
        def _():
            source = dp + 2 * hop
            send(source, 2, pair).wait_recv()
            spread(source, place > 0, False)

        @pl.when(place - hop >= 0)
        def _():
            unpack(dp - 2 * hop)

        @pl.when(place + hop < m)
        def _():
            unpack(dp + 2 * hop)

        return 0

    lax.fori_loop(1, m, one, 0)

    def other(step, _):
        source = step * 2 + 1 - side
        send(source, 2, pair).wait_recv()
        unpack(source)
        return 0

    lax.fori_loop(0, m, other, 0)

    def finish(step, _):
        source = step * 2 + side
        spread_done(
            source,
            (place > 0) & (step >= place),
            (place < m - 1) & (step <= place),
        )
        return 0

    lax.fori_loop(0, m, finish, 0)


def gather_masters(masters, norm, n):
    count, block = masters.shape[0], masters.shape[-1]
    wide = tiles_up(count * block)
    norm_rows = -(-norm.shape[0] // 128)
    norm_tile = jnp.pad(norm, (0, norm_rows * 128 - norm.shape[0])).reshape(norm_rows, 128)
    blocks, norms = pl.pallas_call(
        functools.partial(gather_kernel, n, count, block, wide, norm_rows),
        out_shape=[
            jax.ShapeDtypeStruct((n * count, block, block), BF16),
            jax.ShapeDtypeStruct((n, 16, 128), BF16),
        ],
        in_specs=[VM, VM],
        out_specs=[VM, VM],
        scratch_shapes=[
            pltpu.VMEM((n, block, wide + 128), BF16),
            pltpu.SemaphoreType.DMA((n, 3)),
            pltpu.SemaphoreType.DMA((n,)),
        ],
        compiler_params=pltpu.CompilerParams(collective_id=1, has_side_effects=True, vmem_limit_bytes=10 * MIB),
        name="gather_masters",
    )(masters, norm_tile)
    return blocks, norms.reshape(n, 16 * 128)[:, : norm.shape[0]].reshape(-1)


def assemble_kernel(rows, cols, block, slot_ref, u_ref, w_ref):
    def one(row, _):
        strip = jnp.concatenate([u_ref[slot_ref[row * cols + c]] for c in range(cols)], axis=1)
        w_ref[pl.ds(pl.multiple_of(row * block, block), block), :] = strip
        return 0

    lax.fori_loop(0, rows, one, 0)


def assemble(slots, blocks, rows):
    block = blocks.shape[-1]
    cols = blocks.shape[0] // rows
    return pl.pallas_call(
        functools.partial(assemble_kernel, rows, cols, block),
        out_shape=jax.ShapeDtypeStruct((rows * block, cols * block), BF16),
        in_specs=[pl.BlockSpec(memory_space=pltpu.SMEM), VM],
        out_specs=VM,
        compiler_params=pltpu.CompilerParams(vmem_limit_bytes=4 * MIB),
        name="assemble",
    )(slots, blocks)


def disperse_kernel(rows, cols, block, n, count, wide, inverse_ref, g_ref, p_ref, u_scr):
    def cut(row, _):
        strip = g_ref[pl.ds(pl.multiple_of(row * block, block), block), :]
        for c in range(cols):
            u_scr[row * cols + c] = strip[:, c * block : (c + 1) * block].astype(BF16)
        return 0

    lax.fori_loop(0, rows, cut, 0)

    def lay(d, _):
        for k in range(count):
            p_ref[d, :, k * block : (k + 1) * block] = u_scr[inverse_ref[d * count + k]]
        if wide > count * block:
            p_ref[d, :, count * block : wide] = jnp.zeros((block, wide - count * block), BF16)
        return 0

    lax.fori_loop(0, n, lay, 0)


def disperse(inverse, grads, n, block):
    rows, cols = grads.shape[0] // block, grads.shape[1] // block
    count = rows * cols // n
    wide = tiles_up(count * block)
    return pl.pallas_call(
        functools.partial(disperse_kernel, rows, cols, block, n, count, wide),
        out_shape=jax.ShapeDtypeStruct((n, block, wide), BF16),
        in_specs=[pl.BlockSpec(memory_space=pltpu.SMEM), VM],
        out_specs=VM,
        scratch_shapes=[pltpu.VMEM((rows * cols, block, block), BF16)],
        compiler_params=pltpu.CompilerParams(vmem_limit_bytes=16 * MIB),
        name="disperse",
    )(inverse, grads)


def scatter_kernel(n, p_ref, g_ref, xin, lin, rin, x_send, x_recv, l_send, l_recv, r_send, r_recv):
    m = n // 2
    dp, t = lax.axis_index("dp"), lax.axis_index("tensor")
    place, side = dp // 2, lax.rem(dp, 2)
    pair = (place * 2 + 1 - side, t)
    line_greet(dp, t, m)

    def across(q):
        return remote(p_ref.at[q * 2 + 1 - side], xin.at[q], x_send.at[q], x_recv.at[q], pair)

    def rightward(q, src):
        return remote(src.at[q], lin.at[q], r_send.at[q], l_recv.at[q], (dp + 2, t))

    def leftward(q, src):
        return remote(src.at[q], rin.at[q], l_send.at[q], r_recv.at[q], (dp - 2, t))

    def far_first(one):
        def both(step, _):
            hop = m - 1 - step

            @pl.when(place + hop < m)
            def _():
                one(place + hop, True)

            @pl.when((place - hop >= 0) & (hop > 0))
            def _():
                one(place - hop, False)

            return 0

        lax.fori_loop(0, m, both, 0)

    far_first(lambda q, right: across(q).start())

    def work(q, right):
        across(q).wait_recv()
        own = p_ref[q * 2 + side].astype(F32) + xin[q].astype(F32)
        if right:
            @pl.when((q > place) & (place > 0))
            def _():
                rightward(q, lin).wait_recv()
                lin[q] = (own + lin[q].astype(F32)).astype(BF16)

            @pl.when((q > place) & (place == 0))
            def _():
                lin[q] = own.astype(BF16)

            @pl.when(q > place)
            def _():
                rightward(q, lin).start()

            @pl.when((q == place) & (place > 0) & (place < m - 1))
            def _():
                rightward(q, lin).wait_recv()
                leftward(q, rin).wait_recv()
                g_ref[...] = own + (lin[q].astype(F32) + rin[q].astype(F32))

            @pl.when((q == place) & (place == 0))
            def _():
                leftward(q, rin).wait_recv()
                g_ref[...] = own + rin[q].astype(F32)

            @pl.when((q == place) & (place == m - 1))
            def _():
                rightward(q, lin).wait_recv()
                g_ref[...] = own + lin[q].astype(F32)
        else:
            @pl.when(place < m - 1)
            def _():
                leftward(q, rin).wait_recv()
                rin[q] = (own + rin[q].astype(F32)).astype(BF16)

            @pl.when(place == m - 1)
            def _():
                rin[q] = own.astype(BF16)

            leftward(q, rin).start()

    far_first(work)

    def finish(q, _):
        across(q).wait_send()

        @pl.when(q > place)
        def _():
            rightward(q, lin).wait_send()

        @pl.when(q < place)
        def _():
            leftward(q, rin).wait_send()

        return 0

    lax.fori_loop(0, m, finish, 0)


def scatter_grads(packed):
    n, block, wide = packed.shape
    m = n // 2
    return pl.pallas_call(
        functools.partial(scatter_kernel, n),
        out_shape=jax.ShapeDtypeStruct((block, wide), F32),
        in_specs=[VM],
        out_specs=VM,
        scratch_shapes=[pltpu.VMEM((m, block, wide), BF16)] * 3 + [pltpu.SemaphoreType.DMA((m,))] * 6,
        compiler_params=pltpu.CompilerParams(collective_id=2, has_side_effects=True, vmem_limit_bytes=16 * MIB),
        name="scatter_grads",
    )(packed)


def total_kernel(pieces, x_ref, out_ref, near, mine, far, near_mine, near_far, *sems):
    (a_send, a_recv, b_send, b_recv, c_send, c_recv, d_send, d_recv) = sems
    dp, t = lax.axis_index("dp"), lax.axis_index("tensor")
    up, core = t // 2, lax.rem(t, 2)
    beside = (dp, up * 2 + 1 - core)
    over = (dp, (1 - up) * 2 + core)
    half = x_ref.shape[0] // 2
    piece = half // pieces
    greet([beside, over])

    def rows(base, j):
        return pl.ds(pl.multiple_of(base * half + j * piece, piece), piece)

    def part(ref, j):
        return ref.at[pl.ds(j * piece, piece)]

    first = [
        remote(x_ref.at[rows(1 - core, j)], part(near, j), a_send.at[j], a_recv.at[j], beside)
        for j in range(pieces)
    ]
    cross = [remote(part(mine, j), part(far, j), b_send.at[j], b_recv.at[j], over) for j in range(pieces)]
    share = [remote(part(mine, j), part(near_mine, j), c_send.at[j], c_recv.at[j], beside) for j in range(pieces)]
    relay = [remote(part(far, j), part(near_far, j), d_send.at[j], d_recv.at[j], beside) for j in range(pieces)]
    for j in range(pieces):
        first[j].start()
    for j in range(pieces):
        here = pl.ds(j * piece, piece)
        first[j].wait_recv()
        mine[here] = (x_ref[rows(core, j)].astype(F32) + near[here].astype(F32)).astype(BF16)
        cross[j].start()
        share[j].start()
    for j in range(pieces):
        here = pl.ds(j * piece, piece)
        cross[j].wait_recv()
        relay[j].start()
        out_ref[rows(core, j)] = mine[here].astype(F32) + far[here].astype(F32)
    for j in range(pieces):
        here = pl.ds(j * piece, piece)
        share[j].wait_recv()
        relay[j].wait_recv()
        out_ref[rows(1 - core, j)] = near_mine[here].astype(F32) + near_far[here].astype(F32)
    for j in range(pieces):
        first[j].wait_send()
        cross[j].wait_send()
        share[j].wait_send()
        relay[j].wait_send()


def tensor_total(part, ident):
    length, width = part.shape
    pieces = 4
    half = length // 2
    return pl.pallas_call(
        functools.partial(total_kernel, pieces),
        out_shape=jax.ShapeDtypeStruct((length, width), F32),
        in_specs=[VM],
        out_specs=VM,
        scratch_shapes=[pltpu.VMEM((half, width), BF16)] * 5 + [pltpu.SemaphoreType.DMA((pieces,))] * 8,
        compiler_params=pltpu.CompilerParams(collective_id=ident, has_side_effects=True, vmem_limit_bytes=16 * MIB),
        name="tensor_total",
    )(part)


def everyone(dp, t):
    return [(dp, lax.rem(t + hop, 4)) for hop in (1, 2, 3)]


def share_kernel(x_ref, out_ref, held, send_sem, recv_sem):
    dp, t = lax.axis_index("dp"), lax.axis_index("tensor")
    greet(everyone(dp, t))

    @pl.when(t == 0)
    def _():
        copies = [remote(x_ref, held, send_sem.at[i], recv_sem, (dp, i + 1)) for i in range(3)]
        for copy in copies:
            copy.start()
        out_ref[...] = x_ref[...]
        for copy in copies:
            copy.wait_send()

    @pl.when(t > 0)
    def _():
        remote(x_ref, held, send_sem.at[0], recv_sem, (dp, 0)).wait_recv()
        out_ref[...] = held[...]


def share_first(first):
    return pl.pallas_call(
        share_kernel,
        out_shape=jax.ShapeDtypeStruct(first.shape, first.dtype),
        in_specs=[VM],
        out_specs=VM,
        scratch_shapes=[
            pltpu.VMEM(first.shape, first.dtype),
            pltpu.SemaphoreType.DMA((3,)),
            pltpu.SemaphoreType.DMA,
        ],
        compiler_params=pltpu.CompilerParams(collective_id=3, has_side_effects=True),
        name="share_first",
    )(first)


def collect_kernel(x_ref, out_ref, held, send_sem, recv_sem):
    dp, t = lax.axis_index("dp"), lax.axis_index("tensor")
    greet(everyone(dp, t))

    @pl.when(t > 0)
    def _():
        copy = remote(x_ref, held.at[t - 1], send_sem, recv_sem.at[t - 1], (dp, 0))
        copy.start()
        out_ref[...] = jnp.zeros_like(out_ref)
        copy.wait_send()

    @pl.when(t == 0)
    def _():
        total = x_ref[...].astype(F32)
        for i in range(3):
            remote(x_ref, held.at[i], send_sem, recv_sem.at[i], (dp, i + 1)).wait_recv()
            total = total + held[i].astype(F32)
        out_ref[...] = total


def collect_first(part):
    return pl.pallas_call(
        collect_kernel,
        out_shape=jax.ShapeDtypeStruct(part.shape, F32),
        in_specs=[VM],
        out_specs=VM,
        scratch_shapes=[
            pltpu.VMEM((3,) + part.shape, BF16),
            pltpu.SemaphoreType.DMA,
            pltpu.SemaphoreType.DMA((3,)),
        ],
        compiler_params=pltpu.CompilerParams(collective_id=4, has_side_effects=True),
        name="collect_first",
    )(part)


def normalize(rows):
    centered = rows - jnp.mean(rows, axis=-1, keepdims=True)
    inverse_std = lax.rsqrt(jnp.mean(centered * centered, axis=-1, keepdims=True) + norm_eps)
    return (centered * inverse_std, inverse_std)


def norm_back(plain, inverse_std, grad):
    return inverse_std * (
        grad
        - jnp.mean(grad, axis=-1, keepdims=True)
        - plain * jnp.mean(grad * plain, axis=-1, keepdims=True)
    )


def contract_rows(left, right):
    return lax.dot_general(
        left, right, (((0,), (0,)), ((), ())), preferred_element_type=jnp.float32
    )


def contract_cols(left, right):
    return lax.dot_general(
        left, right, (((1,), (1,)), ((), ())), preferred_element_type=jnp.float32
    )


def row_masks(row_seg):
    position = jnp.arange(row_seg.shape[0], dtype=jnp.int32)
    same = row_seg[:, None] == row_seg[None, :]
    return (
        same & (position[None, :] <= position[:, None]),
        same & (position[None, :] < position[:, None]),
    )


def penalty_from(first_raw, strict):
    picks = jnp.where(strict, jax.nn.softplus(first_raw - shift_for(first_raw.shape[0])), 0.0)
    running = jnp.cumsum(picks, axis=0)
    return jnp.concatenate([jnp.zeros((1, picks.shape[1]), picks.dtype), running[:-1]], axis=0)


def later_sums(grads):
    suffix = jnp.cumsum(grads[::-1], axis=0)[::-1]
    return jnp.concatenate([suffix[1:], jnp.zeros((1, suffix.shape[1]), suffix.dtype)], axis=0)


def split_heads(row_proj, rank_attn):
    length = row_proj.shape[0]

    def heads_of(piece):
        return piece.reshape(length, -1, HD).transpose(1, 0, 2)

    return (
        heads_of(row_proj[:, :rank_attn]),
        heads_of(row_proj[:, rank_attn : 2 * rank_attn]),
        heads_of(row_proj[:, 2 * rank_attn :]),
    )


def merge_heads(heads):
    return heads.transpose(1, 0, 2).reshape(heads.shape[1], -1)


def split3(v):
    hi = v.astype(BF16)
    return hi, (v - hi.astype(F32)).astype(BF16)

def prod(left, right, dims):
    lh, ll = left
    rh, rl = right
    spec = (dims, ((), ()))
    def one(a, b):
        return lax.dot_general(a, b, spec, preferred_element_type=F32)
    return one(lh, rh) + (one(lh, rl) + one(ll, rh))

NN = ((1,), (0,))
NT = ((1,), (1,))
TN = ((0,), (0,))

def soap_kernel(count, chunk, block, g_ref, m_ref, f_ref, s_ref, l_ref, r_ref, ql_ref, qr_ref,
                nf_ref, ns_ref, nm_ref, nl_ref, nr_ref, bl_ref, br_ref, a_scr, t_scr):
    step = pl.program_id(0)
    tiles = block // 8
    for c in range(chunk):
        g = g_ref[c]
        ql, qr = split3(ql_ref[c]), split3(qr_ref[c])
        gs = split3(g)
        gt = split3(g.T)
        new_left = beta_stats * l_ref[c] + (1.0 - beta_stats) * prod(gs, gs, NT)
        new_right = beta_stats * r_ref[c] + (1.0 - beta_stats) * prod(gt, gt, NT)
        nl_ref[c] = new_left
        nr_ref[c] = new_right
        half = prod(gt, ql, NN)
        rot = prod(split3(half.T), qr, NN)
        first = beta_one * f_ref[c] + (1.0 - beta_one) * rot
        second = beta_two * s_ref[c] + (1.0 - beta_two) * rot * rot
        nf_ref[c] = first
        ns_ref[c] = second
        direction = first / (1.0 - beta_one**STEP) / (
            jnp.sqrt(second / (1.0 - beta_two**STEP)) + adam_eps)
        moved = prod(split3(prod(ql, split3(direction), NN)), qr, NT)
        master = m_ref[c]
        nm_ref[c] = master - learn_rate * (moved + weight_decay * master)
        a_scr[0, step * chunk + c] = prod(split3(new_left), ql, NN)
        a_scr[1, step * chunk + c] = prod(split3(new_right), qr, NN)

    @pl.when(step == pl.num_programs(0) - 1)
    def _():
        def bring(i, _):
            for s in range(2):
                slab = a_scr[s, :, pl.ds(i, 1), :].reshape(128, block)
                t_scr[s, i] = slab.T
            return 0
        lax.fori_loop(0, block, bring, 0, unroll=4)
        sub = lax.broadcasted_iota(jnp.int32, (8, 128), 0)
        norms = [[None] * tiles, [None] * tiles]
        for kt in range(tiles):
            def one(kk, carry):
                k = kt * 8 + kk
                acc = [[jnp.zeros((8, 128), F32) for _ in range(kt, tiles)] for _ in range(2)]
                for i in range(block):
                    for s in range(2):
                        row = jnp.broadcast_to(t_scr[s, i, pl.ds(k, 1), :], (8, 128))
                        for j in range(kt, tiles):
                            acc[s][j - kt] += row * t_scr[s, i, 8 * j : 8 * j + 8, :]
                out = []
                for s in range(2):
                    here = sub == kk
                    size = jnp.sum(jnp.where(here, acc[s][0], 0.0), axis=0, keepdims=True)
                    size = jnp.broadcast_to(size, (8, 128))
                    inv = 1.0 / size
                    acc[s] = [v * inv for v in acc[s]]
                    acc[s][0] = jnp.where(sub > kk, acc[s][0], 0.0)
                    out.append(jnp.where(here, size, carry[s]))
                for i in range(block):
                    for s in range(2):
                        row = jnp.broadcast_to(t_scr[s, i, pl.ds(k, 1), :], (8, 128))
                        for j in range(kt, tiles):
                            t_scr[s, i, 8 * j : 8 * j + 8, :] -= row * acc[s][j - kt]
                return tuple(out)
            res = lax.fori_loop(0, 8, one, (jnp.ones((8, 128), F32),) * 2)
            for s in range(2):
                norms[s][kt] = lax.rsqrt(res[s])
        scale = [jnp.concatenate(norms[s], axis=0) for s in range(2)]
        def back(i, _):
            for s, ref in ((0, bl_ref), (1, br_ref)):
                done = (t_scr[s, i] * scale[s]).T
                ref[:, pl.ds(i, 1), :] = done[:count].reshape(count, 1, block)
            return 0
        lax.fori_loop(0, block, back, 0, unroll=4)

def soap(g, m, f, s, l, r, ql, qr):
    count, block = g.shape[0], g.shape[-1]
    chunk = math.gcd(count, 8)
    spec = pl.BlockSpec((chunk, block, block), lambda i: (i, 0, 0))
    whole = pl.BlockSpec((count, block, block), lambda i: (0, 0, 0))
    shape = jax.ShapeDtypeStruct(g.shape, F32)
    return pl.pallas_call(
        functools.partial(soap_kernel, count, chunk, block),
        grid=(count // chunk,),
        in_specs=[spec] * 8,
        out_specs=[spec] * 5 + [whole] * 2,
        out_shape=[shape] * 7,
        scratch_shapes=[pltpu.VMEM((2, 128, block, block), F32), pltpu.VMEM((2, block, block, 128), F32)],
        compiler_params=pltpu.CompilerParams(vmem_limit_bytes=48 * 2**20),
        name="soap",
    )(g, m, f, s, l, r, ql, qr)


def norm_update(grad, master, first, second):
    new_first = beta_one * first + (1.0 - beta_one) * grad
    new_second = beta_two * second + (1.0 - beta_two) * grad * grad
    direction = (
        new_first
        / (1.0 - beta_one**STEP)
        / (jnp.sqrt(new_second / (1.0 - beta_two**STEP)) + adam_eps)
    )
    return (new_first, new_second, master - norm_rate * direction)


def body(
    inputs,
    segments,
    cotangent,
    owner,
    masters,
    first_moment,
    second_moment,
    left_stats,
    right_stats,
    left_basis,
    right_basis,
    norm_master,
    norm_first,
    norm_second,
):
    length = inputs.shape[1]
    width = inputs.shape[2]
    n_dp = lax.axis_size("dp")
    tensor_count = lax.axis_size("tensor")
    rank_attn = width // tensor_count
    per_dev = masters.shape[1]
    block = masters.shape[-1]
    scale = HD ** (-0.5)
    sel_shift = shift_for(length)
    tensor_index = lax.axis_index("tensor")
    blocks, shared_norms = gather_masters(masters[0], norm_master, n_dp)
    slots, inverse = block_slots(owner, per_dev)
    weight_matrix = assemble(slots, blocks, width // block)
    rank_mlp = (weight_matrix.shape[1] - 4 * rank_attn) // 2
    w_first = share_first(
        jnp.concatenate([weight_matrix[:, :HD], weight_matrix[:, rank_attn : rank_attn + HD]], axis=1)
    )
    w_project = jnp.concatenate([weight_matrix[:, : 3 * rank_attn], w_first], axis=1)
    w_up = weight_matrix[:, 3 * rank_attn : 3 * rank_attn + rank_mlp]
    w_out_side = weight_matrix[:, 3 * rank_attn + rank_mlp : 4 * rank_attn + rank_mlp]
    w_down_side = weight_matrix[:, 4 * rank_attn + rank_mlp :]
    norms = shared_norms.astype(F32).reshape(4, width)
    tokens = inputs.reshape(length, width).astype(F32)
    plain_one, inverse_one = normalize(tokens)
    normed_one = (plain_one * norms[0] + norms[1]).astype(BF16)
    projected = jnp.dot(normed_one, w_project, preferred_element_type=F32).astype(BF16)
    queries, keys, values = split_heads(projected[:, : 3 * rank_attn], rank_attn)
    first_query = projected[:, 3 * rank_attn : 3 * rank_attn + HD]
    first_key = projected[:, 3 * rank_attn + HD :]
    allowed, strict = row_masks(segments[0])
    first_raw = contract_cols(first_query, first_key) * scale
    penalty = penalty_from(first_raw, strict).astype(BF16).astype(F32)
    raw = jnp.einsum("hqd,hkd->hqk", queries, keys, preferred_element_type=F32) * scale
    logits = jnp.where(allowed[None], raw - penalty[None], -1e30)
    top = jnp.max(logits, axis=-1, keepdims=True)
    weights = jnp.exp(logits - top)
    total = jnp.sum(weights, axis=-1, keepdims=True)
    probs = weights / total
    mixed = jnp.einsum("hqk,hkd->hqd", probs.astype(BF16), values, preferred_element_type=F32)
    attended = merge_heads(mixed).astype(BF16)
    attn_total = tensor_total(contract_cols(attended, w_out_side).astype(BF16), 5)
    resid = tokens + attn_total
    plain_two, inverse_two = normalize(resid)
    normed_two = (plain_two * norms[2] + norms[3]).astype(BF16)
    up_pre = jnp.dot(normed_two, w_up, preferred_element_type=F32)
    activated = jax.nn.gelu(up_pre, approximate=True).astype(BF16)
    mlp_total = tensor_total(contract_cols(activated, w_down_side).astype(BF16), 6)
    output = (resid + mlp_total).astype(BF16).reshape(inputs.shape)
    back_out = cotangent.reshape(length, width)
    d_act = jnp.dot(back_out, w_down_side, preferred_element_type=F32)
    grad_down_side = contract_rows(back_out, activated)

    def gelu_tanh(values):
        return jax.nn.gelu(values, approximate=True)

    d_up = jax.vjp(gelu_tanh, up_pre)[1](d_act)[0].astype(BF16)
    grad_up = contract_rows(normed_two, d_up)
    d_two = tensor_total(contract_cols(d_up, w_up).astype(BF16), 7)
    grad_gain_two = jnp.sum(d_two * plain_two, axis=0)
    grad_bias_two = jnp.sum(d_two, axis=0)
    d_resid = back_out.astype(F32) + norm_back(plain_two, inverse_two, d_two * norms[2])
    d_resid_low = d_resid.astype(BF16)
    d_attended = jnp.dot(d_resid_low, w_out_side, preferred_element_type=F32).astype(BF16)
    grad_out_side = contract_rows(d_resid_low, attended)
    back_heads = d_attended.reshape(length, -1, HD).transpose(1, 0, 2)
    d_probs = jnp.einsum("hqd,hkd->hqk", back_heads, values, preferred_element_type=F32)
    inner = jnp.sum(d_probs * probs, axis=-1, keepdims=True)
    d_logits = probs * (d_probs - inner)
    later = later_sums(-jnp.sum(d_logits, axis=0))
    first_part = jnp.where(strict, jax.nn.sigmoid(first_raw - sel_shift) * later, 0.0).astype(BF16)
    d_raw = d_logits.astype(BF16)
    d_query = jnp.einsum("hqk,hkd->hqd", d_raw, keys, preferred_element_type=F32) * scale
    d_key = jnp.einsum("hqk,hqd->hkd", d_raw, queries, preferred_element_type=F32) * scale
    d_value = jnp.einsum("hqk,hqd->hkd", probs.astype(BF16), back_heads, preferred_element_type=F32)
    d_first = jnp.concatenate(
        [
            jnp.dot(first_part, first_key, preferred_element_type=F32) * scale,
            contract_rows(first_part, first_query) * scale,
        ],
        axis=1,
    )
    d_projected = jnp.concatenate(
        [merge_heads(d_query), merge_heads(d_key), merge_heads(d_value), d_first], axis=1
    ).astype(BF16)
    d_one = tensor_total(contract_cols(d_projected, w_project).astype(BF16), 8)
    grad_project = contract_rows(normed_one, d_projected)
    first_grad = collect_first(grad_project[:, 3 * rank_attn :].astype(BF16))
    blank = jnp.zeros((width, rank_attn - HD), F32)
    grad_project = grad_project[:, : 3 * rank_attn] + jnp.concatenate(
        [first_grad[:, :HD], blank, first_grad[:, HD:], blank, jnp.zeros((width, rank_attn), F32)], axis=1
    )
    grad_gain_one = jnp.sum(d_one * plain_one, axis=0)
    grad_bias_one = jnp.sum(d_one, axis=0)
    input_grad = (d_resid + norm_back(plain_one, inverse_one, d_one * norms[0])).reshape(inputs.shape)
    grad_matrix = jnp.concatenate([grad_project, grad_up, grad_out_side, grad_down_side], axis=1)
    norm_grads = jnp.concatenate([grad_gain_one, grad_bias_one, grad_gain_two, grad_bias_two], axis=0)
    own_packed = scatter_grads(disperse(inverse, grad_matrix, n_dp, block))
    own_grads = own_packed[:, : per_dev * block].reshape(block, per_dev, block).transpose(1, 0, 2)
    own_norm_grads = lax.psum_scatter(norm_grads, "dp", scatter_dimension=0, tiled=True)
    new_first, new_second, new_master, new_left, new_right, left_next, right_next = soap(
        own_grads,
        masters[0],
        first_moment[0],
        second_moment[0],
        left_stats[0],
        right_stats[0],
        left_basis[0],
        right_basis[0],
    )
    norm_first_new, norm_second_new, norm_new = norm_update(
        own_norm_grads, norm_master, norm_first, norm_second
    )
    return (
        output,
        input_grad,
        new_first[None],
        new_second[None],
        new_master[None],
        new_left[None],
        new_right[None],
        left_next[None],
        right_next[None],
        norm_first_new,
        norm_second_new,
        norm_new,
    )


def solution(mesh):
    in_specs = (
        P("dp", None, None),
        P("dp", None),
        P("dp", None, None),
        P(),
        P("tensor", "dp", None, None),
        P("tensor", "dp", None, None),
        P("tensor", "dp", None, None),
        P("tensor", "dp", None, None),
        P("tensor", "dp", None, None),
        P("tensor", "dp", None, None),
        P("tensor", "dp", None, None),
        P("dp"),
        P("dp"),
        P("dp"),
    )
    out_specs = (
        P("dp", None, None),
        P("dp", None, None),
        P("tensor", "dp", None, None),
        P("tensor", "dp", None, None),
        P("tensor", "dp", None, None),
        P("tensor", "dp", None, None),
        P("tensor", "dp", None, None),
        P("tensor", "dp", None, None),
        P("tensor", "dp", None, None),
        P("dp"),
        P("dp"),
        P("dp"),
    )
    return jax.shard_map(body, mesh=mesh, in_specs=in_specs, out_specs=out_specs, check_vma=False)
```

```python
import functools
import math

import jax
import jax.numpy as jnp
from jax import lax
from jax.experimental import pallas as pl
from jax.experimental.pallas import tpu as pltpu
from jax.sharding import PartitionSpec as P

HD = 64
STEP = 10
F32 = jnp.float32
BF16 = jnp.bfloat16
LAYER_LIMIT = 48 * 2**20

norm_eps = 1e-05
beta_one = 0.9
beta_two = 0.95
beta_stats = 0.95
learn_rate = 0.03
norm_rate = 0.4
weight_decay = 0.01
adam_eps = 1e-08


def shift_for(length):
    return math.log(length / 8.0)


def block_slots(owner, per_dev):
    count = owner.shape[0]
    index = jnp.arange(count, dtype=jnp.int32)
    earlier = (owner[:, None] == owner[None, :]) & (index[None, :] < index[:, None])
    rank = jnp.sum(earlier.astype(jnp.int32), axis=1)
    slots = owner * per_dev + rank
    inverse = jnp.sum(jnp.where(slots[None, :] == index[:, None], index[None, :], 0), axis=1)
    return (slots, inverse)


def norm_back(plain, inverse_std, grad):
    return inverse_std * (
        grad
        - jnp.mean(grad, axis=-1, keepdims=True)
        - plain * jnp.mean(grad * plain, axis=-1, keepdims=True)
    )


def split3(v):
    hi = v.astype(BF16)
    return hi, (v - hi.astype(F32)).astype(BF16)

def prod(left, right, dims):
    lh, ll = left
    rh, rl = right
    spec = (dims, ((), ()))
    def one(a, b):
        return lax.dot_general(a, b, spec, preferred_element_type=F32)
    return one(lh, rh) + (one(lh, rl) + one(ll, rh))

NN = ((1,), (0,))
NT = ((1,), (1,))
TN = ((0,), (0,))

def soap_kernel(count, chunk, block, g_ref, m_ref, f_ref, s_ref, l_ref, r_ref, ql_ref, qr_ref,
                nf_ref, ns_ref, nm_ref, nl_ref, nr_ref, bl_ref, br_ref, a_scr, t_scr):
    step = pl.program_id(0)
    tiles = block // 8
    for c in range(chunk):
        g = g_ref[c]
        ql, qr = split3(ql_ref[c]), split3(qr_ref[c])
        gs = split3(g)
        gt = split3(g.T)
        new_left = beta_stats * l_ref[c] + (1.0 - beta_stats) * prod(gs, gs, NT)
        new_right = beta_stats * r_ref[c] + (1.0 - beta_stats) * prod(gt, gt, NT)
        nl_ref[c] = new_left
        nr_ref[c] = new_right
        half = prod(gt, ql, NN)
        rot = prod(split3(half.T), qr, NN)
        first = beta_one * f_ref[c] + (1.0 - beta_one) * rot
        second = beta_two * s_ref[c] + (1.0 - beta_two) * rot * rot
        nf_ref[c] = first
        ns_ref[c] = second
        direction = first / (1.0 - beta_one**STEP) / (
            jnp.sqrt(second / (1.0 - beta_two**STEP)) + adam_eps)
        moved = prod(split3(prod(ql, split3(direction), NN)), qr, NT)
        master = m_ref[c]
        nm_ref[c] = master - learn_rate * (moved + weight_decay * master)
        a_scr[0, step * chunk + c] = prod(split3(new_left), ql, NN)
        a_scr[1, step * chunk + c] = prod(split3(new_right), qr, NN)

    @pl.when(step == pl.num_programs(0) - 1)
    def _():
        def bring(i, _):
            for s in range(2):
                slab = a_scr[s, :, pl.ds(i, 1), :].reshape(128, block)
                t_scr[s, i] = slab.T
            return 0
        lax.fori_loop(0, block, bring, 0, unroll=4)
        sub = lax.broadcasted_iota(jnp.int32, (8, 128), 0)
        norms = [[None] * tiles, [None] * tiles]
        for kt in range(tiles):
            def one(kk, carry):
                k = kt * 8 + kk
                acc = [[jnp.zeros((8, 128), F32) for _ in range(kt, tiles)] for _ in range(2)]
                for i in range(block):
                    for s in range(2):
                        row = jnp.broadcast_to(t_scr[s, i, pl.ds(k, 1), :], (8, 128))
                        for j in range(kt, tiles):
                            acc[s][j - kt] += row * t_scr[s, i, 8 * j : 8 * j + 8, :]
                out = []
                for s in range(2):
                    here = sub == kk
                    size = jnp.sum(jnp.where(here, acc[s][0], 0.0), axis=0, keepdims=True)
                    size = jnp.broadcast_to(size, (8, 128))
                    inv = 1.0 / size
                    acc[s] = [v * inv for v in acc[s]]
                    acc[s][0] = jnp.where(sub > kk, acc[s][0], 0.0)
                    out.append(jnp.where(here, size, carry[s]))
                for i in range(block):
                    for s in range(2):
                        row = jnp.broadcast_to(t_scr[s, i, pl.ds(k, 1), :], (8, 128))
                        for j in range(kt, tiles):
                            t_scr[s, i, 8 * j : 8 * j + 8, :] -= row * acc[s][j - kt]
                return tuple(out)
            res = lax.fori_loop(0, 8, one, (jnp.ones((8, 128), F32),) * 2)
            for s in range(2):
                norms[s][kt] = lax.rsqrt(res[s])
        scale = [jnp.concatenate(norms[s], axis=0) for s in range(2)]
        def back(i, _):
            for s, ref in ((0, bl_ref), (1, br_ref)):
                done = (t_scr[s, i] * scale[s]).T
                ref[:, pl.ds(i, 1), :] = done[:count].reshape(count, 1, block)
            return 0
        lax.fori_loop(0, block, back, 0, unroll=4)

def soap(g, m, f, s, l, r, ql, qr):
    count, block = g.shape[0], g.shape[-1]
    chunk = math.gcd(count, 8)
    spec = pl.BlockSpec((chunk, block, block), lambda i: (i, 0, 0))
    whole = pl.BlockSpec((count, block, block), lambda i: (0, 0, 0))
    shape = jax.ShapeDtypeStruct(g.shape, F32)
    return pl.pallas_call(
        functools.partial(soap_kernel, count, chunk, block),
        grid=(count // chunk,),
        in_specs=[spec] * 8,
        out_specs=[spec] * 5 + [whole] * 2,
        out_shape=[shape] * 7,
        scratch_shapes=[pltpu.VMEM((2, 128, block, block), F32), pltpu.VMEM((2, block, block, 128), F32)],
        compiler_params=pltpu.CompilerParams(vmem_limit_bytes=48 * 2**20),
        name="soap",
    )(g, m, f, s, l, r, ql, qr)


MESH = pl.DeviceIdType.MESH
VM = pl.BlockSpec(memory_space=pltpu.VMEM)
MIB = 2**20


def tiles_up(value):
    return -(-value // 128) * 128


def remote(src, dst, send, recv, where):
    return pltpu.make_async_remote_copy(
        src_ref=src, dst_ref=dst, send_sem=send, recv_sem=recv, device_id=where, device_id_type=MESH
    )


def greet(devices):
    barrier = pltpu.get_barrier_semaphore()
    for device in devices:
        pl.semaphore_signal(barrier, inc=1, device_id=device, device_id_type=MESH)
    pl.semaphore_wait(barrier, len(devices))


def line_greet(dp, t, m):
    place, side = dp // 2, lax.rem(dp, 2)
    barrier = pltpu.get_barrier_semaphore()
    pl.semaphore_signal(barrier, inc=1, device_id=(place * 2 + 1 - side, t), device_id_type=MESH)

    @pl.when(place > 0)
    def _():
        pl.semaphore_signal(barrier, inc=1, device_id=(dp - 2, t), device_id_type=MESH)

    @pl.when(place < m - 1)
    def _():
        pl.semaphore_signal(barrier, inc=1, device_id=(dp + 2, t), device_id_type=MESH)

    ends = (place == 0).astype(jnp.int32) + (place == m - 1).astype(jnp.int32)
    pl.semaphore_wait(barrier, 3 - ends)


def gather_kernel(n, count, block, wide, norm_rows, m_ref, norm_ref, u_ref, nout_ref, held, send_sem, recv_sem):
    m = n // 2
    dp, t = lax.axis_index("dp"), lax.axis_index("tensor")
    place, side = dp // 2, lax.rem(dp, 2)
    pair = (place * 2 + 1 - side, t)
    for k in range(count):
        held[dp, :, k * block : (k + 1) * block] = m_ref[k].astype(BF16)
    if wide > count * block:
        held[dp, :, count * block : wide] = jnp.zeros((block, wide - count * block), BF16)
    held[dp, :, wide : wide + 128] = jnp.concatenate(
        [norm_ref[...], jnp.zeros((block - norm_rows, 128), F32)], axis=0
    ).astype(BF16)
    line_greet(dp, t, m)

    def send(source, way, where):
        return remote(held.at[source], held.at[source], send_sem.at[source, way], recv_sem.at[source], where)

    def unpack(source):
        for k in range(count):
            u_ref[source * count + k] = held[source, :, k * block : (k + 1) * block]
        nout_ref[source] = held[source, :16, wide : wide + 128]

    def spread(source, left, right):
        send(source, 2, pair).start()

        @pl.when(left)
        def _():
            send(source, 0, (dp - 2, t)).start()

        @pl.when(right)
        def _():
            send(source, 1, (dp + 2, t)).start()

    def spread_done(source, left, right):
        send(source, 2, pair).wait_send()

        @pl.when(left)
        def _():
            send(source, 0, (dp - 2, t)).wait_send()

        @pl.when(right)
        def _():
            send(source, 1, (dp + 2, t)).wait_send()

    spread(dp, place > 0, place < m - 1)
    unpack(dp)

    def one(hop, _):
        @pl.when(place - hop >= 0)
        def _():
            source = dp - 2 * hop
            send(source, 2, pair).wait_recv()
            spread(source, False, place < m - 1)

        @pl.when(place + hop < m)
        def _():
            source = dp + 2 * hop
            send(source, 2, pair).wait_recv()
            spread(source, place > 0, False)

        @pl.when(place - hop >= 0)
        def _():
            unpack(dp - 2 * hop)

        @pl.when(place + hop < m)
        def _():
            unpack(dp + 2 * hop)

        return 0

    lax.fori_loop(1, m, one, 0)

    def other(step, _):
        source = step * 2 + 1 - side
        send(source, 2, pair).wait_recv()
        unpack(source)
        return 0

    lax.fori_loop(0, m, other, 0)

    def finish(step, _):
        source = step * 2 + side
        spread_done(
            source,
            (place > 0) & (step >= place),
            (place < m - 1) & (step <= place),
        )
        return 0

    lax.fori_loop(0, m, finish, 0)


def gather_masters(masters, norm, n):
    count, block = masters.shape[0], masters.shape[-1]
    wide = tiles_up(count * block)
    norm_rows = -(-norm.shape[0] // 128)
    norm_tile = jnp.pad(norm, (0, norm_rows * 128 - norm.shape[0])).reshape(norm_rows, 128)
    blocks, norms = pl.pallas_call(
        functools.partial(gather_kernel, n, count, block, wide, norm_rows),
        out_shape=[
            jax.ShapeDtypeStruct((n * count, block, block), BF16),
            jax.ShapeDtypeStruct((n, 16, 128), BF16),
        ],
        in_specs=[VM, VM],
        out_specs=[VM, VM],
        scratch_shapes=[
            pltpu.VMEM((n, block, wide + 128), BF16),
            pltpu.SemaphoreType.DMA((n, 3)),
            pltpu.SemaphoreType.DMA((n,)),
        ],
        compiler_params=pltpu.CompilerParams(collective_id=1, has_side_effects=True, vmem_limit_bytes=10 * MIB),
        name="gather_masters",
    )(masters, norm_tile)
    return blocks, norms.reshape(n, 16 * 128)[:, : norm.shape[0]].reshape(-1)


def assemble_kernel(rows, cols, block, cuts, slot_ref, u_ref, *w_refs):
    def one(row, _):
        for first, last, w_ref in zip(cuts, cuts[1:], w_refs):
            strip = jnp.concatenate([u_ref[slot_ref[row * cols + c]] for c in range(first, last)], axis=1)
            w_ref[pl.ds(pl.multiple_of(row * block, block), block), :] = strip
        return 0

    lax.fori_loop(0, rows, one, 0)


def piece_cuts(rows, cols, parts):
    attn = rows // parts
    hidden = (cols - 4 * attn) // 2
    return (0, 3 * attn, 3 * attn + hidden, 4 * attn + hidden, cols)


def assemble(slots, blocks, rows, parts):
    block = blocks.shape[-1]
    cols = blocks.shape[0] // rows
    cuts = piece_cuts(rows, cols, parts)
    return pl.pallas_call(
        functools.partial(assemble_kernel, rows, cols, block, cuts),
        out_shape=[
            jax.ShapeDtypeStruct((rows * block, (last - first) * block), BF16)
            for first, last in zip(cuts, cuts[1:])
        ],
        in_specs=[pl.BlockSpec(memory_space=pltpu.SMEM), VM],
        out_specs=[VM] * 4,
        compiler_params=pltpu.CompilerParams(vmem_limit_bytes=4 * MIB),
        name="assemble",
    )(slots, blocks)


def disperse_kernel(rows, cols, block, cuts, n, count, wide, inverse_ref, *refs):
    g_refs, p_ref, u_scr = refs[:4], refs[4], refs[5]

    def cut(row, _):
        for first, last, g_ref in zip(cuts, cuts[1:], g_refs):
            strip = g_ref[pl.ds(pl.multiple_of(row * block, block), block), :]
            for c in range(first, last):
                u_scr[row * cols + c] = strip[:, (c - first) * block : (c - first + 1) * block]
        return 0

    lax.fori_loop(0, rows, cut, 0)

    def lay(d, _):
        for k in range(count):
            p_ref[d, :, k * block : (k + 1) * block] = u_scr[inverse_ref[d * count + k]]
        if wide > count * block:
            p_ref[d, :, count * block : wide] = jnp.zeros((block, wide - count * block), BF16)
        return 0

    lax.fori_loop(0, n, lay, 0)


def disperse(inverse, grads, n, block, parts):
    rows = grads[0].shape[0] // block
    cols = sum(grad.shape[1] for grad in grads) // block
    count = rows * cols // n
    wide = tiles_up(count * block)
    return pl.pallas_call(
        functools.partial(
            disperse_kernel, rows, cols, block, piece_cuts(rows, cols, parts), n, count, wide
        ),
        out_shape=jax.ShapeDtypeStruct((n, block, wide), BF16),
        in_specs=[pl.BlockSpec(memory_space=pltpu.SMEM)] + [VM] * 4,
        out_specs=VM,
        scratch_shapes=[pltpu.VMEM((rows * cols, block, block), BF16)],
        compiler_params=pltpu.CompilerParams(vmem_limit_bytes=16 * MIB),
        name="disperse",
    )(inverse, *grads)


BLK = 128


def plain_norm(rows):
    centered = rows - jnp.mean(rows, axis=-1, keepdims=True)
    inverse_std = lax.rsqrt(jnp.mean(centered * centered, axis=-1, keepdims=True) + norm_eps)
    return centered * inverse_std, inverse_std


def dot(left, right, dims):
    return lax.dot_general(left, right, (dims, ((), ())), preferred_element_type=F32)


class Total:
    def __init__(self, dp, t, x, near, mine, far, near_mine, near_far, sems):
        up, core = t // 2, lax.rem(t, 2)
        self.core = core
        self.beside = (dp, up * 2 + 1 - core)
        self.over = (dp, (1 - up) * 2 + core)
        self.x, self.near, self.mine, self.far = x, near, mine, far
        self.near_mine, self.near_far, self.sems = near_mine, near_far, sems
        self.blocks = sems.shape[1]
        self.size = x.shape[0] // self.blocks
        self.half = self.size // 2

    def rows(self, b, core):
        return pl.ds(pl.multiple_of(b * self.size + core * self.half, self.half), self.half)

    def part(self, b):
        return pl.ds(pl.multiple_of(b * self.half, self.half), self.half)

    def copy(self, kind, b):
        here = self.part(b)
        src, dst, where = (
            (self.x.at[self.rows(b, 1 - self.core)], self.near, self.beside),
            (self.mine.at[here], self.far, self.over),
            (self.mine.at[here], self.near_mine, self.beside),
            (self.far.at[here], self.near_far, self.beside),
        )[kind]
        return remote(src, dst.at[here], self.sems.at[2 * kind, b], self.sems.at[2 * kind + 1, b], where)

    def enter(self, b):
        self.copy(0, b).start()

    def add(self, b):
        here = self.part(b)
        self.copy(0, b).wait_recv()
        self.mine[here] = (self.x[self.rows(b, self.core)].astype(F32) + self.near[here].astype(F32)).astype(BF16)

    def cross(self, b):
        self.copy(1, b).start()
        self.copy(2, b).start()

    def relay(self, b):
        self.copy(1, b).wait_recv()
        self.copy(3, b).start()

    def arrived(self, b):
        self.copy(2, b).wait_recv()
        self.copy(3, b).wait_recv()

    def sums(self, b):
        here = self.part(b)
        own = self.mine[here].astype(F32) + self.far[here].astype(F32)
        other = self.near_mine[here].astype(F32) + self.near_far[here].astype(F32)
        low = self.core == 0
        return jnp.concatenate([jnp.where(low, own, other), jnp.where(low, other, own)], axis=0)

    def close(self, b):
        for kind in range(4):
            self.copy(kind, b).wait_send()


def layer_kernel(
    heads,
    shift,
    x_ref,
    seg_row_ref,
    seg_col_ref,
    dy_ref,
    wp_ref,
    w1_ref,
    wo_ref,
    w2_ref,
    norm_ref,
    gp_ref,
    g1_ref,
    go_ref,
    g2_ref,
    out_ref,
    da_ref,
    resid_ref,
    dres_ref,
    ng_ref,
    a_ref,
    wf_ref,
    qkv_ref,
    pen_ref,
    lse_ref,
    o_ref,
    cn_ref,
    s_ref,
    du_ref,
    dhb_ref,
    dproj_ref,
    dkv_ref,
    carry_ref,
    x1_ref,
    near1,
    mine1,
    far1,
    near_mine1,
    near_far1,
    sem1,
    x3_ref,
    near3,
    mine3,
    far3,
    near_mine3,
    near_far3,
    sem3,
    gf_ref,
    gf_near,
    gf_far,
    share_sem,
    collect_sem,
):
    dp, t = lax.axis_index("dp"), lax.axis_index("tensor")
    up, core = t // 2, lax.rem(t, 2)
    beside, over = (dp, up * 2 + 1 - core), (dp, (1 - up) * 2 + core)
    length, width = x_ref.shape
    blocks = length // BLK
    span = min(length // 2 + BLK, length)
    attn = heads * HD
    one = Total(dp, t, x1_ref, near1, mine1, far1, near_mine1, near_far1, sem1)
    three = Total(dp, t, x3_ref, near3, mine3, far3, near_mine3, near_far3, sem3)
    greet([beside, over])

    def give(where, i):
        return remote(wf_ref, wf_ref, share_sem.at[i], share_sem.at[2], where)

    @pl.when(t == 0)
    def _():
        wf_ref[:, :HD] = wp_ref[:, :HD]
        wf_ref[:, HD:] = wp_ref[:, attn : attn + HD]
        give(over, 0).start()
        give(beside, 1).start()

    def rows_of(b):
        return pl.ds(pl.multiple_of(b * BLK, BLK), BLK)

    gain_one, bias_one = norm_ref[0:1, :], norm_ref[1:2, :]
    gain_two, bias_two = norm_ref[2:3, :], norm_ref[3:4, :]
    wide = 2 * BLK

    def wide_rows(i):
        return pl.ds(pl.multiple_of(i * wide, wide), wide)

    def project(i, _):
        rows = wide_rows(i)
        plain, _ = plain_norm(x_ref[rows].astype(F32))
        a = (plain * gain_one + bias_one).astype(BF16)
        a_ref[rows] = a
        projected = dot(a, wp_ref[...], NN)
        for h in range(heads):
            qkv_ref[h, rows] = projected[:, h * HD : (h + 1) * HD].astype(BF16) * 0.125
        for h in range(heads, 3 * heads):
            qkv_ref[h, rows] = projected[:, h * HD : (h + 1) * HD].astype(BF16)
        return 0

    lax.fori_loop(0, length // wide, project, 0)

    @pl.when(t == 2)
    def _():
        give(over, 0).wait_recv()
        give(beside, 1).start()

    @pl.when((t == 1) | (t == 3))
    def _():
        give(beside, 1).wait_recv()

    def project_first(i, _):
        rows = wide_rows(i)
        projected = dot(a_ref[rows], wf_ref[...], NN)
        qkv_ref[3 * heads, rows] = projected[:, :HD].astype(BF16) * 0.125
        qkv_ref[3 * heads + 1, rows] = projected[:, HD:].astype(BF16)
        return 0

    lax.fori_loop(0, length // wide, project_first, 0)

    row_in = lax.broadcasted_iota(jnp.int32, (BLK, 1), 0)
    col_in = lax.broadcasted_iota(jnp.int32, (1, span), 1)
    square_row = lax.broadcasted_iota(jnp.int32, (BLK, BLK), 0)
    square_col = lax.broadcasted_iota(jnp.int32, (BLK, BLK), 1)
    earlier = (square_col < square_row).astype(F32).astype(BF16)
    later = (square_col > square_row).astype(F32).astype(BF16)

    def window(b):
        start = pl.multiple_of(jnp.maximum(b * BLK + BLK - span, 0), BLK)
        return start, pl.ds(start, span)

    def masks(b):
        start, keys = window(b)
        same = seg_col_ref[rows_of(b)] == seg_row_ref[:, keys]
        behind = (row_in + (b * BLK - start)) - col_in
        return same & (behind >= 0), same & (behind > 0)

    def two_part(matrix, values):
        high = values.astype(BF16)
        low = (values - high.astype(F32)).astype(BF16)
        return dot(matrix, high, NN) + dot(matrix, low, NN)

    carry_ref[...] = jnp.zeros_like(carry_ref)

    def attend(b, _):
        rows = rows_of(b)
        _, keys = window(b)
        allowed, strict = masks(b)
        first = dot(qkv_ref[3 * heads, rows], qkv_ref[3 * heads + 1, keys], NT) - shift
        soft = jnp.maximum(first, 0.0) + jnp.log1p(jnp.exp(-jnp.abs(first)))
        picks = jnp.where(strict, soft, 0.0)
        before = carry_ref[0:1, keys]
        penalty = (two_part(earlier, picks) + before).astype(BF16)
        carry_ref[0:1, keys] = before + jnp.sum(picks, axis=0, keepdims=True)
        pen_ref[rows] = penalty
        penalty = penalty.astype(F32)
        mixed = []
        for h in range(heads):
            raw = dot(qkv_ref[h, rows], qkv_ref[heads + h, keys], NT)
            logits = jnp.where(allowed, raw - penalty, -1e30)
            top = jnp.max(logits, axis=-1, keepdims=True)
            weights = jnp.exp(logits - top)
            total = jnp.sum(weights, axis=-1, keepdims=True)
            lse_ref[h, rows] = top + jnp.log(total)
            probs = (weights * (1.0 / total)).astype(BF16)
            mixed.append(dot(probs, qkv_ref[2 * heads + h, keys], NN))
        o = jnp.concatenate(mixed, axis=1).astype(BF16)
        o_ref[rows] = o
        x1_ref[rows] = dot(o, wo_ref[...], NT).astype(BF16)
        one.enter(b)

        @pl.when(b > 0)
        def _():
            one.add(b - 1)
            one.cross(b - 1)

        return 0

    lax.fori_loop(0, blocks, attend, 0)
    one.add(blocks - 1)
    one.cross(blocks - 1)

    def act_back(i, _):
        rows = wide_rows(i)
        dres_ref[rows] = dot(dy_ref[rows], w2_ref[...], NN)
        return 0

    lax.fori_loop(0, length // wide, act_back, 0)

    def mlp(b, _):
        @pl.when(b == 0)
        def _():
            one.relay(0)

        @pl.when(b < blocks - 1)
        def _():
            one.relay(b + 1)

        @pl.when(b == blocks - 2)
        def _():
            for early in (0, 1):
                three.add(early)
                three.cross(early)

        one.arrived(b)
        rows = rows_of(b)
        resid = x_ref[rows].astype(F32) + one.sums(b)
        resid_ref[rows] = resid
        plain, _ = plain_norm(resid)
        cn = (plain * gain_two + bias_two).astype(BF16)
        cn_ref[rows] = cn
        u = dot(cn, w1_ref[...], NN)
        root = math.sqrt(2.0 / math.pi)
        square = u * u
        bent = jnp.tanh(root * u * (1.0 + 0.044715 * square))
        half = 0.5 * (1.0 + bent)
        s_ref[rows] = (u * half).astype(BF16)
        slope = half + 0.5 * u * (1.0 - bent * bent) * (root * (1.0 + 3 * 0.044715 * square))
        du = (dres_ref[rows] * slope).astype(BF16)
        du_ref[rows] = du
        x3_ref[rows] = dot(du, w1_ref[...], NT).astype(BF16)
        three.enter(b)
        return 0

    lax.fori_loop(0, blocks, mlp, 0)

    def cross_back(i, _):
        three.add(blocks - 1 - i)
        three.cross(blocks - 1 - i)
        return 0

    lax.fori_loop(0, blocks - 2, cross_back, 0)
    g2_ref[...] = dot(dy_ref[...], s_ref[...], TN).astype(BF16)
    g1_ref[...] = dot(cn_ref[...], du_ref[...], TN).astype(BF16)

    for early in (0, 1):
        three.relay(early)
    three.relay(blocks - 1)
    ng_ref[...] = jnp.zeros_like(ng_ref)
    carry_ref[...] = jnp.zeros_like(carry_ref)
    dkv_ref[...] = jnp.zeros_like(dkv_ref)

    def back(i, _):
        b = blocks - 1 - i

        @pl.when(b > 2)
        def _():
            three.relay(b - 1)

        three.arrived(b)
        rows = rows_of(b)
        _, keys = window(b)
        plain, inverse_std = plain_norm(resid_ref[rows])
        d_two = three.sums(b)
        ng_ref[0:1, :] += jnp.sum(d_two * plain, axis=0, keepdims=True)
        ng_ref[1:2, :] += jnp.sum(d_two, axis=0, keepdims=True)
        dres = dy_ref[rows].astype(F32) + norm_back(plain, inverse_std, d_two * gain_two)
        dres_ref[rows] = dres
        dhb = dres.astype(BF16)
        dhb_ref[rows] = dhb
        do = dot(dhb, wo_ref[...], NN).astype(BF16)
        allowed, strict = masks(b)
        penalty = pen_ref[rows].astype(F32)
        total = None
        dq = []
        for h in range(heads):
            q, k, v = qkv_ref[h, rows], qkv_ref[heads + h, keys], qkv_ref[2 * heads + h, keys]
            do_h = do[:, h * HD : (h + 1) * HD]
            logits = jnp.where(allowed, dot(q, k, NT) - penalty, -1e30)
            probs = jnp.exp(logits - lse_ref[h, rows])
            dprobs = dot(do_h, v, NT)
            inner = jnp.sum(dprobs * probs, axis=-1, keepdims=True)
            dlogits = probs * (dprobs - inner)
            total = dlogits if total is None else total + dlogits
            draw = dlogits.astype(BF16)
            dq.append(dot(draw, k, NN) * 0.125)
            dkv_ref[h * HD : (h + 1) * HD, keys] += dot(q, draw, TN)
            dkv_ref[attn + h * HD : attn + (h + 1) * HD, keys] += dot(do_h, probs.astype(BF16), TN)
        q, k = qkv_ref[3 * heads, rows], qkv_ref[3 * heads + 1, keys]
        first = dot(q, k, NT) - shift
        picked = 1.0 / (1.0 + jnp.exp(-first))
        after = carry_ref[0:1, keys]
        suffix = two_part(later, total) + after
        carry_ref[0:1, keys] = after + jnp.sum(total, axis=0, keepdims=True)
        draw = jnp.where(strict, -picked * suffix, 0.0).astype(BF16)
        dq.append(dot(draw, k, NN) * 0.125)
        dkv_ref[2 * attn : 2 * attn + HD, keys] += dot(q, draw, TN)
        dproj_ref[rows, :attn] = jnp.concatenate(dq[:heads], axis=1).astype(BF16)
        dproj_ref[rows, 3 * attn : 3 * attn + HD] = dq[heads].astype(BF16)
        return 0

    lax.fori_loop(0, blocks, back, 0)
    turned = dkv_ref[...].T.astype(BF16)
    dproj_ref[:, attn : 3 * attn] = turned[:, : 2 * attn]
    dproj_ref[:, 3 * attn + HD : 3 * attn + 2 * HD] = turned[:, 2 * attn :]

    def collect(src, dst, where, i):
        return remote(src, dst, collect_sem.at[i], collect_sem.at[i + 2], where)

    gf_ref[...] = dot(a_ref[...], dproj_ref[:, 3 * attn :], TN).astype(BF16)

    @pl.when(core == 1)
    def _():
        collect(gf_ref, gf_near, beside, 0).start()

    @pl.when(core == 0)
    def _():
        collect(gf_ref, gf_near, beside, 0).wait_recv()
        gf_ref[...] = (gf_ref[...].astype(F32) + gf_near[...].astype(F32)).astype(BF16)

    @pl.when(t == 2)
    def _():
        collect(gf_ref, gf_far, over, 1).start()

    go_ref[...] = dot(dhb_ref[...], o_ref[...], TN).astype(BF16)
    grad = dot(a_ref[...], dproj_ref[:, : 3 * attn], TN)
    gp_ref[...] = grad.astype(BF16)

    def finish(i, _):
        rows = wide_rows(i)
        out_ref[rows] = dot(s_ref[rows], w2_ref[...], NT).astype(BF16)
        da = dot(dproj_ref[rows, : 3 * attn], wp_ref[...], NT)
        da_ref[rows] = (da + dot(dproj_ref[rows, 3 * attn :], wf_ref[...], NT)).astype(BF16)
        return 0

    lax.fori_loop(0, length // wide, finish, 0)

    @pl.when(t == 0)
    def _():
        collect(gf_ref, gf_far, over, 1).wait_recv()
        extra = gf_ref[...].astype(F32) + gf_far[...].astype(F32)
        gp_ref[:, :HD] = (gp_ref[:, :HD].astype(F32) + extra[:, :HD]).astype(BF16)
        gp_ref[:, attn : attn + HD] = (gp_ref[:, attn : attn + HD].astype(F32) + extra[:, HD:]).astype(BF16)
        give(over, 0).wait_send()

    @pl.when(core == 0)
    def _():
        give(beside, 1).wait_send()

    @pl.when(core == 1)
    def _():
        collect(gf_ref, gf_near, beside, 0).wait_send()

    @pl.when(t == 2)
    def _():
        collect(gf_ref, gf_far, over, 1).wait_send()

    def close(b, _):
        one.close(b)
        three.close(b)
        return 0

    lax.fori_loop(0, blocks, close, 0)


def layer(inputs, segments, cotangent, wp, w1, wo, w2, norms):
    length, width = inputs.shape
    attn, hidden = wo.shape[1], w1.shape[1]
    heads = attn // HD
    blocks = length // BLK
    span = min(length // 2 + BLK, length)

    def low(*shape):
        return pltpu.VMEM(shape, BF16)

    half = length // 2
    total = [low(length, width)] + [low(half, width)] * 5 + [pltpu.SemaphoreType.DMA((8, blocks))]

    def out(shape, dtype):
        return jax.ShapeDtypeStruct(shape, dtype)

    return pl.pallas_call(
        functools.partial(layer_kernel, heads, shift_for(length)),
        out_shape=[
            out(wp.shape, BF16),
            out(w1.shape, BF16),
            out(wo.shape, BF16),
            out(w2.shape, BF16),
            out((length, width), BF16),
            out((length, width), BF16),
            out((length, width), F32),
            out((length, width), F32),
            out((2, width), F32),
        ],
        in_specs=[VM] * 9,
        out_specs=[VM] * 9,
        scratch_shapes=[
            low(length, width),
            low(width, 2 * HD),
            low(3 * heads + 2, length, HD),
            low(length, span),
            pltpu.VMEM((heads, length, 1), F32),
            low(length, attn),
            low(length, width),
            low(length, hidden),
            low(length, hidden),
            low(length, width),
            low(length, 3 * attn + 2 * HD),
            pltpu.VMEM((2 * attn + HD, length), F32),
            pltpu.VMEM((8, length), F32),
        ]
        + total
        + total
        + [low(width, 2 * HD)] * 3
        + [pltpu.SemaphoreType.DMA((3,)), pltpu.SemaphoreType.DMA((4,))],
        compiler_params=pltpu.CompilerParams(
            collective_id=3, has_side_effects=True, vmem_limit_bytes=LAYER_LIMIT
        ),
        name="layer",
    )(
        inputs,
        segments.reshape(1, length),
        segments.reshape(length, 1),
        cotangent,
        wp,
        w1,
        wo,
        w2,
        norms,
    )


def settle_kernel(
    n,
    p_ref,
    out_in,
    da_in,
    resid_ref,
    dres_ref,
    x_ref,
    norm_ref,
    ng_in,
    g_ref,
    output_ref,
    grad_ref,
    ng_ref,
    xin,
    lin,
    rin,
    x_send,
    x_recv,
    l_send,
    l_recv,
    r_send,
    r_recv,
    near4,
    mine4,
    far4,
    near_mine4,
    near_far4,
    sem4,
    near2,
    mine2,
    far2,
    near_mine2,
    near_far2,
    sem2,
    norm_held,
    norm_send,
    norm_recv,
):
    m = n // 2
    dp, t = lax.axis_index("dp"), lax.axis_index("tensor")
    place, side = dp // 2, lax.rem(dp, 2)
    pair = (place * 2 + 1 - side, t)
    four = Total(dp, t, da_in, near4, mine4, far4, near_mine4, near_far4, sem4)
    two = Total(dp, t, out_in, near2, mine2, far2, near_mine2, near_far2, sem2)
    blocks = four.blocks
    peers = [lax.rem(dp + hop, n) for hop in range(1, n)]
    greet([four.beside, four.over] + [(peer, t) for peer in peers])

    def across(q):
        return remote(p_ref.at[q * 2 + 1 - side], xin.at[q], x_send.at[q], x_recv.at[q], pair)

    def rightward(q):
        return remote(lin.at[q], lin.at[q], r_send.at[q], l_recv.at[q], (dp + 2, t))

    def leftward(q):
        return remote(rin.at[q], rin.at[q], l_send.at[q], r_recv.at[q], (dp - 2, t))

    def both(hop, one):
        @pl.when(place + hop < m)
        def _():
            one(place + hop, True)

        if hop > 0:
            @pl.when(place - hop >= 0)
            def _():
                one(place - hop, False)

    def work(q, right):
        across(q).wait_recv()
        own = p_ref[q * 2 + side].astype(F32) + xin[q].astype(F32)
        if right:
            @pl.when(place > 0)
            def _():
                rightward(q).wait_recv()
                lin[q] = (own + lin[q].astype(F32)).astype(BF16)

            @pl.when(place == 0)
            def _():
                lin[q] = own.astype(BF16)

            rightward(q).start()
        else:
            @pl.when(place < m - 1)
            def _():
                leftward(q).wait_recv()
                rin[q] = (own + rin[q].astype(F32)).astype(BF16)

            @pl.when(place == m - 1)
            def _():
                rin[q] = own.astype(BF16)

            leftward(q).start()

    def keep():
        q = place
        across(q).wait_recv()
        g_ref[...] = p_ref[q * 2 + side].astype(F32) + xin[q].astype(F32)

        @pl.when(place > 0)
        def _():
            rightward(q).wait_recv()
            g_ref[...] += lin[q].astype(F32)

        @pl.when(place < m - 1)
        def _():
            leftward(q).wait_recv()
            g_ref[...] += rin[q].astype(F32)

    def norm_copy(peer):
        return remote(ng_ref, norm_held.at[dp], norm_send.at[peer], norm_recv.at[dp], (peer, t))

    def norm_from(peer):
        return remote(ng_ref, norm_held.at[peer], norm_send.at[peer], norm_recv.at[peer], (peer, t))

    for hop in reversed(range(m)):
        both(hop, lambda q, right: across(q).start())
    for b in range(blocks):
        four.enter(b)
    for b in range(blocks):
        two.enter(b)
    for b in range(blocks):
        four.add(b)
        four.cross(b)
    for b in range(blocks):
        two.add(b)
        two.cross(b)
    ng_ref[...] = jnp.zeros_like(ng_ref)
    gain = norm_ref[0:1, :]

    def rows_of(b):
        return pl.ds(b * four.size, four.size)

    def grad_block(b):
        rows = rows_of(b)
        four.arrived(b)
        d_one = four.sums(b)
        plain, inverse_std = plain_norm(x_ref[rows].astype(F32))
        ng_ref[0:1, :] += jnp.sum(d_one * plain, axis=0, keepdims=True)
        ng_ref[1:2, :] += jnp.sum(d_one, axis=0, keepdims=True)
        grad_ref[rows] = dres_ref[rows] + norm_back(plain, inverse_std, d_one * gain)

    def out_block(b):
        rows = rows_of(b)
        two.arrived(b)
        output_ref[rows] = (resid_ref[rows] + two.sums(b)).astype(BF16)

    def norms_out():
        ng_ref[2:4, :] = ng_in[...]
        for peer in peers:
            norm_copy(peer).start()

    def norms_in():
        for peer in peers:
            norm_from(peer).wait_recv()
        total = None
        for source in range(n):
            term = jnp.where(dp == source, ng_ref[...], norm_held[source])
            total = term if total is None else total + term
        for peer in peers:
            norm_copy(peer).wait_send()
        ng_ref[...] = total

    tasks = []
    for b in range(blocks):
        tasks.append(functools.partial(four.relay, b))
        if b > 0:
            tasks.append(functools.partial(grad_block, b - 1))
    tasks.append(functools.partial(grad_block, blocks - 1))
    tasks.append(norms_out)
    for b in range(blocks):
        tasks.append(functools.partial(two.relay, b))
        if b > 0:
            tasks.append(functools.partial(out_block, b - 1))
    tasks.append(functools.partial(out_block, blocks - 1))
    done = 0
    for step, hop in enumerate(reversed(range(1, m))):
        until = len(tasks) * (step + 1) // m
        while done < until:
            tasks[done]()
            done += 1
        both(hop, work)
    while done < len(tasks):
        tasks[done]()
        done += 1
    keep()
    norms_in()

    def finish(q, _):
        across(q).wait_send()

        @pl.when(q > place)
        def _():
            rightward(q).wait_send()

        @pl.when(q < place)
        def _():
            leftward(q).wait_send()

        return 0

    lax.fori_loop(0, m, finish, 0)
    for b in range(blocks):
        four.close(b)
        two.close(b)


def settle(packed, out_part, da_part, resid, dres, inputs, norms, ng):
    n, block, wide = packed.shape
    m = n // 2
    length, width = inputs.shape
    blocks = 4

    def low(*shape):
        return pltpu.VMEM(shape, BF16)

    half = length // 2
    total = [low(half, width)] * 5 + [pltpu.SemaphoreType.DMA((8, blocks))]
    return pl.pallas_call(
        functools.partial(settle_kernel, n),
        out_shape=[
            jax.ShapeDtypeStruct((block, wide), F32),
            jax.ShapeDtypeStruct((length, width), BF16),
            jax.ShapeDtypeStruct((length, width), F32),
            jax.ShapeDtypeStruct((4, width), F32),
        ],
        in_specs=[VM] * 8,
        out_specs=[VM] * 4,
        scratch_shapes=[low(m, block, wide)] * 3
        + [pltpu.SemaphoreType.DMA((m,))] * 6
        + total
        + total
        + [pltpu.VMEM((n, 4, width), F32), pltpu.SemaphoreType.DMA((n,)), pltpu.SemaphoreType.DMA((n,))],
        compiler_params=pltpu.CompilerParams(
            collective_id=2, has_side_effects=True, vmem_limit_bytes=24 * MIB
        ),
        name="settle",
    )(packed, out_part, da_part, resid, dres, inputs, norms, ng)


def norm_update(grad, master, first, second):
    new_first = beta_one * first + (1.0 - beta_one) * grad
    new_second = beta_two * second + (1.0 - beta_two) * grad * grad
    direction = (
        new_first
        / (1.0 - beta_one**STEP)
        / (jnp.sqrt(new_second / (1.0 - beta_two**STEP)) + adam_eps)
    )
    return (new_first, new_second, master - norm_rate * direction)


def body(
    inputs,
    segments,
    cotangent,
    owner,
    masters,
    first_moment,
    second_moment,
    left_stats,
    right_stats,
    left_basis,
    right_basis,
    norm_master,
    norm_first,
    norm_second,
):
    length = inputs.shape[1]
    width = inputs.shape[2]
    n_dp = lax.axis_size("dp")
    parts = lax.axis_size("tensor")
    per_dev = masters.shape[1]
    block = masters.shape[-1]
    blocks, shared_norms = gather_masters(masters[0], norm_master, n_dp)
    slots, inverse = block_slots(owner, per_dev)
    pieces = assemble(slots, blocks, width // block, parts)
    norms = shared_norms.astype(F32).reshape(4, width)
    *grads, out_part, da_part, resid, dres, norm_grads = layer(
        inputs[0], segments[0], cotangent[0], *pieces, norms
    )
    packed = disperse(inverse, grads, n_dp, block, parts)
    own_packed, output, input_grad, norm_grads = settle(
        packed, out_part, da_part, resid, dres, inputs[0], norms, norm_grads
    )
    own_grads = own_packed[:, : per_dev * block].reshape(block, per_dev, block).transpose(1, 0, 2)
    norm_per = norm_master.shape[0]
    own_norm_grads = lax.dynamic_slice_in_dim(
        norm_grads.reshape(-1), lax.axis_index("dp") * norm_per, norm_per
    )
    new_first, new_second, new_master, new_left, new_right, left_next, right_next = soap(
        own_grads,
        masters[0],
        first_moment[0],
        second_moment[0],
        left_stats[0],
        right_stats[0],
        left_basis[0],
        right_basis[0],
    )
    norm_first_new, norm_second_new, norm_new = norm_update(
        own_norm_grads, norm_master, norm_first, norm_second
    )
    return (
        output[None],
        input_grad[None],
        new_first[None],
        new_second[None],
        new_master[None],
        new_left[None],
        new_right[None],
        left_next[None],
        right_next[None],
        norm_first_new,
        norm_second_new,
        norm_new,
    )


def solution(mesh):
    in_specs = (
        P("dp", None, None),
        P("dp", None),
        P("dp", None, None),
        P(),
        P("tensor", "dp", None, None),
        P("tensor", "dp", None, None),
        P("tensor", "dp", None, None),
        P("tensor", "dp", None, None),
        P("tensor", "dp", None, None),
        P("tensor", "dp", None, None),
        P("tensor", "dp", None, None),
        P("dp"),
        P("dp"),
        P("dp"),
    )
    out_specs = (
        P("dp", None, None),
        P("dp", None, None),
        P("tensor", "dp", None, None),
        P("tensor", "dp", None, None),
        P("tensor", "dp", None, None),
        P("tensor", "dp", None, None),
        P("tensor", "dp", None, None),
        P("tensor", "dp", None, None),
        P("tensor", "dp", None, None),
        P("dp"),
        P("dp"),
        P("dp"),
    )
    return jax.shard_map(body, mesh=mesh, in_specs=in_specs, out_specs=out_specs, check_vma=False)
```

```python
import functools
import math

import jax
import jax.numpy as jnp
from jax import lax
from jax.experimental import pallas as pl
from jax.experimental.pallas import tpu as pltpu
from jax.sharding import PartitionSpec as P

HD = 64
STEP = 10
F32 = jnp.float32
BF16 = jnp.bfloat16
LAYER_LIMIT = 48 * 2**20

norm_eps = 1e-05
beta_one = 0.9
beta_two = 0.95
beta_stats = 0.95
learn_rate = 0.03
norm_rate = 0.4
weight_decay = 0.01
adam_eps = 1e-08


def shift_for(length):
    return math.log(length / 8.0)


def block_slots(owner, per_dev):
    count = owner.shape[0]
    index = jnp.arange(count, dtype=jnp.int32)
    earlier = (owner[:, None] == owner[None, :]) & (index[None, :] < index[:, None])
    rank = jnp.sum(earlier.astype(jnp.int32), axis=1)
    slots = owner * per_dev + rank
    inverse = jnp.sum(jnp.where(slots[None, :] == index[:, None], index[None, :], 0), axis=1)
    return (slots, inverse)


def norm_back(plain, inverse_std, grad):
    return inverse_std * (
        grad
        - jnp.mean(grad, axis=-1, keepdims=True)
        - plain * jnp.mean(grad * plain, axis=-1, keepdims=True)
    )


MESH = pl.DeviceIdType.MESH
VM = pl.BlockSpec(memory_space=pltpu.VMEM)
MIB = 2**20


def tiles_up(value):
    return -(-value // 128) * 128


def remote(src, dst, send, recv, where):
    return pltpu.make_async_remote_copy(
        src_ref=src, dst_ref=dst, send_sem=send, recv_sem=recv, device_id=where, device_id_type=MESH
    )


def greet(devices):
    barrier = pltpu.get_barrier_semaphore()
    for device in devices:
        pl.semaphore_signal(barrier, inc=1, device_id=device, device_id_type=MESH)
    pl.semaphore_wait(barrier, len(devices))


def line_greet(dp, t, m):
    place, side = dp // 2, lax.rem(dp, 2)
    barrier = pltpu.get_barrier_semaphore()
    pl.semaphore_signal(barrier, inc=1, device_id=(place * 2 + 1 - side, t), device_id_type=MESH)

    @pl.when(place > 0)
    def _():
        pl.semaphore_signal(barrier, inc=1, device_id=(dp - 2, t), device_id_type=MESH)

    @pl.when(place < m - 1)
    def _():
        pl.semaphore_signal(barrier, inc=1, device_id=(dp + 2, t), device_id_type=MESH)

    ends = (place == 0).astype(jnp.int32) + (place == m - 1).astype(jnp.int32)
    pl.semaphore_wait(barrier, 3 - ends)


def gather_kernel(n, count, block, wide, norm_rows, m_ref, norm_ref, u_ref, nout_ref, held, send_sem, recv_sem):
    m = n // 2
    dp, t = lax.axis_index("dp"), lax.axis_index("tensor")
    place, side = dp // 2, lax.rem(dp, 2)
    pair = (place * 2 + 1 - side, t)
    for k in range(count):
        held[dp, :, k * block : (k + 1) * block] = m_ref[k].astype(BF16)
    if wide > count * block:
        held[dp, :, count * block : wide] = jnp.zeros((block, wide - count * block), BF16)
    held[dp, :, wide : wide + 128] = jnp.concatenate(
        [norm_ref[...], jnp.zeros((block - norm_rows, 128), F32)], axis=0
    ).astype(BF16)
    line_greet(dp, t, m)

    def send(source, way, where):
        return remote(held.at[source], held.at[source], send_sem.at[source, way], recv_sem.at[source], where)

    def unpack(source):
        for k in range(count):
            u_ref[source * count + k] = held[source, :, k * block : (k + 1) * block]
        nout_ref[source] = held[source, :16, wide : wide + 128]

    def spread(source, left, right):
        send(source, 2, pair).start()

        @pl.when(left)
        def _():
            send(source, 0, (dp - 2, t)).start()

        @pl.when(right)
        def _():
            send(source, 1, (dp + 2, t)).start()

    def spread_done(source, left, right):
        send(source, 2, pair).wait_send()

        @pl.when(left)
        def _():
            send(source, 0, (dp - 2, t)).wait_send()

        @pl.when(right)
        def _():
            send(source, 1, (dp + 2, t)).wait_send()

    spread(dp, place > 0, place < m - 1)
    unpack(dp)

    def one(hop, _):
        @pl.when(place - hop >= 0)
        def _():
            source = dp - 2 * hop
            send(source, 2, pair).wait_recv()
            spread(source, False, place < m - 1)

        @pl.when(place + hop < m)
        def _():
            source = dp + 2 * hop
            send(source, 2, pair).wait_recv()
            spread(source, place > 0, False)

        @pl.when(place - hop >= 0)
        def _():
            unpack(dp - 2 * hop)

        @pl.when(place + hop < m)
        def _():
            unpack(dp + 2 * hop)

        return 0

    lax.fori_loop(1, m, one, 0)

    def other(step, _):
        source = step * 2 + 1 - side
        send(source, 2, pair).wait_recv()
        unpack(source)
        return 0

    lax.fori_loop(0, m, other, 0)

    def finish(step, _):
        source = step * 2 + side
        spread_done(
            source,
            (place > 0) & (step >= place),
            (place < m - 1) & (step <= place),
        )
        return 0

    lax.fori_loop(0, m, finish, 0)


def gather_masters(masters, norm, n):
    count, block = masters.shape[0], masters.shape[-1]
    wide = tiles_up(count * block)
    norm_rows = -(-norm.shape[0] // 128)
    norm_tile = jnp.pad(norm, (0, norm_rows * 128 - norm.shape[0])).reshape(norm_rows, 128)
    blocks, norms = pl.pallas_call(
        functools.partial(gather_kernel, n, count, block, wide, norm_rows),
        out_shape=[
            jax.ShapeDtypeStruct((n * count, block, block), BF16),
            jax.ShapeDtypeStruct((n, 16, 128), BF16),
        ],
        in_specs=[VM, VM],
        out_specs=[VM, VM],
        scratch_shapes=[
            pltpu.VMEM((n, block, wide + 128), BF16),
            pltpu.SemaphoreType.DMA((n, 3)),
            pltpu.SemaphoreType.DMA((n,)),
        ],
        compiler_params=pltpu.CompilerParams(collective_id=1, has_side_effects=True, vmem_limit_bytes=10 * MIB),
        name="gather_masters",
    )(masters, norm_tile)
    return blocks, norms.reshape(n, 16 * 128)[:, : norm.shape[0]].reshape(-1)


NN = ((1,), (0,))
NT = ((1,), (1,))
TN = ((0,), (0,))


def lane_prod(n, lanes, left_row, right_tile, put, group=4):
    tiles = n // 8

    def some(step, _):
        base = step * group

        def one(k, acc):
            rights = [right_tile(k, j) for j in range(tiles)]
            out = []
            for r in range(group):
                row = jnp.broadcast_to(left_row(base + r, k), (8, lanes))
                out.append(tuple(acc[r][j] + row * rights[j] for j in range(tiles)))
            return tuple(out)

        zero = tuple(tuple(jnp.zeros((8, lanes), F32) for _ in range(tiles)) for _ in range(group))
        acc = lax.fori_loop(0, n, one, zero, unroll=8)
        for r in range(group):
            for j in range(tiles):
                put(base + r, j, acc[r][j])
        return 0

    lax.fori_loop(0, n // group, some, 0)


def lane_gram(n, lanes, row, tile, put, put_turned):
    tiles = n // 8
    for first in range(tiles):
        columns = range(first, tiles)

        def some(step, _):
            base = first * 8 + step * 4

            def one(k, acc):
                rights = [tile(k, j) for j in columns]
                out = []
                for r in range(4):
                    left = jnp.broadcast_to(row(base + r, k), (8, lanes))
                    out.append(tuple(a + left * right for a, right in zip(acc[r], rights)))
                return tuple(out)

            zero = tuple(tuple(jnp.zeros((8, lanes), F32) for _ in columns) for _ in range(4))
            acc = lax.fori_loop(0, n, one, zero, unroll=8)
            for r in range(4):
                for j in columns:
                    put(base + r, j, acc[r][j - first])
                    if j > first:
                        put_turned(base + r, j, acc[r][j - first])
            return 0

        lax.fori_loop(0, 2, some, 0)


def soap_kernel(
    n,
    count,
    packed_ref,
    m_ref,
    f_ref,
    s_ref,
    l_ref,
    r_ref,
    ql_ref,
    qr_ref,
    nf_out,
    ns_out,
    nm_out,
    nl_out,
    nr_out,
    bl_out,
    br_out,
    nf_ref,
    ns_ref,
    nm_ref,
    nl_ref,
    nr_ref,
    basis_ref,
    u_scr,
    g_ref,
    gt_ref,
    qt_ref,
    h_ref,
    d_ref,
    sems,
):
    tiles = n // 8

    def at(ref):
        def row(i, k):
            return ref[pl.ds(i * n + k, 1), :]

        return row

    def at_turned(ref):
        def row(i, k):
            return ref[pl.ds(k * n + i, 1), :]

        return row

    def tile(ref):
        def one(k, j):
            return ref[pl.ds(pl.multiple_of(k * n + 8 * j, 8), 8), :]

        return one

    def turned(i, j):
        return pl.ds(8 * j * n + i, 8, stride=n)

    def turn_into(dst, src):
        def one(k, _):
            for j in range(tiles):
                dst[here(k, j), :] = src[turned(k, j), :]
            return 0

        lax.fori_loop(0, n, one, 0, unroll=4)

    def here(i, j):
        return pl.ds(pl.multiple_of(i * n + 8 * j, 8), 8)

    def send(place, src, dst):
        return pltpu.make_async_copy(src, dst, sems.at[place])

    for c in range(count):
        u_scr[c] = packed_ref[:, c * n : (c + 1) * n]

    def turn(i, _):
        slab = u_scr[:, pl.ds(i, 1), :].reshape(count, n)
        g_ref[pl.ds(pl.multiple_of(i * n, 8), n), :] = slab.T
        return 0

    lax.fori_loop(0, n, turn, 0, unroll=4)

    turn_into(gt_ref, g_ref)
    turn_into(qt_ref, qr_ref)

    def blend(dst, old):
        def put(i, j, value):
            where = here(i, j)
            dst[where, :] = beta_stats * old[where, :] + (1.0 - beta_stats) * value

        def put_turned(i, j, value):
            where = turned(i, j)
            dst[where, :] = beta_stats * old[where, :] + (1.0 - beta_stats) * value

        return put, put_turned

    def store(ref, base=0):
        def put(i, j, value):
            ref[pl.ds(pl.multiple_of(base + i * n + 8 * j, 8), 8), :] = value

        return put

    lane_gram(n, count, at_turned(gt_ref), tile(gt_ref), *blend(nl_ref, l_ref))
    send(3, nl_ref, nl_out).start()
    lane_gram(n, count, at_turned(g_ref), tile(g_ref), *blend(nr_ref, r_ref))
    send(4, nr_ref, nr_out).start()
    lane_prod(n, count, at(nl_ref), tile(ql_ref), store(basis_ref))
    lane_prod(n, count, at(nr_ref), tile(qr_ref), store(basis_ref, n * n))

    sub = lax.broadcasted_iota(jnp.int32, (8, count), 0)
    for panel in range(tiles):
        def side(s, _):
            base = pl.multiple_of(s * n * n, 8)

            def spot(i, j):
                return pl.ds(pl.multiple_of(base + i * n + 8 * j, 8), 8)

            rows = [basis_ref[spot(i, panel), :] for i in range(n)]
            sizes = jnp.ones((8, count), F32)
            for k in range(8):
                heads = [jnp.broadcast_to(row[k : k + 1], (8, count)) for row in rows]
                terms = [head * row for head, row in zip(heads, rows)]
                while len(terms) > 1:
                    terms = [sum(terms[p : p + 2][1:], terms[p]) for p in range(0, len(terms), 2)]
                size = jnp.broadcast_to(terms[0][k : k + 1], (8, count))
                sizes = jnp.where(sub == k, size, sizes)
                factor = jnp.where(sub > k, terms[0] * (1.0 / size), 0.0)
                rows = [row - head * factor for head, row in zip(heads, rows)]
            scale = lax.rsqrt(sizes)
            for i in range(n):
                basis_ref[spot(i, panel), :] = rows[i] * scale
            for start in range(panel + 1, tiles, 3):
                columns = range(start, min(start + 3, tiles))

                def heads_of(i):
                    return [
                        jnp.broadcast_to(basis_ref[pl.ds(base + i * n + 8 * panel + k, 1), :], (8, count))
                        for k in range(8)
                    ]

                def project(i, acc):
                    heads = heads_of(i)
                    values = [basis_ref[spot(i, j), :] for j in columns]
                    return tuple(
                        tuple(a + head * value for a, value in zip(acc[k], values))
                        for k, head in enumerate(heads)
                    )

                zero = tuple(tuple(jnp.zeros((8, count), F32) for _ in columns) for _ in range(8))
                parts = lax.fori_loop(0, n, project, zero, unroll=4)

                def take(i, _):
                    heads = heads_of(i)
                    for c, j in enumerate(columns):
                        value = basis_ref[spot(i, j), :]
                        for k in range(8):
                            value = value - heads[k] * parts[k][c]
                        basis_ref[spot(i, j), :] = value
                    return 0

                lax.fori_loop(0, n, take, 0, unroll=4)
            return 0

        lax.fori_loop(0, 2, side, 0)
    left_basis, right_basis = basis_ref.at[: n * n], basis_ref.at[n * n :]
    send(5, left_basis, bl_out).start()
    send(6, right_basis, br_out).start()

    def put_moments(i, j, rot):
        first = beta_one * f_ref[here(i, j), :] + (1.0 - beta_one) * rot
        second = beta_two * s_ref[here(i, j), :] + (1.0 - beta_two) * rot * rot
        nf_ref[here(i, j), :] = first
        ns_ref[here(i, j), :] = second
        d_ref[here(i, j), :] = first / (1.0 - beta_one**STEP) / (
            jnp.sqrt(second / (1.0 - beta_two**STEP)) + adam_eps
        )

    def put_master(i, j, moved):
        master = m_ref[here(i, j), :]
        nm_ref[here(i, j), :] = master - learn_rate * (moved + weight_decay * master)

    lane_prod(n, count, at_turned(ql_ref), tile(g_ref), store(h_ref))
    lane_prod(n, count, at(h_ref), tile(qr_ref), put_moments)
    send(0, nf_ref, nf_out).start()
    send(1, ns_ref, ns_out).start()
    lane_prod(n, count, at(ql_ref), tile(d_ref), store(h_ref))
    lane_prod(n, count, at(h_ref), tile(qt_ref), put_master)
    send(2, nm_ref, nm_out).start()
    sources = (nf_ref, ns_ref, nm_ref, nl_ref, nr_ref, left_basis, right_basis)
    targets = (nf_out, ns_out, nm_out, nl_out, nr_out, bl_out, br_out)
    for place, (src, dst) in enumerate(zip(sources, targets)):
        send(place, src, dst).wait()


def soap(packed, *state):
    count, n = state[0].shape[0], state[0].shape[-1]
    flat = [item.transpose(1, 2, 0).reshape(n * n, count) for item in state]
    shape = jax.ShapeDtypeStruct((n * n, count), F32)
    room = pltpu.VMEM((n * n, count), F32)
    outs = pl.pallas_call(
        functools.partial(soap_kernel, n, count),
        out_shape=[shape] * 7,
        in_specs=[VM] * 8,
        out_specs=[pl.BlockSpec(memory_space=pl.ANY)] * 7,
        scratch_shapes=[room] * 5
        + [pltpu.VMEM((2 * n * n, count), F32), pltpu.VMEM((count, n, n), F32)]
        + [room] * 5
        + [pltpu.SemaphoreType.DMA((7,))],
        compiler_params=pltpu.CompilerParams(vmem_limit_bytes=24 * MIB),
        name="soap",
    )(packed, *flat)
    return [item.reshape(n, n, count).transpose(2, 0, 1) for item in outs]


def assemble_kernel(rows, cols, block, cuts, slot_ref, u_ref, *w_refs):
    def one(row, _):
        for first, last, w_ref in zip(cuts, cuts[1:], w_refs):
            strip = jnp.concatenate([u_ref[slot_ref[row * cols + c]] for c in range(first, last)], axis=1)
            w_ref[pl.ds(pl.multiple_of(row * block, block), block), :] = strip
        return 0

    lax.fori_loop(0, rows, one, 0)


def piece_cuts(rows, cols, parts):
    attn = rows // parts
    hidden = (cols - 4 * attn) // 2
    return (0, 3 * attn, 3 * attn + hidden, 4 * attn + hidden, cols)


def assemble(slots, blocks, rows, parts):
    block = blocks.shape[-1]
    cols = blocks.shape[0] // rows
    cuts = piece_cuts(rows, cols, parts)
    return pl.pallas_call(
        functools.partial(assemble_kernel, rows, cols, block, cuts),
        out_shape=[
            jax.ShapeDtypeStruct((rows * block, (last - first) * block), BF16)
            for first, last in zip(cuts, cuts[1:])
        ],
        in_specs=[pl.BlockSpec(memory_space=pltpu.SMEM), VM],
        out_specs=[VM] * 4,
        compiler_params=pltpu.CompilerParams(vmem_limit_bytes=4 * MIB),
        name="assemble",
    )(slots, blocks)


def disperse_kernel(rows, cols, block, cuts, n, count, wide, inverse_ref, *refs):
    g_refs, p_ref, u_scr = refs[:4], refs[4], refs[5]

    def cut(row, _):
        for first, last, g_ref in zip(cuts, cuts[1:], g_refs):
            strip = g_ref[pl.ds(pl.multiple_of(row * block, block), block), :]
            for c in range(first, last):
                u_scr[row * cols + c] = strip[:, (c - first) * block : (c - first + 1) * block]
        return 0

    lax.fori_loop(0, rows, cut, 0)

    def lay(d, _):
        for k in range(count):
            p_ref[d, :, k * block : (k + 1) * block] = u_scr[inverse_ref[d * count + k]]
        if wide > count * block:
            p_ref[d, :, count * block : wide] = jnp.zeros((block, wide - count * block), BF16)
        return 0

    lax.fori_loop(0, n, lay, 0)


def disperse(inverse, grads, n, block, parts):
    rows = grads[0].shape[0] // block
    cols = sum(grad.shape[1] for grad in grads) // block
    count = rows * cols // n
    wide = tiles_up(count * block)
    return pl.pallas_call(
        functools.partial(
            disperse_kernel, rows, cols, block, piece_cuts(rows, cols, parts), n, count, wide
        ),
        out_shape=jax.ShapeDtypeStruct((n, block, wide), BF16),
        in_specs=[pl.BlockSpec(memory_space=pltpu.SMEM)] + [VM] * 4,
        out_specs=VM,
        scratch_shapes=[pltpu.VMEM((rows * cols, block, block), BF16)],
        compiler_params=pltpu.CompilerParams(vmem_limit_bytes=16 * MIB),
        name="disperse",
    )(inverse, *grads)


BLK = 128


def plain_norm(rows):
    centered = rows - jnp.mean(rows, axis=-1, keepdims=True)
    inverse_std = lax.rsqrt(jnp.mean(centered * centered, axis=-1, keepdims=True) + norm_eps)
    return centered * inverse_std, inverse_std


def dot(left, right, dims):
    return lax.dot_general(left, right, (dims, ((), ())), preferred_element_type=F32)


class Total:
    def __init__(self, dp, t, x, near, mine, far, near_mine, near_far, sems):
        up, core = t // 2, lax.rem(t, 2)
        self.core = core
        self.beside = (dp, up * 2 + 1 - core)
        self.over = (dp, (1 - up) * 2 + core)
        self.x, self.near, self.mine, self.far = x, near, mine, far
        self.near_mine, self.near_far, self.sems = near_mine, near_far, sems
        self.blocks = sems.shape[1]
        self.size = x.shape[0] // self.blocks
        self.half = self.size // 2

    def rows(self, b, core):
        return pl.ds(pl.multiple_of(b * self.size + core * self.half, self.half), self.half)

    def part(self, b):
        return pl.ds(pl.multiple_of(b * self.half, self.half), self.half)

    def copy(self, kind, b):
        here = self.part(b)
        src, dst, where = (
            (self.x.at[self.rows(b, 1 - self.core)], self.near, self.beside),
            (self.mine.at[here], self.far, self.over),
            (self.mine.at[here], self.near_mine, self.beside),
            (self.far.at[here], self.near_far, self.beside),
        )[kind]
        return remote(src, dst.at[here], self.sems.at[2 * kind, b], self.sems.at[2 * kind + 1, b], where)

    def enter(self, b):
        self.copy(0, b).start()

    def add(self, b):
        here = self.part(b)
        self.copy(0, b).wait_recv()
        self.mine[here] = (self.x[self.rows(b, self.core)].astype(F32) + self.near[here].astype(F32)).astype(BF16)

    def cross(self, b):
        self.copy(1, b).start()
        self.copy(2, b).start()

    def relay(self, b):
        self.copy(1, b).wait_recv()
        self.copy(3, b).start()

    def arrived(self, b):
        self.copy(2, b).wait_recv()
        self.copy(3, b).wait_recv()

    def sums(self, b):
        here = self.part(b)
        own = self.mine[here].astype(F32) + self.far[here].astype(F32)
        other = self.near_mine[here].astype(F32) + self.near_far[here].astype(F32)
        low = self.core == 0
        return jnp.concatenate([jnp.where(low, own, other), jnp.where(low, other, own)], axis=0)

    def close(self, b):
        for kind in range(4):
            self.copy(kind, b).wait_send()


def layer_kernel(
    heads,
    shift,
    x_ref,
    seg_row_ref,
    seg_col_ref,
    dy_ref,
    wp_ref,
    w1_ref,
    wo_ref,
    w2_ref,
    norm_ref,
    gp_ref,
    g1_ref,
    go_ref,
    g2_ref,
    out_ref,
    da_ref,
    resid_ref,
    dres_ref,
    ng_ref,
    a_ref,
    wf_ref,
    qkv_ref,
    pen_ref,
    lse_ref,
    o_ref,
    cn_ref,
    s_ref,
    du_ref,
    dhb_ref,
    dproj_ref,
    dkv_ref,
    carry_ref,
    x1_ref,
    near1,
    mine1,
    far1,
    near_mine1,
    near_far1,
    sem1,
    x3_ref,
    near3,
    mine3,
    far3,
    near_mine3,
    near_far3,
    sem3,
    gf_ref,
    gf_near,
    gf_far,
    share_sem,
    collect_sem,
):
    dp, t = lax.axis_index("dp"), lax.axis_index("tensor")
    up, core = t // 2, lax.rem(t, 2)
    beside, over = (dp, up * 2 + 1 - core), (dp, (1 - up) * 2 + core)
    length, width = x_ref.shape
    blocks = length // BLK
    span = min(length // 2 + BLK, length)
    attn = heads * HD
    one = Total(dp, t, x1_ref, near1, mine1, far1, near_mine1, near_far1, sem1)
    three = Total(dp, t, x3_ref, near3, mine3, far3, near_mine3, near_far3, sem3)
    greet([beside, over])

    def give(where, i):
        return remote(wf_ref, wf_ref, share_sem.at[i], share_sem.at[2], where)

    @pl.when(t == 0)
    def _():
        wf_ref[:, :HD] = wp_ref[:, :HD]
        wf_ref[:, HD:] = wp_ref[:, attn : attn + HD]
        give(over, 0).start()
        give(beside, 1).start()

    def rows_of(b):
        return pl.ds(pl.multiple_of(b * BLK, BLK), BLK)

    gain_one, bias_one = norm_ref[0:1, :], norm_ref[1:2, :]
    gain_two, bias_two = norm_ref[2:3, :], norm_ref[3:4, :]
    wide = 2 * BLK

    def wide_rows(i):
        return pl.ds(pl.multiple_of(i * wide, wide), wide)

    def project(i, _):
        rows = wide_rows(i)
        plain, _ = plain_norm(x_ref[rows].astype(F32))
        a = (plain * gain_one + bias_one).astype(BF16)
        a_ref[rows] = a
        projected = dot(a, wp_ref[...], NN)
        for h in range(heads):
            qkv_ref[h, rows] = projected[:, h * HD : (h + 1) * HD].astype(BF16) * 0.125
        for h in range(heads, 3 * heads):
            qkv_ref[h, rows] = projected[:, h * HD : (h + 1) * HD].astype(BF16)
        return 0

    lax.fori_loop(0, length // wide, project, 0)

    @pl.when(t == 2)
    def _():
        give(over, 0).wait_recv()
        give(beside, 1).start()

    @pl.when((t == 1) | (t == 3))
    def _():
        give(beside, 1).wait_recv()

    def project_first(i, _):
        rows = wide_rows(i)
        projected = dot(a_ref[rows], wf_ref[...], NN)
        qkv_ref[3 * heads, rows] = projected[:, :HD].astype(BF16) * 0.125
        qkv_ref[3 * heads + 1, rows] = projected[:, HD:].astype(BF16)
        return 0

    lax.fori_loop(0, length // wide, project_first, 0)

    row_in = lax.broadcasted_iota(jnp.int32, (BLK, 1), 0)
    col_in = lax.broadcasted_iota(jnp.int32, (1, span), 1)
    square_row = lax.broadcasted_iota(jnp.int32, (BLK, BLK), 0)
    square_col = lax.broadcasted_iota(jnp.int32, (BLK, BLK), 1)
    earlier = (square_col < square_row).astype(F32).astype(BF16)
    later = (square_col > square_row).astype(F32).astype(BF16)

    def window(b):
        start = pl.multiple_of(jnp.maximum(b * BLK + BLK - span, 0), BLK)
        return start, pl.ds(start, span)

    def masks(b):
        start, keys = window(b)
        same = seg_col_ref[rows_of(b)] == seg_row_ref[:, keys]
        behind = (row_in + (b * BLK - start)) - col_in
        return same & (behind >= 0), same & (behind > 0)

    def two_part(matrix, values):
        high = values.astype(BF16)
        low = (values - high.astype(F32)).astype(BF16)
        return dot(matrix, high, NN) + dot(matrix, low, NN)

    carry_ref[...] = jnp.zeros_like(carry_ref)

    def attend(b, _):
        rows = rows_of(b)
        _, keys = window(b)
        allowed, strict = masks(b)
        first = dot(qkv_ref[3 * heads, rows], qkv_ref[3 * heads + 1, keys], NT) - shift
        soft = jnp.maximum(first, 0.0) + jnp.log1p(jnp.exp(-jnp.abs(first)))
        picks = jnp.where(strict, soft, 0.0)
        before = carry_ref[0:1, keys]
        penalty = (two_part(earlier, picks) + before).astype(BF16)
        carry_ref[0:1, keys] = before + jnp.sum(picks, axis=0, keepdims=True)
        pen_ref[rows] = penalty
        penalty = penalty.astype(F32)
        mixed = []
        for h in range(heads):
            raw = dot(qkv_ref[h, rows], qkv_ref[heads + h, keys], NT)
            logits = jnp.where(allowed, raw - penalty, -1e30)
            top = jnp.max(logits, axis=-1, keepdims=True)
            weights = jnp.exp(logits - top)
            total = jnp.sum(weights, axis=-1, keepdims=True)
            lse_ref[h, rows] = top + jnp.log(total)
            probs = (weights * (1.0 / total)).astype(BF16)
            mixed.append(dot(probs, qkv_ref[2 * heads + h, keys], NN))
        o = jnp.concatenate(mixed, axis=1).astype(BF16)
        o_ref[rows] = o
        x1_ref[rows] = dot(o, wo_ref[...], NT).astype(BF16)
        one.enter(b)

        @pl.when(b > 0)
        def _():
            one.add(b - 1)
            one.cross(b - 1)

        return 0

    lax.fori_loop(0, blocks, attend, 0)
    one.add(blocks - 1)
    one.cross(blocks - 1)

    def act_back(i, _):
        rows = wide_rows(i)
        dres_ref[rows] = dot(dy_ref[rows], w2_ref[...], NN)
        return 0

    lax.fori_loop(0, length // wide, act_back, 0)

    def mlp(b, _):
        @pl.when(b == 0)
        def _():
            one.relay(0)

        @pl.when(b < blocks - 1)
        def _():
            one.relay(b + 1)

        @pl.when(b == blocks - 2)
        def _():
            for early in (0, 1):
                three.add(early)
                three.cross(early)

        one.arrived(b)
        rows = rows_of(b)
        resid = x_ref[rows].astype(F32) + one.sums(b)
        resid_ref[rows] = resid
        plain, _ = plain_norm(resid)
        cn = (plain * gain_two + bias_two).astype(BF16)
        cn_ref[rows] = cn
        u = dot(cn, w1_ref[...], NN)
        root = math.sqrt(2.0 / math.pi)
        square = u * u
        bent = jnp.tanh(root * u * (1.0 + 0.044715 * square))
        half = 0.5 * (1.0 + bent)
        s_ref[rows] = (u * half).astype(BF16)
        slope = half + 0.5 * u * (1.0 - bent * bent) * (root * (1.0 + 3 * 0.044715 * square))
        du = (dres_ref[rows] * slope).astype(BF16)
        du_ref[rows] = du
        x3_ref[rows] = dot(du, w1_ref[...], NT).astype(BF16)
        three.enter(b)
        return 0

    lax.fori_loop(0, blocks, mlp, 0)

    def cross_back(i, _):
        three.add(blocks - 1 - i)
        three.cross(blocks - 1 - i)
        return 0

    lax.fori_loop(0, blocks - 2, cross_back, 0)
    g2_ref[...] = dot(dy_ref[...], s_ref[...], TN).astype(BF16)
    g1_ref[...] = dot(cn_ref[...], du_ref[...], TN).astype(BF16)

    for early in (0, 1):
        three.relay(early)
    three.relay(blocks - 1)
    ng_ref[...] = jnp.zeros_like(ng_ref)
    carry_ref[...] = jnp.zeros_like(carry_ref)
    dkv_ref[...] = jnp.zeros_like(dkv_ref)

    def back(i, _):
        b = blocks - 1 - i

        @pl.when(b > 2)
        def _():
            three.relay(b - 1)

        three.arrived(b)
        rows = rows_of(b)
        _, keys = window(b)
        plain, inverse_std = plain_norm(resid_ref[rows])
        d_two = three.sums(b)
        ng_ref[0:1, :] += jnp.sum(d_two * plain, axis=0, keepdims=True)
        ng_ref[1:2, :] += jnp.sum(d_two, axis=0, keepdims=True)
        dres = dy_ref[rows].astype(F32) + norm_back(plain, inverse_std, d_two * gain_two)
        dres_ref[rows] = dres
        dhb = dres.astype(BF16)
        dhb_ref[rows] = dhb
        do = dot(dhb, wo_ref[...], NN).astype(BF16)
        allowed, strict = masks(b)
        penalty = pen_ref[rows].astype(F32)
        total = None
        dq = []
        for h in range(heads):
            q, k, v = qkv_ref[h, rows], qkv_ref[heads + h, keys], qkv_ref[2 * heads + h, keys]
            do_h = do[:, h * HD : (h + 1) * HD]
            logits = jnp.where(allowed, dot(q, k, NT) - penalty, -1e30)
            probs = jnp.exp(logits - lse_ref[h, rows])
            dprobs = dot(do_h, v, NT)
            inner = jnp.sum(dprobs * probs, axis=-1, keepdims=True)
            dlogits = probs * (dprobs - inner)
            total = dlogits if total is None else total + dlogits
            draw = dlogits.astype(BF16)
            dq.append(dot(draw, k, NN) * 0.125)
            dkv_ref[h * HD : (h + 1) * HD, keys] += dot(q, draw, TN)
            dkv_ref[attn + h * HD : attn + (h + 1) * HD, keys] += dot(do_h, probs.astype(BF16), TN)
        q, k = qkv_ref[3 * heads, rows], qkv_ref[3 * heads + 1, keys]
        first = dot(q, k, NT) - shift
        picked = 1.0 / (1.0 + jnp.exp(-first))
        after = carry_ref[0:1, keys]
        suffix = two_part(later, total) + after
        carry_ref[0:1, keys] = after + jnp.sum(total, axis=0, keepdims=True)
        draw = jnp.where(strict, -picked * suffix, 0.0).astype(BF16)
        dq.append(dot(draw, k, NN) * 0.125)
        dkv_ref[2 * attn : 2 * attn + HD, keys] += dot(q, draw, TN)
        dproj_ref[rows, :attn] = jnp.concatenate(dq[:heads], axis=1).astype(BF16)
        dproj_ref[rows, 3 * attn : 3 * attn + HD] = dq[heads].astype(BF16)
        return 0

    lax.fori_loop(0, blocks, back, 0)
    turned = dkv_ref[...].T.astype(BF16)
    dproj_ref[:, attn : 3 * attn] = turned[:, : 2 * attn]
    dproj_ref[:, 3 * attn + HD : 3 * attn + 2 * HD] = turned[:, 2 * attn :]

    def collect(src, dst, where, i):
        return remote(src, dst, collect_sem.at[i], collect_sem.at[i + 2], where)

    gf_ref[...] = dot(a_ref[...], dproj_ref[:, 3 * attn :], TN).astype(BF16)

    @pl.when(core == 1)
    def _():
        collect(gf_ref, gf_near, beside, 0).start()

    @pl.when(core == 0)
    def _():
        collect(gf_ref, gf_near, beside, 0).wait_recv()
        gf_ref[...] = (gf_ref[...].astype(F32) + gf_near[...].astype(F32)).astype(BF16)

    @pl.when(t == 2)
    def _():
        collect(gf_ref, gf_far, over, 1).start()

    go_ref[...] = dot(dhb_ref[...], o_ref[...], TN).astype(BF16)
    grad = dot(a_ref[...], dproj_ref[:, : 3 * attn], TN)
    gp_ref[...] = grad.astype(BF16)

    def finish(i, _):
        rows = wide_rows(i)
        out_ref[rows] = dot(s_ref[rows], w2_ref[...], NT).astype(BF16)
        da = dot(dproj_ref[rows, : 3 * attn], wp_ref[...], NT)
        da_ref[rows] = (da + dot(dproj_ref[rows, 3 * attn :], wf_ref[...], NT)).astype(BF16)
        return 0

    lax.fori_loop(0, length // wide, finish, 0)

    @pl.when(t == 0)
    def _():
        collect(gf_ref, gf_far, over, 1).wait_recv()
        extra = gf_ref[...].astype(F32) + gf_far[...].astype(F32)
        gp_ref[:, :HD] = (gp_ref[:, :HD].astype(F32) + extra[:, :HD]).astype(BF16)
        gp_ref[:, attn : attn + HD] = (gp_ref[:, attn : attn + HD].astype(F32) + extra[:, HD:]).astype(BF16)
        give(over, 0).wait_send()

    @pl.when(core == 0)
    def _():
        give(beside, 1).wait_send()

    @pl.when(core == 1)
    def _():
        collect(gf_ref, gf_near, beside, 0).wait_send()

    @pl.when(t == 2)
    def _():
        collect(gf_ref, gf_far, over, 1).wait_send()

    def close(b, _):
        one.close(b)
        three.close(b)
        return 0

    lax.fori_loop(0, blocks, close, 0)


def layer(inputs, segments, cotangent, wp, w1, wo, w2, norms):
    length, width = inputs.shape
    attn, hidden = wo.shape[1], w1.shape[1]
    heads = attn // HD
    blocks = length // BLK
    span = min(length // 2 + BLK, length)

    def low(*shape):
        return pltpu.VMEM(shape, BF16)

    half = length // 2
    total = [low(length, width)] + [low(half, width)] * 5 + [pltpu.SemaphoreType.DMA((8, blocks))]

    def out(shape, dtype):
        return jax.ShapeDtypeStruct(shape, dtype)

    return pl.pallas_call(
        functools.partial(layer_kernel, heads, shift_for(length)),
        out_shape=[
            out(wp.shape, BF16),
            out(w1.shape, BF16),
            out(wo.shape, BF16),
            out(w2.shape, BF16),
            out((length, width), BF16),
            out((length, width), BF16),
            out((length, width), F32),
            out((length, width), F32),
            out((2, width), F32),
        ],
        in_specs=[VM] * 9,
        out_specs=[VM] * 9,
        scratch_shapes=[
            low(length, width),
            low(width, 2 * HD),
            low(3 * heads + 2, length, HD),
            low(length, span),
            pltpu.VMEM((heads, length, 1), F32),
            low(length, attn),
            low(length, width),
            low(length, hidden),
            low(length, hidden),
            low(length, width),
            low(length, 3 * attn + 2 * HD),
            pltpu.VMEM((2 * attn + HD, length), F32),
            pltpu.VMEM((8, length), F32),
        ]
        + total
        + total
        + [low(width, 2 * HD)] * 3
        + [pltpu.SemaphoreType.DMA((3,)), pltpu.SemaphoreType.DMA((4,))],
        compiler_params=pltpu.CompilerParams(
            collective_id=3, has_side_effects=True, vmem_limit_bytes=LAYER_LIMIT
        ),
        name="layer",
    )(
        inputs,
        segments.reshape(1, length),
        segments.reshape(length, 1),
        cotangent,
        wp,
        w1,
        wo,
        w2,
        norms,
    )


def settle_kernel(
    n,
    p_ref,
    out_in,
    da_in,
    resid_ref,
    dres_ref,
    x_ref,
    norm_ref,
    ng_in,
    g_ref,
    output_ref,
    grad_ref,
    ng_ref,
    xin,
    lin,
    rin,
    x_send,
    x_recv,
    l_send,
    l_recv,
    r_send,
    r_recv,
    near4,
    mine4,
    far4,
    near_mine4,
    near_far4,
    sem4,
    near2,
    mine2,
    far2,
    near_mine2,
    near_far2,
    sem2,
    norm_held,
    norm_send,
    norm_recv,
):
    m = n // 2
    dp, t = lax.axis_index("dp"), lax.axis_index("tensor")
    place, side = dp // 2, lax.rem(dp, 2)
    pair = (place * 2 + 1 - side, t)
    four = Total(dp, t, da_in, near4, mine4, far4, near_mine4, near_far4, sem4)
    two = Total(dp, t, out_in, near2, mine2, far2, near_mine2, near_far2, sem2)
    blocks = four.blocks
    peers = [lax.rem(dp + hop, n) for hop in range(1, n)]
    greet([four.beside, four.over] + [(peer, t) for peer in peers])

    def across(q):
        return remote(p_ref.at[q * 2 + 1 - side], xin.at[q], x_send.at[q], x_recv.at[q], pair)

    def rightward(q):
        return remote(lin.at[q], lin.at[q], r_send.at[q], l_recv.at[q], (dp + 2, t))

    def leftward(q):
        return remote(rin.at[q], rin.at[q], l_send.at[q], r_recv.at[q], (dp - 2, t))

    def both(hop, one):
        @pl.when(place + hop < m)
        def _():
            one(place + hop, True)

        if hop > 0:
            @pl.when(place - hop >= 0)
            def _():
                one(place - hop, False)

    def work(q, right):
        across(q).wait_recv()
        own = p_ref[q * 2 + side].astype(F32) + xin[q].astype(F32)
        if right:
            @pl.when(place > 0)
            def _():
                rightward(q).wait_recv()
                lin[q] = (own + lin[q].astype(F32)).astype(BF16)

            @pl.when(place == 0)
            def _():
                lin[q] = own.astype(BF16)

            rightward(q).start()
        else:
            @pl.when(place < m - 1)
            def _():
                leftward(q).wait_recv()
                rin[q] = (own + rin[q].astype(F32)).astype(BF16)

            @pl.when(place == m - 1)
            def _():
                rin[q] = own.astype(BF16)

            leftward(q).start()

    def keep():
        q = place
        across(q).wait_recv()
        g_ref[...] = p_ref[q * 2 + side].astype(F32) + xin[q].astype(F32)

        @pl.when(place > 0)
        def _():
            rightward(q).wait_recv()
            g_ref[...] += lin[q].astype(F32)

        @pl.when(place < m - 1)
        def _():
            leftward(q).wait_recv()
            g_ref[...] += rin[q].astype(F32)

    def norm_copy(peer):
        return remote(ng_ref, norm_held.at[dp], norm_send.at[peer], norm_recv.at[dp], (peer, t))

    def norm_from(peer):
        return remote(ng_ref, norm_held.at[peer], norm_send.at[peer], norm_recv.at[peer], (peer, t))

    for hop in reversed(range(m)):
        both(hop, lambda q, right: across(q).start())
    for b in range(blocks):
        four.enter(b)
    for b in range(blocks):
        two.enter(b)
    for b in range(blocks):
        four.add(b)
        four.cross(b)
    for b in range(blocks):
        two.add(b)
        two.cross(b)
    ng_ref[...] = jnp.zeros_like(ng_ref)
    gain = norm_ref[0:1, :]

    def rows_of(b):
        return pl.ds(b * four.size, four.size)

    def grad_block(b):
        rows = rows_of(b)
        four.arrived(b)
        d_one = four.sums(b)
        plain, inverse_std = plain_norm(x_ref[rows].astype(F32))
        ng_ref[0:1, :] += jnp.sum(d_one * plain, axis=0, keepdims=True)
        ng_ref[1:2, :] += jnp.sum(d_one, axis=0, keepdims=True)
        grad_ref[rows] = dres_ref[rows] + norm_back(plain, inverse_std, d_one * gain)

    def out_block(b):
        rows = rows_of(b)
        two.arrived(b)
        output_ref[rows] = (resid_ref[rows] + two.sums(b)).astype(BF16)

    def norms_out():
        ng_ref[2:4, :] = ng_in[...]
        for peer in peers:
            norm_copy(peer).start()

    def norms_in():
        for peer in peers:
            norm_from(peer).wait_recv()
        total = None
        for source in range(n):
            term = jnp.where(dp == source, ng_ref[...], norm_held[source])
            total = term if total is None else total + term
        for peer in peers:
            norm_copy(peer).wait_send()
        ng_ref[...] = total

    tasks = []
    for b in range(blocks):
        tasks.append(functools.partial(four.relay, b))
        if b > 0:
            tasks.append(functools.partial(grad_block, b - 1))
    tasks.append(functools.partial(grad_block, blocks - 1))
    tasks.append(norms_out)
    for b in range(blocks):
        tasks.append(functools.partial(two.relay, b))
        if b > 0:
            tasks.append(functools.partial(out_block, b - 1))
    tasks.append(functools.partial(out_block, blocks - 1))
    done = 0
    for step, hop in enumerate(reversed(range(1, m))):
        until = len(tasks) * (step + 1) // m
        while done < until:
            tasks[done]()
            done += 1
        both(hop, work)
    while done < len(tasks):
        tasks[done]()
        done += 1
    keep()
    norms_in()

    def finish(q, _):
        across(q).wait_send()

        @pl.when(q > place)
        def _():
            rightward(q).wait_send()

        @pl.when(q < place)
        def _():
            leftward(q).wait_send()

        return 0

    lax.fori_loop(0, m, finish, 0)
    for b in range(blocks):
        four.close(b)
        two.close(b)


def settle(packed, out_part, da_part, resid, dres, inputs, norms, ng):
    n, block, wide = packed.shape
    m = n // 2
    length, width = inputs.shape
    blocks = 4

    def low(*shape):
        return pltpu.VMEM(shape, BF16)

    half = length // 2
    total = [low(half, width)] * 5 + [pltpu.SemaphoreType.DMA((8, blocks))]
    return pl.pallas_call(
        functools.partial(settle_kernel, n),
        out_shape=[
            jax.ShapeDtypeStruct((block, wide), F32),
            jax.ShapeDtypeStruct((length, width), BF16),
            jax.ShapeDtypeStruct((length, width), F32),
            jax.ShapeDtypeStruct((4, width), F32),
        ],
        in_specs=[VM] * 8,
        out_specs=[VM] * 4,
        scratch_shapes=[low(m, block, wide)] * 3
        + [pltpu.SemaphoreType.DMA((m,))] * 6
        + total
        + total
        + [pltpu.VMEM((n, 4, width), F32), pltpu.SemaphoreType.DMA((n,)), pltpu.SemaphoreType.DMA((n,))],
        compiler_params=pltpu.CompilerParams(
            collective_id=2, has_side_effects=True, vmem_limit_bytes=24 * MIB
        ),
        name="settle",
    )(packed, out_part, da_part, resid, dres, inputs, norms, ng)


def norm_update(grad, master, first, second):
    new_first = beta_one * first + (1.0 - beta_one) * grad
    new_second = beta_two * second + (1.0 - beta_two) * grad * grad
    direction = (
        new_first
        / (1.0 - beta_one**STEP)
        / (jnp.sqrt(new_second / (1.0 - beta_two**STEP)) + adam_eps)
    )
    return (new_first, new_second, master - norm_rate * direction)


def body(
    inputs,
    segments,
    cotangent,
    owner,
    masters,
    first_moment,
    second_moment,
    left_stats,
    right_stats,
    left_basis,
    right_basis,
    norm_master,
    norm_first,
    norm_second,
):
    length = inputs.shape[1]
    width = inputs.shape[2]
    n_dp = lax.axis_size("dp")
    parts = lax.axis_size("tensor")
    per_dev = masters.shape[1]
    block = masters.shape[-1]
    blocks, shared_norms = gather_masters(masters[0], norm_master, n_dp)
    slots, inverse = block_slots(owner, per_dev)
    pieces = assemble(slots, blocks, width // block, parts)
    norms = shared_norms.astype(F32).reshape(4, width)
    *grads, out_part, da_part, resid, dres, norm_grads = layer(
        inputs[0], segments[0], cotangent[0], *pieces, norms
    )
    packed = disperse(inverse, grads, n_dp, block, parts)
    own_packed, output, input_grad, norm_grads = settle(
        packed, out_part, da_part, resid, dres, inputs[0], norms, norm_grads
    )
    norm_per = norm_master.shape[0]
    own_norm_grads = lax.dynamic_slice_in_dim(
        norm_grads.reshape(-1), lax.axis_index("dp") * norm_per, norm_per
    )
    new_first, new_second, new_master, new_left, new_right, left_next, right_next = soap(
        own_packed,
        masters[0],
        first_moment[0],
        second_moment[0],
        left_stats[0],
        right_stats[0],
        left_basis[0],
        right_basis[0],
    )
    norm_first_new, norm_second_new, norm_new = norm_update(
        own_norm_grads, norm_master, norm_first, norm_second
    )
    return (
        output[None],
        input_grad[None],
        new_first[None],
        new_second[None],
        new_master[None],
        new_left[None],
        new_right[None],
        left_next[None],
        right_next[None],
        norm_first_new,
        norm_second_new,
        norm_new,
    )


def solution(mesh):
    in_specs = (
        P("dp", None, None),
        P("dp", None),
        P("dp", None, None),
        P(),
        P("tensor", "dp", None, None),
        P("tensor", "dp", None, None),
        P("tensor", "dp", None, None),
        P("tensor", "dp", None, None),
        P("tensor", "dp", None, None),
        P("tensor", "dp", None, None),
        P("tensor", "dp", None, None),
        P("dp"),
        P("dp"),
        P("dp"),
    )
    out_specs = (
        P("dp", None, None),
        P("dp", None, None),
        P("tensor", "dp", None, None),
        P("tensor", "dp", None, None),
        P("tensor", "dp", None, None),
        P("tensor", "dp", None, None),
        P("tensor", "dp", None, None),
        P("tensor", "dp", None, None),
        P("tensor", "dp", None, None),
        P("dp"),
        P("dp"),
        P("dp"),
    )
    return jax.shard_map(body, mesh=mesh, in_specs=in_specs, out_specs=out_specs, check_vma=False)
```

```python
import functools
import math

import jax
import jax.numpy as jnp
from jax import lax
from jax.experimental import pallas as pl
from jax.experimental.pallas import tpu as pltpu
from jax.sharding import PartitionSpec as P

HD = 64
STEP = 10
F32 = jnp.float32
BF16 = jnp.bfloat16
LAYER_LIMIT = 33 * 2**20

norm_eps = 1e-05
beta_one = 0.9
beta_two = 0.95
beta_stats = 0.95
learn_rate = 0.03
norm_rate = 0.4
weight_decay = 0.01
adam_eps = 1e-08


def shift_for(length):
    return math.log(length / 8.0)


def block_slots(owner, per_dev):
    count = owner.shape[0]
    index = jnp.arange(count, dtype=jnp.int32)
    earlier = (owner[:, None] == owner[None, :]) & (index[None, :] < index[:, None])
    rank = jnp.sum(earlier.astype(jnp.int32), axis=1)
    slots = owner * per_dev + rank
    inverse = jnp.sum(jnp.where(slots[None, :] == index[:, None], index[None, :], 0), axis=1)
    return (slots, inverse)


def norm_back(plain, inverse_std, grad):
    return inverse_std * (
        grad
        - jnp.mean(grad, axis=-1, keepdims=True)
        - plain * jnp.mean(grad * plain, axis=-1, keepdims=True)
    )


MESH = pl.DeviceIdType.MESH
VM = pl.BlockSpec(memory_space=pltpu.VMEM)
MIB = 2**20


def tiles_up(value):
    return -(-value // 128) * 128


def remote(src, dst, send, recv, where):
    return pltpu.make_async_remote_copy(
        src_ref=src, dst_ref=dst, send_sem=send, recv_sem=recv, device_id=where, device_id_type=MESH
    )


def greet(devices):
    barrier = pltpu.get_barrier_semaphore()
    for device in devices:
        pl.semaphore_signal(barrier, inc=1, device_id=device, device_id_type=MESH)
    pl.semaphore_wait(barrier, len(devices))


def line_greet(dp, t, m):
    place, side = dp // 2, lax.rem(dp, 2)
    barrier = pltpu.get_barrier_semaphore()
    pl.semaphore_signal(barrier, inc=1, device_id=(place * 2 + 1 - side, t), device_id_type=MESH)

    @pl.when(place > 0)
    def _():
        pl.semaphore_signal(barrier, inc=1, device_id=(dp - 2, t), device_id_type=MESH)

    @pl.when(place < m - 1)
    def _():
        pl.semaphore_signal(barrier, inc=1, device_id=(dp + 2, t), device_id_type=MESH)

    ends = (place == 0).astype(jnp.int32) + (place == m - 1).astype(jnp.int32)
    pl.semaphore_wait(barrier, 3 - ends)


def gather_kernel(n, count, block, wide, norm_rows, m_ref, norm_ref, u_ref, nout_ref, held, send_sem, recv_sem):
    m = n // 2
    dp, t = lax.axis_index("dp"), lax.axis_index("tensor")
    place, side = dp // 2, lax.rem(dp, 2)
    pair = (place * 2 + 1 - side, t)
    for k in range(count):
        held[dp, :, k * block : (k + 1) * block] = m_ref[k].astype(BF16)
    if wide > count * block:
        held[dp, :, count * block : wide] = jnp.zeros((block, wide - count * block), BF16)
    held[dp, :, wide : wide + 128] = jnp.concatenate(
        [norm_ref[...], jnp.zeros((block - norm_rows, 128), F32)], axis=0
    ).astype(BF16)
    line_greet(dp, t, m)

    def send(source, way, where):
        return remote(held.at[source], held.at[source], send_sem.at[source, way], recv_sem.at[source], where)

    def unpack(source):
        for k in range(count):
            u_ref[source * count + k] = held[source, :, k * block : (k + 1) * block]
        nout_ref[source] = held[source, :16, wide : wide + 128]

    def spread(source, left, right):
        send(source, 2, pair).start()

        @pl.when(left)
        def _():
            send(source, 0, (dp - 2, t)).start()

        @pl.when(right)
        def _():
            send(source, 1, (dp + 2, t)).start()

    def spread_done(source, left, right):
        send(source, 2, pair).wait_send()

        @pl.when(left)
        def _():
            send(source, 0, (dp - 2, t)).wait_send()

        @pl.when(right)
        def _():
            send(source, 1, (dp + 2, t)).wait_send()

    spread(dp, place > 0, place < m - 1)
    unpack(dp)

    def one(hop, _):
        @pl.when(place - hop >= 0)
        def _():
            source = dp - 2 * hop
            send(source, 2, pair).wait_recv()
            spread(source, False, place < m - 1)

        @pl.when(place + hop < m)
        def _():
            source = dp + 2 * hop
            send(source, 2, pair).wait_recv()
            spread(source, place > 0, False)

        @pl.when(place - hop >= 0)
        def _():
            unpack(dp - 2 * hop)

        @pl.when(place + hop < m)
        def _():
            unpack(dp + 2 * hop)

        return 0

    lax.fori_loop(1, m, one, 0)

    def other(step, _):
        source = step * 2 + 1 - side
        send(source, 2, pair).wait_recv()
        unpack(source)
        return 0

    lax.fori_loop(0, m, other, 0)

    def finish(step, _):
        source = step * 2 + side
        spread_done(
            source,
            (place > 0) & (step >= place),
            (place < m - 1) & (step <= place),
        )
        return 0

    lax.fori_loop(0, m, finish, 0)


def gather_masters(masters, norm, n):
    count, block = masters.shape[0], masters.shape[-1]
    wide = tiles_up(count * block)
    norm_rows = -(-norm.shape[0] // 128)
    norm_tile = jnp.pad(norm, (0, norm_rows * 128 - norm.shape[0])).reshape(norm_rows, 128)
    blocks, norms = pl.pallas_call(
        functools.partial(gather_kernel, n, count, block, wide, norm_rows),
        out_shape=[
            jax.ShapeDtypeStruct((n * count, block, block), BF16),
            jax.ShapeDtypeStruct((n, 16, 128), BF16),
        ],
        in_specs=[VM, VM],
        out_specs=[VM, VM],
        scratch_shapes=[
            pltpu.VMEM((n, block, wide + 128), BF16),
            pltpu.SemaphoreType.DMA((n, 3)),
            pltpu.SemaphoreType.DMA((n,)),
        ],
        compiler_params=pltpu.CompilerParams(collective_id=1, has_side_effects=True, vmem_limit_bytes=10 * MIB),
        name="gather_masters",
    )(masters, norm_tile)
    return blocks, norms.reshape(n, 16 * 128)[:, : norm.shape[0]].reshape(-1)


NN = ((1,), (0,))
NT = ((1,), (1,))
TN = ((0,), (0,))


def lane_prod(n, lanes, left_row, right_tile, put, group=4):
    tiles = n // 8

    def some(step, _):
        base = step * group

        def one(k, acc):
            rights = [right_tile(k, j) for j in range(tiles)]
            out = []
            for r in range(group):
                row = jnp.broadcast_to(left_row(base + r, k), (8, lanes))
                out.append(tuple(acc[r][j] + row * rights[j] for j in range(tiles)))
            return tuple(out)

        zero = tuple(tuple(jnp.zeros((8, lanes), F32) for _ in range(tiles)) for _ in range(group))
        acc = lax.fori_loop(0, n, one, zero, unroll=8)
        for r in range(group):
            for j in range(tiles):
                put(base + r, j, acc[r][j])
        return 0

    lax.fori_loop(0, n // group, some, 0)


def lane_gram(n, lanes, row, tile, put, put_turned):
    tiles = n // 8
    for first in range(tiles):
        columns = range(first, tiles)

        def some(step, _):
            base = first * 8 + step * 4

            def one(k, acc):
                rights = [tile(k, j) for j in columns]
                out = []
                for r in range(4):
                    left = jnp.broadcast_to(row(base + r, k), (8, lanes))
                    out.append(tuple(a + left * right for a, right in zip(acc[r], rights)))
                return tuple(out)

            zero = tuple(tuple(jnp.zeros((8, lanes), F32) for _ in columns) for _ in range(4))
            acc = lax.fori_loop(0, n, one, zero, unroll=8)
            for r in range(4):
                for j in columns:
                    put(base + r, j, acc[r][j - first])
                    if j > first:
                        put_turned(base + r, j, acc[r][j - first])
            return 0

        lax.fori_loop(0, 2, some, 0)


def soap_kernel(
    n,
    count,
    packed_ref,
    y_ref,
    dx_ref,
    m_ref,
    f_ref,
    s_ref,
    l_ref,
    r_ref,
    ql_ref,
    qr_ref,
    nf_out,
    ns_out,
    nm_out,
    nl_out,
    nr_out,
    bl_out,
    br_out,
    y_out,
    dx_out,
    nf_ref,
    ns_ref,
    nm_ref,
    nl_ref,
    nr_ref,
    basis_ref,
    u_scr,
    g_ref,
    gt_ref,
    qt_ref,
    h_ref,
    d_ref,
    sems,
):
    tiles = n // 8

    def at(ref):
        def row(i, k):
            return ref[pl.ds(i * n + k, 1), :]

        return row

    def at_turned(ref):
        def row(i, k):
            return ref[pl.ds(k * n + i, 1), :]

        return row

    def tile(ref):
        def one(k, j):
            return ref[pl.ds(pl.multiple_of(k * n + 8 * j, 8), 8), :]

        return one

    def turned(i, j):
        return pl.ds(8 * j * n + i, 8, stride=n)

    def turn_into(dst, src):
        def one(k, _):
            for j in range(tiles):
                dst[here(k, j), :] = src[turned(k, j), :]
            return 0

        lax.fori_loop(0, n, one, 0, unroll=4)

    def here(i, j):
        return pl.ds(pl.multiple_of(i * n + 8 * j, 8), 8)

    def send(place, src, dst):
        return pltpu.make_async_copy(src, dst, sems.at[place])

    send(7, y_ref, y_out).start()
    send(8, dx_ref, dx_out).start()
    for c in range(count):
        u_scr[c] = packed_ref[:, c * n : (c + 1) * n]

    def turn(i, _):
        slab = u_scr[:, pl.ds(i, 1), :].reshape(count, n)
        g_ref[pl.ds(pl.multiple_of(i * n, 8), n), :] = slab.T
        return 0

    lax.fori_loop(0, n, turn, 0, unroll=4)

    turn_into(gt_ref, g_ref)
    turn_into(qt_ref, qr_ref)

    def blend(dst, old):
        def put(i, j, value):
            where = here(i, j)
            dst[where, :] = beta_stats * old[where, :] + (1.0 - beta_stats) * value

        def put_turned(i, j, value):
            where = turned(i, j)
            dst[where, :] = beta_stats * old[where, :] + (1.0 - beta_stats) * value

        return put, put_turned

    def store(ref, base=0):
        def put(i, j, value):
            ref[pl.ds(pl.multiple_of(base + i * n + 8 * j, 8), 8), :] = value

        return put

    lane_gram(n, count, at_turned(gt_ref), tile(gt_ref), *blend(nl_ref, l_ref))
    send(3, nl_ref, nl_out).start()
    lane_gram(n, count, at_turned(g_ref), tile(g_ref), *blend(nr_ref, r_ref))
    send(4, nr_ref, nr_out).start()
    lane_prod(n, count, at(nl_ref), tile(ql_ref), store(basis_ref))
    lane_prod(n, count, at(nr_ref), tile(qr_ref), store(basis_ref, n * n))

    sub = lax.broadcasted_iota(jnp.int32, (8, count), 0)
    for panel in range(tiles):
        def side(s, _):
            base = pl.multiple_of(s * n * n, 8)

            def spot(i, j):
                return pl.ds(pl.multiple_of(base + i * n + 8 * j, 8), 8)

            rows = [basis_ref[spot(i, panel), :] for i in range(n)]
            sizes = jnp.ones((8, count), F32)
            for k in range(8):
                heads = [jnp.broadcast_to(row[k : k + 1], (8, count)) for row in rows]
                terms = [head * row for head, row in zip(heads, rows)]
                while len(terms) > 1:
                    terms = [sum(terms[p : p + 2][1:], terms[p]) for p in range(0, len(terms), 2)]
                size = jnp.broadcast_to(terms[0][k : k + 1], (8, count))
                sizes = jnp.where(sub == k, size, sizes)
                factor = jnp.where(sub > k, terms[0] * (1.0 / size), 0.0)
                rows = [row - head * factor for head, row in zip(heads, rows)]
            scale = lax.rsqrt(sizes)
            for i in range(n):
                basis_ref[spot(i, panel), :] = rows[i] * scale
            for start in range(panel + 1, tiles, 3):
                columns = range(start, min(start + 3, tiles))

                def heads_of(i):
                    return [
                        jnp.broadcast_to(basis_ref[pl.ds(base + i * n + 8 * panel + k, 1), :], (8, count))
                        for k in range(8)
                    ]

                def project(i, acc):
                    heads = heads_of(i)
                    values = [basis_ref[spot(i, j), :] for j in columns]
                    return tuple(
                        tuple(a + head * value for a, value in zip(acc[k], values))
                        for k, head in enumerate(heads)
                    )

                zero = tuple(tuple(jnp.zeros((8, count), F32) for _ in columns) for _ in range(8))
                parts = lax.fori_loop(0, n, project, zero, unroll=4)

                def take(i, _):
                    heads = heads_of(i)
                    for c, j in enumerate(columns):
                        value = basis_ref[spot(i, j), :]
                        for k in range(8):
                            value = value - heads[k] * parts[k][c]
                        basis_ref[spot(i, j), :] = value
                    return 0

                lax.fori_loop(0, n, take, 0, unroll=4)
            return 0

        lax.fori_loop(0, 2, side, 0)
    left_basis, right_basis = basis_ref.at[: n * n], basis_ref.at[n * n :]
    send(5, left_basis, bl_out).start()
    send(6, right_basis, br_out).start()

    def put_moments(i, j, rot):
        first = beta_one * f_ref[here(i, j), :] + (1.0 - beta_one) * rot
        second = beta_two * s_ref[here(i, j), :] + (1.0 - beta_two) * rot * rot
        nf_ref[here(i, j), :] = first
        ns_ref[here(i, j), :] = second
        d_ref[here(i, j), :] = first / (1.0 - beta_one**STEP) / (
            jnp.sqrt(second / (1.0 - beta_two**STEP)) + adam_eps
        )

    def put_master(i, j, moved):
        master = m_ref[here(i, j), :]
        nm_ref[here(i, j), :] = master - learn_rate * (moved + weight_decay * master)

    lane_prod(n, count, at_turned(ql_ref), tile(g_ref), store(h_ref))
    lane_prod(n, count, at(h_ref), tile(qr_ref), put_moments)
    send(0, nf_ref, nf_out).start()
    send(1, ns_ref, ns_out).start()
    lane_prod(n, count, at(ql_ref), tile(d_ref), store(h_ref))
    lane_prod(n, count, at(h_ref), tile(qt_ref), put_master)
    send(2, nm_ref, nm_out).start()
    sources = (nf_ref, ns_ref, nm_ref, nl_ref, nr_ref, left_basis, right_basis, y_ref, dx_ref)
    targets = (nf_out, ns_out, nm_out, nl_out, nr_out, bl_out, br_out, y_out, dx_out)
    for place, (src, dst) in enumerate(zip(sources, targets)):
        send(place, src, dst).wait()


def soap(packed, output, input_grad, *state):
    count, n = state[0].shape[0], state[0].shape[-1]
    flat = [item.transpose(1, 2, 0).reshape(n * n, count) for item in state]
    shape = jax.ShapeDtypeStruct((n * n, count), F32)
    room = pltpu.VMEM((n * n, count), F32)
    outs = pl.pallas_call(
        functools.partial(soap_kernel, n, count),
        out_shape=[shape] * 7 + [jax.ShapeDtypeStruct(item.shape, item.dtype) for item in (output, input_grad)],
        in_specs=[VM] * 10,
        out_specs=[pl.BlockSpec(memory_space=pl.ANY)] * 9,
        scratch_shapes=[room] * 5
        + [pltpu.VMEM((2 * n * n, count), F32), pltpu.VMEM((count, n, n), F32)]
        + [room] * 5
        + [pltpu.SemaphoreType.DMA((9,))],
        compiler_params=pltpu.CompilerParams(vmem_limit_bytes=24 * MIB),
        name="soap",
    )(packed, output, input_grad, *flat)
    return [item.reshape(n, n, count).transpose(2, 0, 1) for item in outs[:7]] + list(outs[7:])


def assemble_kernel(rows, cols, block, cuts, slot_ref, u_ref, *w_refs):
    def one(row, _):
        for first, last, w_ref in zip(cuts, cuts[1:], w_refs):
            strip = jnp.concatenate([u_ref[slot_ref[row * cols + c]] for c in range(first, last)], axis=1)
            w_ref[pl.ds(pl.multiple_of(row * block, block), block), :] = strip
        return 0

    lax.fori_loop(0, rows, one, 0)


def piece_cuts(rows, cols, parts):
    attn = rows // parts
    hidden = (cols - 4 * attn) // 2
    return (0, 3 * attn, 3 * attn + hidden, 4 * attn + hidden, cols)


def assemble(slots, blocks, rows, parts):
    block = blocks.shape[-1]
    cols = blocks.shape[0] // rows
    cuts = piece_cuts(rows, cols, parts)
    return pl.pallas_call(
        functools.partial(assemble_kernel, rows, cols, block, cuts),
        out_shape=[
            jax.ShapeDtypeStruct((rows * block, (last - first) * block), BF16)
            for first, last in zip(cuts, cuts[1:])
        ],
        in_specs=[pl.BlockSpec(memory_space=pltpu.SMEM), VM],
        out_specs=[VM] * 4,
        compiler_params=pltpu.CompilerParams(vmem_limit_bytes=4 * MIB),
        name="assemble",
    )(slots, blocks)


def disperse_kernel(rows, cols, block, cuts, n, count, wide, inverse_ref, *refs):
    g_refs, p_ref, u_scr = refs[:4], refs[4], refs[5]

    def cut(row, _):
        for first, last, g_ref in zip(cuts, cuts[1:], g_refs):
            strip = g_ref[pl.ds(pl.multiple_of(row * block, block), block), :]
            for c in range(first, last):
                u_scr[row * cols + c] = strip[:, (c - first) * block : (c - first + 1) * block]
        return 0

    lax.fori_loop(0, rows, cut, 0)

    some = math.gcd(count, 8)

    def lay(d, _):
        for k in range(0, count, some):
            strip = [u_scr[inverse_ref[d * count + k + e]] for e in range(some)]
            p_ref[d, :, k * block : (k + some) * block] = jnp.concatenate(strip, axis=1)
        if wide > count * block:
            p_ref[d, :, count * block : wide] = jnp.zeros((block, wide - count * block), BF16)
        return 0

    lax.fori_loop(0, n, lay, 0)


def disperse(inverse, grads, n, block, parts):
    rows = grads[0].shape[0] // block
    cols = sum(grad.shape[1] for grad in grads) // block
    count = rows * cols // n
    wide = tiles_up(count * block)
    return pl.pallas_call(
        functools.partial(
            disperse_kernel, rows, cols, block, piece_cuts(rows, cols, parts), n, count, wide
        ),
        out_shape=jax.ShapeDtypeStruct((n, block, wide), BF16),
        in_specs=[pl.BlockSpec(memory_space=pltpu.SMEM)] + [VM] * 4,
        out_specs=VM,
        scratch_shapes=[pltpu.VMEM((rows * cols, block, block), BF16)],
        compiler_params=pltpu.CompilerParams(vmem_limit_bytes=16 * MIB),
        name="disperse",
    )(inverse, *grads)


BLK = 128


def plain_norm(rows):
    centered = rows - jnp.mean(rows, axis=-1, keepdims=True)
    inverse_std = lax.rsqrt(jnp.mean(centered * centered, axis=-1, keepdims=True) + norm_eps)
    return centered * inverse_std, inverse_std


def dot(left, right, dims):
    return lax.dot_general(left, right, (dims, ((), ())), preferred_element_type=F32)


class Total:
    def __init__(self, dp, t, x, near, mine, far, near_mine, near_far, sems):
        up, core = t // 2, lax.rem(t, 2)
        self.up, self.core = up, core
        self.beside = (dp, up * 2 + 1 - core)
        self.over = (dp, (1 - up) * 2 + core)
        self.x, self.near, self.mine, self.far = x, near, mine, far
        self.near_mine, self.near_far, self.sems = near_mine, near_far, sems
        self.blocks = sems.shape[1]
        self.size = x.shape[0] // self.blocks
        self.half = self.size // 2

    def rows(self, b, core):
        return pl.ds(pl.multiple_of(b * self.size + core * self.half, self.half), self.half)

    def part(self, b):
        return pl.ds(pl.multiple_of(b * self.half, self.half), self.half)

    def copy(self, kind, b):
        here = self.part(b)
        src, dst, where = (
            (self.x.at[self.rows(b, 1 - self.core)], self.near, self.beside),
            (self.mine.at[here], self.far, self.over),
            (self.mine.at[here], self.near_mine, self.beside),
            (self.far.at[here], self.near_far, self.beside),
        )[kind]
        return remote(src, dst.at[here], self.sems.at[2 * kind, b], self.sems.at[2 * kind + 1, b], where)

    def enter(self, b):
        self.copy(0, b).start()

    def add(self, b):
        here = self.part(b)
        self.copy(0, b).wait_recv()
        self.mine[here] = (self.x[self.rows(b, self.core)].astype(F32) + self.near[here].astype(F32)).astype(BF16)

    def cross(self, b):
        self.copy(1, b).start()
        self.copy(2, b).start()

    def relay(self, b):
        self.copy(1, b).wait_recv()
        self.copy(3, b).start()

    def arrived(self, b):
        self.copy(2, b).wait_recv()
        self.copy(3, b).wait_recv()

    def sums(self, b):
        here = self.part(b)
        own = self.mine[here].astype(F32) + self.far[here].astype(F32)
        other = self.near_mine[here].astype(F32) + self.near_far[here].astype(F32)
        low = self.core == 0
        return jnp.concatenate([jnp.where(low, own, other), jnp.where(low, other, own)], axis=0)

    def close(self, b):
        for kind in range(4):
            self.copy(kind, b).wait_send()


class Packs:
    def __init__(self, total, own, beside, over, far, sems):
        self.beside, self.over = total.beside, total.over
        self.up, self.core = total.up, total.core
        self.own, self.from_beside, self.from_over, self.from_far, self.sems = own, beside, over, far, sems

    def copy(self, kind, b):
        src, dst, where = (
            (self.own, self.from_beside, self.beside),
            (self.own, self.from_over, self.over),
            (self.from_over, self.from_far, self.beside),
        )[kind]
        return remote(src.at[b], dst.at[b], self.sems.at[2 * kind, b], self.sems.at[2 * kind + 1, b], where)

    def send(self, b):
        self.copy(1, b).start()
        self.copy(0, b).start()

    def relay(self, b):
        self.copy(1, b).wait_recv()
        self.copy(2, b).start()

    def arrived(self, b):
        self.copy(0, b).wait_recv()
        self.copy(2, b).wait_recv()

    def close(self, b):
        for kind in range(3):
            self.copy(kind, b).wait_send()

    def lay(self, b, dst, rows):
        tall = rows.size
        pairs = ((self.up, self.own, self.from_beside), (1 - self.up, self.from_over, self.from_far))
        for up, same, other in pairs:
            for core, ref in ((self.core, same), (1 - self.core, other)):
                dst[rows, pl.ds(pl.multiple_of((up * 2 + core) * 128, 128), 128)] = ref[b, :tall]
            first, second = same[b, tall:], other[b, tall:]
            low = self.core == 0
            zero = jnp.where(low, first.astype(F32), second.astype(F32)).astype(BF16)
            one = jnp.where(low, second.astype(F32), first.astype(F32)).astype(BF16)
            tail = jnp.concatenate(
                [
                    jnp.concatenate([zero[:, :HD], one[:, :HD]], axis=1),
                    jnp.concatenate([zero[:, HD:], one[:, HD:]], axis=1),
                ],
                axis=0,
            )
            dst[rows, pl.ds(pl.multiple_of(512 + up * 128, 128), 128)] = tail

    def pack(self, b, value):
        tall = value.shape[0]
        self.own[b, :tall] = value[:, :128]
        self.own[b, tall:] = jnp.concatenate([value[: tall // 2, 128:], value[tall // 2 :, 128:]], axis=1)


def layer_kernel(
    heads,
    shift,
    x_ref,
    seg_row_ref,
    seg_col_ref,
    dy_ref,
    wp_ref,
    w1_ref,
    wo_ref,
    w2_ref,
    norm_ref,
    gp_ref,
    g1_ref,
    go_ref,
    g2_ref,
    out_ref,
    dproj_ref,
    wf_out,
    resid_ref,
    dres_ref,
    ng_ref,
    a_ref,
    wf_ref,
    qkv_ref,
    pen_ref,
    sig_ref,
    lse_ref,
    o_ref,
    cn_ref,
    s_ref,
    du_ref,
    dhb_ref,
    dkv_ref,
    carry_ref,
    raw_scr,
    back_scr,
    probs_scr,
    draw_scr,
    pick_scr,
    o_own,
    o_beside,
    o_over,
    o_far,
    o_sem,
    o_all,
    wo_own,
    wo_beside,
    wo_over,
    wo_far,
    wo_sem,
    wo_all,
    x3_ref,
    near3,
    mine3,
    far3,
    near_mine3,
    near_far3,
    sem3,
    gf_ref,
    gf_near,
    gf_far,
    share_sem,
    collect_sem,
):
    dp, t = lax.axis_index("dp"), lax.axis_index("tensor")
    up, core = t // 2, lax.rem(t, 2)
    beside, over = (dp, up * 2 + 1 - core), (dp, (1 - up) * 2 + core)
    length, width = x_ref.shape
    blocks = length // BLK
    span = min(length // 2 + BLK, length)
    attn = heads * HD
    three = Total(dp, t, x3_ref, near3, mine3, far3, near_mine3, near_far3, sem3)
    one = Packs(three, o_own, o_beside, o_over, o_far, o_sem)
    outer = Packs(three, wo_own, wo_beside, wo_over, wo_far, wo_sem)
    greet([beside, over])

    def give(where, i):
        return remote(wf_ref, wf_ref, share_sem.at[i], share_sem.at[2], where)

    @pl.when(t == 0)
    def _():
        wf_ref[:, :HD] = wp_ref[:, :HD]
        wf_ref[:, HD:] = wp_ref[:, attn : attn + HD]
        give(over, 0).start()
        give(beside, 1).start()

    outer.pack(0, wo_ref[...])
    outer.send(0)

    def rows_of(b):
        return pl.ds(pl.multiple_of(b * BLK, BLK), BLK)

    gain_one, bias_one = norm_ref[0:1, :], norm_ref[1:2, :]
    gain_two, bias_two = norm_ref[2:3, :], norm_ref[3:4, :]
    wide = 2 * BLK

    def wide_rows(i):
        return pl.ds(pl.multiple_of(i * wide, wide), wide)

    def project(i, _):
        rows = wide_rows(i)
        plain, _ = plain_norm(x_ref[rows].astype(F32))
        a = (plain * gain_one + bias_one).astype(BF16)
        a_ref[rows] = a
        projected = dot(a, wp_ref[...], NN)
        for h in range(heads):
            qkv_ref[h, rows] = projected[:, h * HD : (h + 1) * HD].astype(BF16) * 0.125
        for h in range(heads, 3 * heads):
            qkv_ref[h, rows] = projected[:, h * HD : (h + 1) * HD].astype(BF16)
        return 0

    lax.fori_loop(0, length // wide, project, 0)

    @pl.when(t == 2)
    def _():
        give(over, 0).wait_recv()
        give(beside, 1).start()

    @pl.when((t == 1) | (t == 3))
    def _():
        give(beside, 1).wait_recv()

    def project_first(i, _):
        rows = wide_rows(i)
        projected = dot(a_ref[rows], wf_ref[...], NN)
        qkv_ref[3 * heads, rows] = projected[:, :HD].astype(BF16) * 0.125
        qkv_ref[3 * heads + 1, rows] = projected[:, HD:].astype(BF16)
        return 0

    lax.fori_loop(0, length // wide, project_first, 0)
    wf_out[...] = wf_ref[...]

    square_row = lax.broadcasted_iota(jnp.int32, (BLK, 2 * BLK), 0)
    square_col = lax.rem(lax.broadcasted_iota(jnp.int32, (BLK, 2 * BLK), 1), BLK)
    earlier = (square_col < square_row).astype(F32).astype(BF16)
    later = (square_col > square_row).astype(F32).astype(BF16)
    few = 32

    def every_block(one, backward):
        low = span // BLK - 1

        def early():
            for b in range(low)[:: -1 if backward else 1]:
                one(b, 0, (b + 1) * BLK)

        def rest():
            def step(i, _):
                b = blocks - 1 - i if backward else low + i
                one(b, pl.multiple_of((b - low) * BLK, BLK), span)
                return 0

            lax.fori_loop(0, blocks - low, step, 0)

        for part in (rest, early) if backward else (early, rest):
            part()

    def by_rows(b, one):
        def step(i, _):
            base = pl.multiple_of(i * few, few)
            one(pl.ds(base, few), pl.ds(pl.multiple_of(b * BLK + base, few), few), base)
            return 0

        lax.fori_loop(0, BLK // few, step, 0, unroll=True)

    def two_part(values, part, keys):
        high = values.astype(BF16)
        pick_scr[part, :keys] = high
        pick_scr[pl.ds(pl.multiple_of(part.start + BLK, few), few), :keys] = (
            values - high.astype(F32)
        ).astype(BF16)

    def behind(base, keys):
        row = lax.broadcasted_iota(jnp.int32, (few, keys), 0) + (base + keys - BLK)
        return row - lax.broadcasted_iota(jnp.int32, (few, keys), 1)

    carry_ref[...] = jnp.zeros_like(carry_ref)

    def attend(b, start, keys):
        rows, window = rows_of(b), pl.ds(start, keys)
        raw_scr[heads, :, :keys] = dot(qkv_ref[3 * heads, rows], qkv_ref[3 * heads + 1, window], NT)
        for h in range(heads):
            raw_scr[h, :, :keys] = dot(qkv_ref[h, rows], qkv_ref[heads + h, window], NT)
        seg_row = seg_row_ref[:, window]

        def pick(part, whole, base):
            first = raw_scr[heads, part, :keys] - shift
            small = jnp.exp(-jnp.abs(first))
            soft = jnp.maximum(first, 0.0) + jnp.log(1.0 + small)
            strict = (seg_col_ref[whole] == seg_row) & (behind(base, keys) > 0)
            two_part(jnp.where(strict, soft, 0.0), part, keys)
            share = jnp.where(first >= 0.0, 1.0, small) / (1.0 + small)
            sig_ref[whole, :keys] = jnp.where(strict, share, 0.0).astype(BF16)

        by_rows(b, pick)
        raw_scr[heads, :, :keys] = dot(earlier, pick_scr[:, :keys], NN)
        before = carry_ref[0:1, window]
        last = [pick_scr[end - few : end, :keys].astype(F32)[few - 1 :] for end in (BLK, 2 * BLK)]
        carry_ref[0:1, window] = before + raw_scr[heads, BLK - 1 : BLK, :keys] + (last[0] + last[1])

        def soften(part, whole, base):
            allowed = (seg_col_ref[whole] == seg_row) & (behind(base, keys) >= 0)
            penalty = jnp.where(allowed, raw_scr[heads, part, :keys] + before, 1e30).astype(BF16)
            pen_ref[whole, :keys] = penalty
            penalty = penalty.astype(F32)
            for h in range(heads):
                logits = raw_scr[h, part, :keys] - penalty
                top = jnp.max(logits, axis=-1, keepdims=True)
                weights = jnp.exp(logits - top)
                total = jnp.sum(weights, axis=-1, keepdims=True)
                lse_ref[whole, h : h + 1] = top + jnp.log(total)
                probs_scr[h, part, :keys] = (weights * (1.0 / total)).astype(BF16)

        by_rows(b, soften)
        mixed = [dot(probs_scr[h, :, :keys], qkv_ref[2 * heads + h, window], NN) for h in range(heads)]
        o = jnp.concatenate(mixed, axis=1).astype(BF16)
        o_ref[rows] = o
        one.pack(b, o)
        one.send(b)

    def act_back(i, _):
        rows = wide_rows(i)
        dres_ref[rows] = dot(dy_ref[rows], w2_ref[...], NN)
        return 0

    lax.fori_loop(0, length // wide, act_back, 0)
    outer.relay(0)

    def mlp(b):
        one.arrived(b)
        rows = rows_of(b)
        one.lay(b, o_all, pl.ds(0, BLK))
        resid = x_ref[rows].astype(F32) + dot(o_all[...], wo_all[...], NT)
        resid_ref[rows] = resid
        plain, _ = plain_norm(resid)
        cn = (plain * gain_two + bias_two).astype(BF16)
        cn_ref[rows] = cn
        u = dot(cn, w1_ref[...], NN)
        root = math.sqrt(2.0 / math.pi)
        square = u * u
        bent = jnp.tanh(root * u * (1.0 + 0.044715 * square))
        half = 0.5 * (1.0 + bent)
        s_ref[rows] = (u * half).astype(BF16)
        slope = half + 0.5 * u * (1.0 - bent * bent) * (root * (1.0 + 3 * 0.044715 * square))
        du = (dres_ref[rows] * slope).astype(BF16)
        du_ref[rows] = du
        x3_ref[rows] = dot(du, w1_ref[...], NT).astype(BF16)
        three.enter(b)

    lag, turned_from = 3, blocks - 3

    def mlp_and_send(b):
        mlp(b)

        def before():
            three.add(b - 1)
            three.cross(b - 1)

        if isinstance(b, int):
            if 0 < b <= turned_from:
                before()
        else:
            pl.when((b > 0) & (b <= turned_from))(before)

    def forward(b, start, keys):
        attend(b, start, keys)
        if isinstance(b, int):
            if b == lag - 1:
                outer.arrived(0)
                outer.lay(0, wo_all, pl.ds(0, width))
            if b >= lag - 1:
                one.relay(b - lag + 1)
            if b >= lag:
                mlp_and_send(b - lag)
        else:
            one.relay(b - lag + 1)
            mlp_and_send(b - lag)

    every_block(forward, False)

    def forward_last(i, _):
        b = blocks - lag + i

        @pl.when(i < lag - 1)
        def _():
            one.relay(b + 1)

        mlp_and_send(b)
        return 0

    lax.fori_loop(0, lag, forward_last, 0)
    for b in reversed(range(turned_from, blocks)):
        three.add(b)
        three.cross(b)
    g2_ref[...] = dot(dy_ref[...], s_ref[...], TN).astype(BF16)
    g1_ref[...] = dot(cn_ref[...], du_ref[...], TN).astype(BF16)

    def mlp_out(i, _):
        rows = wide_rows(i)
        out_ref[rows] = dot(s_ref[rows], w2_ref[...], NT).astype(BF16)
        return 0

    lax.fori_loop(0, length // wide, mlp_out, 0)

    for early in range(turned_from):
        three.relay(early)
    three.relay(blocks - 1)
    ng_ref[...] = jnp.zeros_like(ng_ref)
    carry_ref[...] = jnp.zeros_like(carry_ref)
    dkv_ref[...] = jnp.zeros_like(dkv_ref)

    def back(b, start, keys):
        def ahead():
            three.relay(b - 1)

        if not isinstance(b, int):
            pl.when(b > turned_from)(ahead)
        elif b > turned_from:
            ahead()
        three.arrived(b)
        rows, window = rows_of(b), pl.ds(start, keys)
        plain, inverse_std = plain_norm(resid_ref[rows])
        d_two = three.sums(b)
        ng_ref[0:1, :] += jnp.sum(d_two * plain, axis=0, keepdims=True)
        ng_ref[1:2, :] += jnp.sum(d_two, axis=0, keepdims=True)
        dres = dy_ref[rows].astype(F32) + norm_back(plain, inverse_std, d_two * gain_two)
        dres_ref[rows] = dres
        dhb = dres.astype(BF16)
        dhb_ref[rows] = dhb
        do = dot(dhb, wo_ref[...], NN).astype(BF16)
        do = [do[:, h * HD : (h + 1) * HD] for h in range(heads)]
        for h in range(heads):
            raw_scr[h, :, :keys] = dot(qkv_ref[h, rows], qkv_ref[heads + h, window], NT)
            back_scr[h, :, :keys] = dot(do[h], qkv_ref[2 * heads + h, window], NT)

        def harden(part, whole, base):
            penalty = pen_ref[whole, :keys].astype(F32)
            total = None
            for h in range(heads):
                probs = jnp.exp(raw_scr[h, part, :keys] - penalty - lse_ref[whole, h : h + 1])
                dprobs = back_scr[h, part, :keys]
                inner = jnp.sum(dprobs * probs, axis=-1, keepdims=True)
                dlogits = probs * (dprobs - inner)
                probs_scr[h, part, :keys] = probs.astype(BF16)
                draw_scr[h, part, :keys] = dlogits.astype(BF16)
                total = dlogits if total is None else total + dlogits
            two_part(total, part, keys)

        by_rows(b, harden)
        raw_scr[heads, :, :keys] = dot(later, pick_scr[:, :keys], NN)
        after = carry_ref[0:1, window]
        top = [pick_scr[start_ : start_ + few, :keys].astype(F32)[:1] for start_ in (0, BLK)]
        carry_ref[0:1, window] = after + raw_scr[heads, 0:1, :keys] + (top[0] + top[1])

        def select(part, whole, base):
            suffix = raw_scr[heads, part, :keys] + after
            draw_scr[heads, part, :keys] = (sig_ref[whole, :keys].astype(F32) * -suffix).astype(BF16)

        by_rows(b, select)
        dq = []
        for h in range(heads):
            draw = draw_scr[h, :, :keys]
            dq.append(dot(draw, qkv_ref[heads + h, window], NN) * 0.125)
            dkv_ref[h * HD : (h + 1) * HD, window] += dot(qkv_ref[h, rows], draw, TN)
            dkv_ref[attn + h * HD : attn + (h + 1) * HD, window] += dot(do[h], probs_scr[h, :, :keys], TN)
        draw = draw_scr[heads, :, :keys]
        dq.append(dot(draw, qkv_ref[3 * heads + 1, window], NN) * 0.125)
        dkv_ref[2 * attn : 2 * attn + HD, window] += dot(qkv_ref[3 * heads, rows], draw, TN)
        dproj_ref[rows, :attn] = jnp.concatenate(dq[:heads], axis=1).astype(BF16)
        dproj_ref[rows, 3 * attn : 3 * attn + HD] = dq[heads].astype(BF16)

    every_block(back, True)
    dproj_ref[:, 3 * attn + HD : 3 * attn + 2 * HD] = dkv_ref[2 * attn :].T.astype(BF16)

    def collect(src, dst, where, i):
        return remote(src, dst, collect_sem.at[i], collect_sem.at[i + 2], where)

    gf_ref[...] = dot(a_ref[...], dproj_ref[:, 3 * attn :], TN).astype(BF16)

    @pl.when(core == 1)
    def _():
        collect(gf_ref, gf_near, beside, 0).start()

    @pl.when(core == 0)
    def _():
        collect(gf_ref, gf_near, beside, 0).wait_recv()
        gf_ref[...] = (gf_ref[...].astype(F32) + gf_near[...].astype(F32)).astype(BF16)

    @pl.when(t == 2)
    def _():
        collect(gf_ref, gf_far, over, 1).start()

    dproj_ref[:, attn : 3 * attn] = dkv_ref[: 2 * attn].T.astype(BF16)
    go_ref[...] = dot(dhb_ref[...], o_ref[...], TN).astype(BF16)
    grad = dot(a_ref[...], dproj_ref[:, : 3 * attn], TN)
    gp_ref[...] = grad.astype(BF16)

    @pl.when(t == 0)
    def _():
        collect(gf_ref, gf_far, over, 1).wait_recv()
        extra = gf_ref[...].astype(F32) + gf_far[...].astype(F32)
        gp_ref[:, :HD] = (gp_ref[:, :HD].astype(F32) + extra[:, :HD]).astype(BF16)
        gp_ref[:, attn : attn + HD] = (gp_ref[:, attn : attn + HD].astype(F32) + extra[:, HD:]).astype(BF16)
        give(over, 0).wait_send()

    @pl.when(core == 0)
    def _():
        give(beside, 1).wait_send()

    @pl.when(core == 1)
    def _():
        collect(gf_ref, gf_near, beside, 0).wait_send()

    @pl.when(t == 2)
    def _():
        collect(gf_ref, gf_far, over, 1).wait_send()

    def close(b, _):
        one.close(b)
        three.close(b)
        return 0

    lax.fori_loop(0, blocks, close, 0)
    outer.close(0)


def layer(inputs, segments, cotangent, wp, w1, wo, w2, norms):
    length, width = inputs.shape
    attn, hidden = wo.shape[1], w1.shape[1]
    heads = attn // HD
    blocks = length // BLK
    span = min(length // 2 + BLK, length)

    def low(*shape):
        return pltpu.VMEM(shape, BF16)

    half = length // 2
    total = [low(length, width)] + [low(half, width)] * 5 + [pltpu.SemaphoreType.DMA((8, blocks))]

    def out(shape, dtype):
        return jax.ShapeDtypeStruct(shape, dtype)

    return pl.pallas_call(
        functools.partial(layer_kernel, heads, shift_for(length)),
        out_shape=[
            out(wp.shape, BF16),
            out(w1.shape, BF16),
            out(wo.shape, BF16),
            out(w2.shape, BF16),
            out((length, width), BF16),
            out((length, 3 * attn + 2 * HD), BF16),
            out((width, 2 * HD), BF16),
            out((length, width), F32),
            out((length, width), F32),
            out((2, width), F32),
        ],
        in_specs=[VM] * 9,
        out_specs=[VM] * 10,
        scratch_shapes=[
            low(length, width),
            low(width, 2 * HD),
            low(3 * heads + 2, length, HD),
            low(length, span),
            low(length, span),
            pltpu.VMEM((length, 8), F32),
            low(length, attn),
            low(length, width),
            low(length, hidden),
            low(length, hidden),
            low(length, width),
            pltpu.VMEM((2 * attn + HD, length), F32),
            pltpu.VMEM((8, length), F32),
            pltpu.VMEM((heads + 1, BLK, span), F32),
            pltpu.VMEM((heads, BLK, span), F32),
            low(heads, BLK, span),
            low(heads + 1, BLK, span),
            low(2 * BLK, span),
        ]
        + [low(blocks, attn, BLK)] * 4
        + [pltpu.SemaphoreType.DMA((6, blocks)), low(BLK, width)]
        + [low(1, width + width // 2, BLK)] * 4
        + [pltpu.SemaphoreType.DMA((6, 1)), low(width, width)]
        + total
        + [low(width, 2 * HD)] * 3
        + [pltpu.SemaphoreType.DMA((3,)), pltpu.SemaphoreType.DMA((4,))],
        compiler_params=pltpu.CompilerParams(
            collective_id=3, has_side_effects=True, vmem_limit_bytes=LAYER_LIMIT
        ),
        name="layer",
    )(
        inputs,
        segments.reshape(1, length),
        segments.reshape(length, 1),
        cotangent,
        wp,
        w1,
        wo,
        w2,
        norms,
    )


def settle_kernel(
    n,
    p_ref,
    out_in,
    dproj_ref,
    wp_ref,
    wf_ref,
    resid_ref,
    dres_ref,
    x_ref,
    norm_ref,
    ng_in,
    g_ref,
    output_ref,
    grad_ref,
    ng_ref,
    xin,
    lin,
    rin,
    x_send,
    x_recv,
    l_send,
    l_recv,
    r_send,
    r_recv,
    near4,
    mine4,
    far4,
    near_mine4,
    near_far4,
    sem4,
    near2,
    mine2,
    far2,
    near_mine2,
    near_far2,
    sem2,
    norm_held,
    norm_send,
    norm_recv,
    da_scr,
):
    m = n // 2
    dp, t = lax.axis_index("dp"), lax.axis_index("tensor")
    place, side = dp // 2, lax.rem(dp, 2)
    pair = (place * 2 + 1 - side, t)
    four = Total(dp, t, da_scr, near4, mine4, far4, near_mine4, near_far4, sem4)
    two = Total(dp, t, out_in, near2, mine2, far2, near_mine2, near_far2, sem2)
    blocks = four.blocks
    peers = [lax.rem(dp + hop, n) for hop in range(1, n)]
    greet([four.beside, four.over] + [(peer, t) for peer in peers])

    def across(q):
        return remote(p_ref.at[q * 2 + 1 - side], xin.at[q], x_send.at[q], x_recv.at[q], pair)

    def rightward(q):
        return remote(lin.at[q], lin.at[q], r_send.at[q], l_recv.at[q], (dp + 2, t))

    def leftward(q):
        return remote(rin.at[q], rin.at[q], l_send.at[q], r_recv.at[q], (dp - 2, t))

    def both(hop, one):
        @pl.when(place + hop < m)
        def _():
            one(place + hop, True)

        if hop > 0:
            @pl.when(place - hop >= 0)
            def _():
                one(place - hop, False)

    def work(q, right):
        across(q).wait_recv()
        own = p_ref[q * 2 + side].astype(F32) + xin[q].astype(F32)
        if right:
            @pl.when(place > 0)
            def _():
                rightward(q).wait_recv()
                lin[q] = (own + lin[q].astype(F32)).astype(BF16)

            @pl.when(place == 0)
            def _():
                lin[q] = own.astype(BF16)

            rightward(q).start()
        else:
            @pl.when(place < m - 1)
            def _():
                leftward(q).wait_recv()
                rin[q] = (own + rin[q].astype(F32)).astype(BF16)

            @pl.when(place == m - 1)
            def _():
                rin[q] = own.astype(BF16)

            leftward(q).start()

    def keep():
        q = place
        across(q).wait_recv()
        g_ref[...] = p_ref[q * 2 + side].astype(F32) + xin[q].astype(F32)

        @pl.when(place > 0)
        def _():
            rightward(q).wait_recv()
            g_ref[...] += lin[q].astype(F32)

        @pl.when(place < m - 1)
        def _():
            leftward(q).wait_recv()
            g_ref[...] += rin[q].astype(F32)

    def norm_copy(peer):
        return remote(ng_ref, norm_held.at[dp], norm_send.at[peer], norm_recv.at[dp], (peer, t))

    def norm_from(peer):
        return remote(ng_ref, norm_held.at[peer], norm_send.at[peer], norm_recv.at[peer], (peer, t))

    for hop in reversed(range(m)):
        both(hop, lambda q, right: across(q).start())
    cut = wp_ref.shape[1]
    for b in range(blocks):
        rows = pl.ds(b * four.size, four.size)
        da = dot(dproj_ref[rows, :cut], wp_ref[...], NT)
        da_scr[rows] = (da + dot(dproj_ref[rows, cut:], wf_ref[...], NT)).astype(BF16)
        four.enter(b)
    for b in range(blocks):
        two.enter(b)
    for b in range(blocks):
        four.add(b)
        four.cross(b)
    for b in range(blocks):
        two.add(b)
        two.cross(b)
    ng_ref[...] = jnp.zeros_like(ng_ref)
    gain = norm_ref[0:1, :]

    def rows_of(b):
        return pl.ds(b * four.size, four.size)

    def grad_block(b):
        rows = rows_of(b)
        four.arrived(b)
        d_one = four.sums(b)
        plain, inverse_std = plain_norm(x_ref[rows].astype(F32))
        ng_ref[0:1, :] += jnp.sum(d_one * plain, axis=0, keepdims=True)
        ng_ref[1:2, :] += jnp.sum(d_one, axis=0, keepdims=True)
        grad_ref[rows] = dres_ref[rows] + norm_back(plain, inverse_std, d_one * gain)

    def out_block(b):
        rows = rows_of(b)
        two.arrived(b)
        output_ref[rows] = (resid_ref[rows] + two.sums(b)).astype(BF16)

    def norms_out():
        ng_ref[2:4, :] = ng_in[...]
        for peer in peers:
            norm_copy(peer).start()

    def norms_in():
        for peer in peers:
            norm_from(peer).wait_recv()
        total = None
        for source in range(n):
            term = jnp.where(dp == source, ng_ref[...], norm_held[source])
            total = term if total is None else total + term
        for peer in peers:
            norm_copy(peer).wait_send()
        ng_ref[...] = total

    tasks = []
    for b in range(blocks):
        tasks.append(functools.partial(four.relay, b))
        if b > 0:
            tasks.append(functools.partial(grad_block, b - 1))
    tasks.append(functools.partial(grad_block, blocks - 1))
    tasks.append(norms_out)
    for b in range(blocks):
        tasks.append(functools.partial(two.relay, b))
        if b > 0:
            tasks.append(functools.partial(out_block, b - 1))
    tasks.append(functools.partial(out_block, blocks - 1))
    done = 0
    for step, hop in enumerate(reversed(range(1, m))):
        until = len(tasks) * (step + 1) // m
        while done < until:
            tasks[done]()
            done += 1
        both(hop, work)
    while done < len(tasks):
        tasks[done]()
        done += 1
    keep()
    norms_in()

    def finish(q, _):
        across(q).wait_send()

        @pl.when(q > place)
        def _():
            rightward(q).wait_send()

        @pl.when(q < place)
        def _():
            leftward(q).wait_send()

        return 0

    lax.fori_loop(0, m, finish, 0)
    for b in range(blocks):
        four.close(b)
        two.close(b)


def settle(packed, out_part, dproj, wp, wf, resid, dres, inputs, norms, ng):
    n, block, wide = packed.shape
    m = n // 2
    length, width = inputs.shape
    blocks = 4

    def low(*shape):
        return pltpu.VMEM(shape, BF16)

    half = length // 2
    total = [low(half, width)] * 5 + [pltpu.SemaphoreType.DMA((8, blocks))]
    return pl.pallas_call(
        functools.partial(settle_kernel, n),
        out_shape=[
            jax.ShapeDtypeStruct((block, wide), F32),
            jax.ShapeDtypeStruct((length, width), BF16),
            jax.ShapeDtypeStruct((length, width), F32),
            jax.ShapeDtypeStruct((4, width), F32),
        ],
        in_specs=[VM] * 10,
        out_specs=[VM] * 4,
        scratch_shapes=[low(m, block, wide)] * 3
        + [pltpu.SemaphoreType.DMA((m,))] * 6
        + total
        + total
        + [pltpu.VMEM((n, 4, width), F32), pltpu.SemaphoreType.DMA((n,)), pltpu.SemaphoreType.DMA((n,))]
        + [low(length, width)],
        compiler_params=pltpu.CompilerParams(
            collective_id=2, has_side_effects=True, vmem_limit_bytes=24 * MIB
        ),
        name="settle",
    )(packed, out_part, dproj, wp, wf, resid, dres, inputs, norms, ng)


def norm_update(grad, master, first, second):
    new_first = beta_one * first + (1.0 - beta_one) * grad
    new_second = beta_two * second + (1.0 - beta_two) * grad * grad
    direction = (
        new_first
        / (1.0 - beta_one**STEP)
        / (jnp.sqrt(new_second / (1.0 - beta_two**STEP)) + adam_eps)
    )
    return (new_first, new_second, master - norm_rate * direction)


def body(
    inputs,
    segments,
    cotangent,
    owner,
    masters,
    first_moment,
    second_moment,
    left_stats,
    right_stats,
    left_basis,
    right_basis,
    norm_master,
    norm_first,
    norm_second,
):
    length = inputs.shape[1]
    width = inputs.shape[2]
    n_dp = lax.axis_size("dp")
    parts = lax.axis_size("tensor")
    per_dev = masters.shape[1]
    block = masters.shape[-1]
    blocks, shared_norms = gather_masters(masters[0], norm_master, n_dp)
    slots, inverse = block_slots(owner, per_dev)
    pieces = assemble(slots, blocks, width // block, parts)
    norms = shared_norms.astype(F32).reshape(4, width)
    *grads, out_part, dproj, w_first, resid, dres, norm_grads = layer(
        inputs[0], segments[0], cotangent[0], *pieces, norms
    )
    packed = disperse(inverse, grads, n_dp, block, parts)
    own_packed, output, input_grad, norm_grads = settle(
        packed, out_part, dproj, pieces[0], w_first, resid, dres, inputs[0], norms, norm_grads
    )
    norm_per = norm_master.shape[0]
    own_norm_grads = lax.dynamic_slice_in_dim(
        norm_grads.reshape(-1), lax.axis_index("dp") * norm_per, norm_per
    )
    *updated, output, input_grad = soap(
        own_packed,
        output,
        input_grad,
        masters[0],
        first_moment[0],
        second_moment[0],
        left_stats[0],
        right_stats[0],
        left_basis[0],
        right_basis[0],
    )
    norm_first_new, norm_second_new, norm_new = norm_update(
        own_norm_grads, norm_master, norm_first, norm_second
    )
    return (
        output[None],
        input_grad[None],
        *[item[None] for item in updated],
        norm_first_new,
        norm_second_new,
        norm_new,
    )


def solution(mesh):
    in_specs = (
        P("dp", None, None),
        P("dp", None),
        P("dp", None, None),
        P(),
        P("tensor", "dp", None, None),
        P("tensor", "dp", None, None),
        P("tensor", "dp", None, None),
        P("tensor", "dp", None, None),
        P("tensor", "dp", None, None),
        P("tensor", "dp", None, None),
        P("tensor", "dp", None, None),
        P("dp"),
        P("dp"),
        P("dp"),
    )
    out_specs = (
        P("dp", None, None),
        P("dp", None, None),
        P("tensor", "dp", None, None),
        P("tensor", "dp", None, None),
        P("tensor", "dp", None, None),
        P("tensor", "dp", None, None),
        P("tensor", "dp", None, None),
        P("tensor", "dp", None, None),
        P("tensor", "dp", None, None),
        P("dp"),
        P("dp"),
        P("dp"),
    )
    return jax.shard_map(body, mesh=mesh, in_specs=in_specs, out_specs=out_specs, check_vma=False)
```

```python
import functools
import math

import jax
import jax.numpy as jnp
from jax import lax
from jax.experimental import pallas as pl
from jax.experimental.pallas import tpu as pltpu
from jax.sharding import PartitionSpec as P

HD = 64
STEP = 10
F32 = jnp.float32
BF16 = jnp.bfloat16
LAYER_LIMIT = 35 * 2**20
GATHER_LIMIT = 35 * 2**20
SETTLE_LIMIT = 31 * 2**20

norm_eps = 1e-05
beta_one = 0.9
beta_two = 0.95
beta_stats = 0.95
learn_rate = 0.03
norm_rate = 0.4
weight_decay = 0.01
adam_eps = 1e-08


def shift_for(length):
    return math.log(length / 8.0)


def block_slots(owner, per_dev):
    count = owner.shape[0]
    index = jnp.arange(count, dtype=jnp.int32)
    earlier = (owner[:, None] == owner[None, :]) & (index[None, :] < index[:, None])
    rank = jnp.sum(earlier.astype(jnp.int32), axis=1)
    slots = owner * per_dev + rank
    inverse = jnp.sum(jnp.where(slots[None, :] == index[:, None], index[None, :], 0), axis=1)
    return (slots, inverse)


def norm_back(plain, inverse_std, grad):
    return inverse_std * (
        grad
        - jnp.mean(grad, axis=-1, keepdims=True)
        - plain * jnp.mean(grad * plain, axis=-1, keepdims=True)
    )


def piece_cuts(rows, cols, parts):
    attn = rows // parts
    hidden = (cols - 4 * attn) // 2
    return (0, 3 * attn, 3 * attn + hidden, 4 * attn + hidden, cols)


MESH = pl.DeviceIdType.MESH
VM = pl.BlockSpec(memory_space=pltpu.VMEM)
MIB = 2**20


def tiles_up(value):
    return -(-value // 128) * 128


def remote(src, dst, send, recv, where):
    return pltpu.make_async_remote_copy(
        src_ref=src, dst_ref=dst, send_sem=send, recv_sem=recv, device_id=where, device_id_type=MESH
    )


def greet(devices):
    barrier = pltpu.get_barrier_semaphore()
    for device in devices:
        pl.semaphore_signal(barrier, inc=1, device_id=device, device_id_type=MESH)
    pl.semaphore_wait(barrier, len(devices))


def line_greet(dp, t, m):
    place, side = dp // 2, lax.rem(dp, 2)
    barrier = pltpu.get_barrier_semaphore()
    pl.semaphore_signal(barrier, inc=1, device_id=(place * 2 + 1 - side, t), device_id_type=MESH)

    @pl.when(place > 0)
    def _():
        pl.semaphore_signal(barrier, inc=1, device_id=(dp - 2, t), device_id_type=MESH)

    @pl.when(place < m - 1)
    def _():
        pl.semaphore_signal(barrier, inc=1, device_id=(dp + 2, t), device_id_type=MESH)

    ends = (place == 0).astype(jnp.int32) + (place == m - 1).astype(jnp.int32)
    pl.semaphore_wait(barrier, 3 - ends)


def gather_kernel(
    n, count, block, wide, norm_rows, norm_per, rows, cuts, slot_ref, m_ref, norm_ref, *refs
):
    w_refs, (nout_ref, u_ref, held, send_sem, recv_sem) = refs[:4], refs[4:]
    m = n // 2
    dp, t = lax.axis_index("dp"), lax.axis_index("tensor")
    place, side = dp // 2, lax.rem(dp, 2)
    pair = (place * 2 + 1 - side, t)
    for k in range(count):
        held[dp, :, k * block : (k + 1) * block] = m_ref[k].astype(BF16)
    if wide > count * block:
        held[dp, :, count * block : wide] = jnp.zeros((block, wide - count * block), BF16)
    held[dp, :, wide : wide + 128] = jnp.concatenate(
        [norm_ref[...], jnp.zeros((block - norm_rows, 128), F32)], axis=0
    ).astype(BF16)
    line_greet(dp, t, m)

    def send(source, way, where):
        return remote(held.at[source], held.at[source], send_sem.at[source, way], recv_sem.at[source], where)

    def unpack(source):
        for k in range(count):
            u_ref[source * count + k] = held[source, :, k * block : (k + 1) * block]

    def spread(source, left, right):
        send(source, 2, pair).start()

        @pl.when(left)
        def _():
            send(source, 0, (dp - 2, t)).start()

        @pl.when(right)
        def _():
            send(source, 1, (dp + 2, t)).start()

    def spread_done(source, left, right):
        send(source, 2, pair).wait_send()

        @pl.when(left)
        def _():
            send(source, 0, (dp - 2, t)).wait_send()

        @pl.when(right)
        def _():
            send(source, 1, (dp + 2, t)).wait_send()

    spread(dp, place > 0, place < m - 1)
    unpack(dp)

    def one(hop, _):
        @pl.when(place - hop >= 0)
        def _():
            source = dp - 2 * hop
            send(source, 2, pair).wait_recv()
            spread(source, False, place < m - 1)

        @pl.when(place + hop < m)
        def _():
            source = dp + 2 * hop
            send(source, 2, pair).wait_recv()
            spread(source, place > 0, False)

        @pl.when(place - hop >= 0)
        def _():
            unpack(dp - 2 * hop)

        @pl.when(place + hop < m)
        def _():
            unpack(dp + 2 * hop)

        return 0

    lax.fori_loop(1, m, one, 0)

    def other(step, _):
        source = step * 2 + 1 - side
        send(source, 2, pair).wait_recv()
        unpack(source)
        return 0

    lax.fori_loop(0, m, other, 0)

    def strip(row, _):
        for first, last, w_ref in zip(cuts, cuts[1:], w_refs):
            w_ref[pl.ds(pl.multiple_of(row * block, block), block), :] = jnp.concatenate(
                [u_ref[slot_ref[row * cuts[-1] + c]] for c in range(first, last)], axis=1
            )
        return 0

    lax.fori_loop(0, rows, strip, 0)

    line = nout_ref.shape[1]
    for source in range(n):
        values = held[source, :16, wide : wide + 128].astype(F32)
        for r in range(norm_rows):
            spot = source * norm_per + r * 128
            size = min(128, norm_per - r * 128)
            nout_ref[spot // line : spot // line + 1, spot % line : spot % line + size] = values[
                r : r + 1, :size
            ]

    def finish(step, _):
        source = step * 2 + side
        spread_done(
            source,
            (place > 0) & (step >= place),
            (place < m - 1) & (step <= place),
        )
        return 0

    lax.fori_loop(0, m, finish, 0)


def gather_masters(slots, masters, norm, n, rows, parts):
    count, block = masters.shape[0], masters.shape[-1]
    wide = tiles_up(count * block)
    norm_rows = -(-norm.shape[0] // 128)
    norm_tile = jnp.pad(norm, (0, norm_rows * 128 - norm.shape[0])).reshape(norm_rows, 128)
    cuts = piece_cuts(rows, n * count // rows, parts)
    *pieces, norms = pl.pallas_call(
        functools.partial(gather_kernel, n, count, block, wide, norm_rows, norm.shape[0], rows, cuts),
        out_shape=[
            jax.ShapeDtypeStruct((rows * block, (last - first) * block), BF16)
            for first, last in zip(cuts, cuts[1:])
        ]
        + [jax.ShapeDtypeStruct((4, n * norm.shape[0] // 4), F32)],
        in_specs=[pl.BlockSpec(memory_space=pltpu.SMEM), VM, VM],
        out_specs=[VM] * 5,
        scratch_shapes=[
            pltpu.VMEM((n * count, block, block), BF16),
            pltpu.VMEM((n, block, wide + 128), BF16),
            pltpu.SemaphoreType.DMA((n, 3)),
            pltpu.SemaphoreType.DMA((n,)),
        ],
        compiler_params=pltpu.CompilerParams(
            collective_id=1, has_side_effects=True, vmem_limit_bytes=GATHER_LIMIT
        ),
        name="gather_masters",
        cost_estimate=pl.CostEstimate(flops=0, bytes_accessed=163200000, transcendentals=0),
    )(slots, masters, norm_tile)
    return pieces, norms


NN = ((1,), (0,))
NT = ((1,), (1,))
TN = ((0,), (0,))


def lane_prod(n, lanes, left_row, right_tile, put, group=4):
    tiles = n // 8

    def some(step, _):
        base = step * group

        def one(k, acc):
            rights = [right_tile(k, j) for j in range(tiles)]
            out = []
            for r in range(group):
                row = jnp.broadcast_to(left_row(base + r, k), (8, lanes))
                out.append(tuple(acc[r][j] + row * rights[j] for j in range(tiles)))
            return tuple(out)

        zero = tuple(tuple(jnp.zeros((8, lanes), F32) for _ in range(tiles)) for _ in range(group))
        acc = lax.fori_loop(0, n, one, zero, unroll=8)
        for r in range(group):
            for j in range(tiles):
                put(base + r, j, acc[r][j])
        return 0

    lax.fori_loop(0, n // group, some, 0)


def lane_gram(n, lanes, row, tile, put, put_turned):
    tiles = n // 8
    for first in range(tiles):
        columns = range(first, tiles)

        def some(step, _):
            base = first * 8 + step * 4

            def one(k, acc):
                rights = [tile(k, j) for j in columns]
                out = []
                for r in range(4):
                    left = jnp.broadcast_to(row(base + r, k), (8, lanes))
                    out.append(tuple(a + left * right for a, right in zip(acc[r], rights)))
                return tuple(out)

            zero = tuple(tuple(jnp.zeros((8, lanes), F32) for _ in columns) for _ in range(4))
            acc = lax.fori_loop(0, n, one, zero, unroll=8)
            for r in range(4):
                for j in columns:
                    put(base + r, j, acc[r][j - first])
                    if j > first:
                        put_turned(base + r, j, acc[r][j - first])
            return 0

        lax.fori_loop(0, 2, some, 0)


def soap_kernel(
    n,
    count,
    packed_ref,
    y_ref,
    dx_ref,
    m_ref,
    f_ref,
    s_ref,
    l_ref,
    r_ref,
    ql_ref,
    qr_ref,
    nf_out,
    ns_out,
    nm_out,
    nl_out,
    nr_out,
    bl_out,
    br_out,
    y_out,
    dx_out,
    nf_ref,
    ns_ref,
    nm_ref,
    nl_ref,
    nr_ref,
    basis_ref,
    u_scr,
    g_ref,
    gt_ref,
    qt_ref,
    h_ref,
    d_ref,
    sems,
):
    tiles = n // 8

    def at(ref):
        def row(i, k):
            return ref[pl.ds(i * n + k, 1), :]

        return row

    def at_turned(ref):
        def row(i, k):
            return ref[pl.ds(k * n + i, 1), :]

        return row

    def tile(ref):
        def one(k, j):
            return ref[pl.ds(pl.multiple_of(k * n + 8 * j, 8), 8), :]

        return one

    def turned(i, j):
        return pl.ds(8 * j * n + i, 8, stride=n)

    def turn_into(dst, src):
        def one(k, _):
            for j in range(tiles):
                dst[here(k, j), :] = src[turned(k, j), :]
            return 0

        lax.fori_loop(0, n, one, 0, unroll=4)

    def here(i, j):
        return pl.ds(pl.multiple_of(i * n + 8 * j, 8), 8)

    def send(place, src, dst):
        return pltpu.make_async_copy(src, dst, sems.at[place])

    send(7, y_ref, y_out).start()
    send(8, dx_ref, dx_out).start()
    for c in range(count):
        u_scr[c] = packed_ref[:, c * n : (c + 1) * n]

    def turn(i, _):
        slab = u_scr[:, pl.ds(i, 1), :].reshape(count, n)
        g_ref[pl.ds(pl.multiple_of(i * n, 8), n), :] = slab.T
        return 0

    lax.fori_loop(0, n, turn, 0, unroll=4)

    turn_into(gt_ref, g_ref)
    turn_into(qt_ref, qr_ref)

    def blend(dst, old):
        def put(i, j, value):
            where = here(i, j)
            dst[where, :] = beta_stats * old[where, :] + (1.0 - beta_stats) * value

        def put_turned(i, j, value):
            where = turned(i, j)
            dst[where, :] = beta_stats * old[where, :] + (1.0 - beta_stats) * value

        return put, put_turned

    def store(ref, base=0):
        def put(i, j, value):
            ref[pl.ds(pl.multiple_of(base + i * n + 8 * j, 8), 8), :] = value

        return put

    lane_gram(n, count, at_turned(gt_ref), tile(gt_ref), *blend(nl_ref, l_ref))
    send(3, nl_ref, nl_out).start()
    lane_gram(n, count, at_turned(g_ref), tile(g_ref), *blend(nr_ref, r_ref))
    send(4, nr_ref, nr_out).start()
    lane_prod(n, count, at(nl_ref), tile(ql_ref), store(basis_ref))
    lane_prod(n, count, at(nr_ref), tile(qr_ref), store(basis_ref, n * n))

    sub = lax.broadcasted_iota(jnp.int32, (8, count), 0)
    for panel in range(tiles):
        def side(s, _):
            base = pl.multiple_of(s * n * n, 8)

            def spot(i, j):
                return pl.ds(pl.multiple_of(base + i * n + 8 * j, 8), 8)

            rows = [basis_ref[spot(i, panel), :] for i in range(n)]
            sizes = jnp.ones((8, count), F32)
            for k in range(8):
                heads = [jnp.broadcast_to(row[k : k + 1], (8, count)) for row in rows]
                terms = [head * row for head, row in zip(heads, rows)]
                while len(terms) > 1:
                    terms = [sum(terms[p : p + 2][1:], terms[p]) for p in range(0, len(terms), 2)]
                size = jnp.broadcast_to(terms[0][k : k + 1], (8, count))
                sizes = jnp.where(sub == k, size, sizes)
                factor = jnp.where(sub > k, terms[0] * (1.0 / size), 0.0)
                rows = [row - head * factor for head, row in zip(heads, rows)]
            scale = lax.rsqrt(sizes)
            for i in range(n):
                basis_ref[spot(i, panel), :] = rows[i] * scale
            for start in range(panel + 1, tiles, 3):
                columns = range(start, min(start + 3, tiles))

                def heads_of(i):
                    return [
                        jnp.broadcast_to(basis_ref[pl.ds(base + i * n + 8 * panel + k, 1), :], (8, count))
                        for k in range(8)
                    ]

                def project(i, acc):
                    heads = heads_of(i)
                    values = [basis_ref[spot(i, j), :] for j in columns]
                    return tuple(
                        tuple(a + head * value for a, value in zip(acc[k], values))
                        for k, head in enumerate(heads)
                    )

                zero = tuple(tuple(jnp.zeros((8, count), F32) for _ in columns) for _ in range(8))
                parts = lax.fori_loop(0, n, project, zero, unroll=4)

                def take(i, _):
                    heads = heads_of(i)
                    for c, j in enumerate(columns):
                        value = basis_ref[spot(i, j), :]
                        for k in range(8):
                            value = value - heads[k] * parts[k][c]
                        basis_ref[spot(i, j), :] = value
                    return 0

                lax.fori_loop(0, n, take, 0, unroll=4)
            return 0

        lax.fori_loop(0, 2, side, 0)
    left_basis, right_basis = basis_ref.at[: n * n], basis_ref.at[n * n :]
    send(5, left_basis, bl_out).start()
    send(6, right_basis, br_out).start()

    def put_moments(i, j, rot):
        first = beta_one * f_ref[here(i, j), :] + (1.0 - beta_one) * rot
        second = beta_two * s_ref[here(i, j), :] + (1.0 - beta_two) * rot * rot
        nf_ref[here(i, j), :] = first
        ns_ref[here(i, j), :] = second
        d_ref[here(i, j), :] = first / (1.0 - beta_one**STEP) / (
            jnp.sqrt(second / (1.0 - beta_two**STEP)) + adam_eps
        )

    def put_master(i, j, moved):
        master = m_ref[here(i, j), :]
        nm_ref[here(i, j), :] = master - learn_rate * (moved + weight_decay * master)

    lane_prod(n, count, at_turned(ql_ref), tile(g_ref), store(h_ref))
    lane_prod(n, count, at(h_ref), tile(qr_ref), put_moments)
    send(0, nf_ref, nf_out).start()
    send(1, ns_ref, ns_out).start()
    lane_prod(n, count, at(ql_ref), tile(d_ref), store(h_ref))
    lane_prod(n, count, at(h_ref), tile(qt_ref), put_master)
    send(2, nm_ref, nm_out).start()
    sources = (nf_ref, ns_ref, nm_ref, nl_ref, nr_ref, left_basis, right_basis, y_ref, dx_ref)
    targets = (nf_out, ns_out, nm_out, nl_out, nr_out, bl_out, br_out, y_out, dx_out)
    for place, (src, dst) in enumerate(zip(sources, targets)):
        send(place, src, dst).wait()


def soap(packed, output, input_grad, *state):
    count, n = state[0].shape[0], state[0].shape[-1]
    flat = [item.transpose(1, 2, 0).reshape(n * n, count) for item in state]
    shape = jax.ShapeDtypeStruct((n * n, count), F32)
    room = pltpu.VMEM((n * n, count), F32)
    outs = pl.pallas_call(
        functools.partial(soap_kernel, n, count),
        out_shape=[shape] * 7 + [jax.ShapeDtypeStruct(item.shape, item.dtype) for item in (output, input_grad)],
        in_specs=[VM] * 10,
        out_specs=[pl.BlockSpec(memory_space=pl.ANY)] * 9,
        scratch_shapes=[room] * 5
        + [pltpu.VMEM((2 * n * n, count), F32), pltpu.VMEM((count, n, n), F32)]
        + [room] * 5
        + [pltpu.SemaphoreType.DMA((9,))],
        compiler_params=pltpu.CompilerParams(vmem_limit_bytes=31 * MIB),
        name="soap",
    )(packed, output, input_grad, *flat)
    return [item.reshape(n, n, count).transpose(2, 0, 1) for item in outs[:7]] + list(outs[7:])


BLK = 128


def plain_norm(rows):
    centered = rows - jnp.mean(rows, axis=-1, keepdims=True)
    inverse_std = lax.rsqrt(jnp.mean(centered * centered, axis=-1, keepdims=True) + norm_eps)
    return centered * inverse_std, inverse_std


def dot(left, right, dims):
    return lax.dot_general(left, right, (dims, ((), ())), preferred_element_type=F32)


class Total:
    def __init__(self, dp, t, x, near, mine, far, near_mine, near_far, sems):
        up, core = t // 2, lax.rem(t, 2)
        self.up, self.core = up, core
        self.beside = (dp, up * 2 + 1 - core)
        self.over = (dp, (1 - up) * 2 + core)
        self.x, self.near, self.mine, self.far = x, near, mine, far
        self.near_mine, self.near_far, self.sems = near_mine, near_far, sems
        self.blocks = sems.shape[1]
        self.size = x.shape[0] // self.blocks
        self.half = self.size // 2

    def rows(self, b, core):
        return pl.ds(pl.multiple_of(b * self.size + core * self.half, self.half), self.half)

    def part(self, b):
        return pl.ds(pl.multiple_of(b * self.half, self.half), self.half)

    def copy(self, kind, b):
        here = self.part(b)
        src, dst, where = (
            (self.x.at[self.rows(b, 1 - self.core)], self.near, self.beside),
            (self.mine.at[here], self.far, self.over),
            (self.mine.at[here], self.near_mine, self.beside),
            (self.far.at[here], self.near_far, self.beside),
        )[kind]
        return remote(src, dst.at[here], self.sems.at[2 * kind, b], self.sems.at[2 * kind + 1, b], where)

    def enter(self, b):
        self.copy(0, b).start()

    def add(self, b):
        here = self.part(b)
        self.copy(0, b).wait_recv()
        self.mine[here] = (self.x[self.rows(b, self.core)].astype(F32) + self.near[here].astype(F32)).astype(BF16)

    def cross(self, b):
        self.copy(1, b).start()
        self.copy(2, b).start()

    def relay(self, b):
        self.copy(1, b).wait_recv()
        self.copy(3, b).start()

    def arrived(self, b):
        self.copy(2, b).wait_recv()
        self.copy(3, b).wait_recv()

    def sums(self, b):
        here = self.part(b)
        own = self.mine[here].astype(F32) + self.far[here].astype(F32)
        other = self.near_mine[here].astype(F32) + self.near_far[here].astype(F32)
        low = self.core == 0
        return jnp.concatenate([jnp.where(low, own, other), jnp.where(low, other, own)], axis=0)

    def close(self, b):
        for kind in range(4):
            self.copy(kind, b).wait_send()


class Packs:
    def __init__(self, total, own, beside, over, far, sems):
        self.beside, self.over = total.beside, total.over
        self.up, self.core = total.up, total.core
        self.own, self.from_beside, self.from_over, self.from_far, self.sems = own, beside, over, far, sems

    def copy(self, kind, b):
        src, dst, where = (
            (self.own, self.from_beside, self.beside),
            (self.own, self.from_over, self.over),
            (self.from_over, self.from_far, self.beside),
        )[kind]
        return remote(src.at[b], dst.at[b], self.sems.at[2 * kind, b], self.sems.at[2 * kind + 1, b], where)

    def send(self, b):
        self.copy(1, b).start()
        self.copy(0, b).start()

    def relay(self, b):
        self.copy(1, b).wait_recv()
        self.copy(2, b).start()

    def arrived(self, b):
        self.copy(0, b).wait_recv()
        self.copy(2, b).wait_recv()

    def close(self, b):
        for kind in range(3):
            self.copy(kind, b).wait_send()

    def lay(self, b, dst, rows):
        tall = rows.size
        pairs = ((self.up, self.own, self.from_beside), (1 - self.up, self.from_over, self.from_far))
        for up, same, other in pairs:
            for core, ref in ((self.core, same), (1 - self.core, other)):
                dst[rows, pl.ds(pl.multiple_of((up * 2 + core) * 128, 128), 128)] = ref[b, :tall]
            first, second = same[b, tall:], other[b, tall:]
            low = self.core == 0
            zero = jnp.where(low, first.astype(F32), second.astype(F32)).astype(BF16)
            one = jnp.where(low, second.astype(F32), first.astype(F32)).astype(BF16)
            tail = jnp.concatenate(
                [
                    jnp.concatenate([zero[:, :HD], one[:, :HD]], axis=1),
                    jnp.concatenate([zero[:, HD:], one[:, HD:]], axis=1),
                ],
                axis=0,
            )
            dst[rows, pl.ds(pl.multiple_of(512 + up * 128, 128), 128)] = tail

    def pack(self, b, value):
        tall = value.shape[0]
        self.own[b, :tall] = value[:, :128]
        self.own[b, tall:] = jnp.concatenate([value[: tall // 2, 128:], value[tall // 2 :, 128:]], axis=1)


def layer_kernel(
    heads,
    shift,
    cuts,
    x_ref,
    seg_in,
    dy_ref,
    wp_ref,
    w1_ref,
    wo_ref,
    w2_ref,
    norm_ref,
    mat_ref,
    out_ref,
    dproj_ref,
    wf_out,
    dhb_ref,
    resid_ref,
    ng_ref,
    a_ref,
    wf_ref,
    qkv_ref,
    pen_ref,
    sig_ref,
    lse_ref,
    o_ref,
    cn_ref,
    s_ref,
    du_ref,
    dkv_ref,
    carry_ref,
    raw_scr,
    back_scr,
    probs_scr,
    draw_scr,
    pick_scr,
    o_own,
    o_beside,
    o_over,
    o_far,
    o_sem,
    o_all,
    wo_own,
    wo_beside,
    wo_over,
    wo_far,
    wo_sem,
    wo_all,
    x3_ref,
    near3,
    mine3,
    far3,
    near_mine3,
    near_far3,
    sem3,
    gf_ref,
    gf_near,
    gf_far,
    share_sem,
    collect_sem,
    seg_row_ref,
    seg_col_ref,
):
    dp, t = lax.axis_index("dp"), lax.axis_index("tensor")
    up, core = t // 2, lax.rem(t, 2)
    beside, over = (dp, up * 2 + 1 - core), (dp, (1 - up) * 2 + core)
    length, width = x_ref.shape
    blocks = length // BLK
    span = min(length // 2 + BLK, length)
    attn = heads * HD
    three = Total(dp, t, x3_ref, near3, mine3, far3, near_mine3, near_far3, sem3)
    one = Packs(three, o_own, o_beside, o_over, o_far, o_sem)
    outer = Packs(three, wo_own, wo_beside, wo_over, wo_far, wo_sem)
    greet([beside, over])
    seg_row_ref[...] = seg_in[...].astype(F32)
    by_block = jnp.concatenate([seg_row_ref[:, b * BLK : (b + 1) * BLK] for b in range(blocks)], axis=0)
    turned_seg = by_block.T
    for b in range(blocks):
        seg_col_ref[b * BLK : (b + 1) * BLK] = turned_seg[:, b : b + 1]

    def give(where, i):
        return remote(wf_ref, wf_ref, share_sem.at[i], share_sem.at[2], where)

    @pl.when(t == 0)
    def _():
        wf_ref[:, :HD] = wp_ref[:, :HD]
        wf_ref[:, HD:] = wp_ref[:, attn : attn + HD]
        give(over, 0).start()
        give(beside, 1).start()

    outer.pack(0, wo_ref[...])
    outer.send(0)

    def rows_of(b):
        return pl.ds(pl.multiple_of(b * BLK, BLK), BLK)

    gain_one, bias_one = norm_ref[0:1, :], norm_ref[1:2, :]
    gain_two, bias_two = norm_ref[2:3, :], norm_ref[3:4, :]
    wide = 2 * BLK

    def wide_rows(i):
        return pl.ds(pl.multiple_of(i * wide, wide), wide)

    def project(i, _):
        rows = wide_rows(i)
        plain, _ = plain_norm(x_ref[rows].astype(F32))
        a = (plain * gain_one + bias_one).astype(BF16)
        a_ref[rows] = a
        projected = dot(a, wp_ref[...], NN)
        for h in range(heads):
            qkv_ref[h, rows] = projected[:, h * HD : (h + 1) * HD].astype(BF16) * 0.125
        for h in range(heads, 3 * heads):
            qkv_ref[h, rows] = projected[:, h * HD : (h + 1) * HD].astype(BF16)
        return 0

    lax.fori_loop(0, length // wide, project, 0)

    @pl.when(t == 2)
    def _():
        give(over, 0).wait_recv()
        give(beside, 1).start()

    @pl.when((t == 1) | (t == 3))
    def _():
        give(beside, 1).wait_recv()

    def project_first(i, _):
        rows = wide_rows(i)
        projected = dot(a_ref[rows], wf_ref[...], NN)
        qkv_ref[3 * heads, rows] = projected[:, :HD].astype(BF16) * 0.125
        qkv_ref[3 * heads + 1, rows] = projected[:, HD:].astype(BF16)
        return 0

    lax.fori_loop(0, length // wide, project_first, 0)
    wf_out[...] = wf_ref[...]

    square_row = lax.broadcasted_iota(jnp.int32, (BLK, 2 * BLK), 0)
    square_col = lax.rem(lax.broadcasted_iota(jnp.int32, (BLK, 2 * BLK), 1), BLK)
    earlier = (square_col < square_row).astype(F32).astype(BF16)
    later = (square_col > square_row).astype(F32).astype(BF16)
    few = 32

    def every_block(one, backward):
        low = span // BLK - 1

        def early():
            for b in range(low)[:: -1 if backward else 1]:
                one(b, 0, (b + 1) * BLK)

        def rest():
            def step(i, _):
                b = blocks - 1 - i if backward else low + i
                one(b, pl.multiple_of((b - low) * BLK, BLK), span)
                return 0

            lax.fori_loop(0, blocks - low, step, 0)

        for part in (rest, early) if backward else (early, rest):
            part()

    def by_rows(b, one):
        def step(i, _):
            base = pl.multiple_of(i * few, few)
            one(pl.ds(base, few), pl.ds(pl.multiple_of(b * BLK + base, few), few), base)
            return 0

        lax.fori_loop(0, BLK // few, step, 0, unroll=True)

    def two_part(values, part, keys):
        high = values.astype(BF16)
        pick_scr[part, :keys] = high
        pick_scr[pl.ds(pl.multiple_of(part.start + BLK, few), few), :keys] = (
            values - high.astype(F32)
        ).astype(BF16)

    def behind(base, keys):
        row = lax.broadcasted_iota(jnp.int32, (few, keys), 0) + (base + keys - BLK)
        return row - lax.broadcasted_iota(jnp.int32, (few, keys), 1)

    carry_ref[...] = jnp.zeros_like(carry_ref)

    def attend(b, start, keys):
        rows, window = rows_of(b), pl.ds(start, keys)
        raw_scr[heads, :, :keys] = dot(qkv_ref[3 * heads, rows], qkv_ref[3 * heads + 1, window], NT)
        for h in range(heads):
            raw_scr[h, :, :keys] = dot(qkv_ref[h, rows], qkv_ref[heads + h, window], NT)
        seg_row = seg_row_ref[:, window]

        def pick(part, whole, base):
            first = raw_scr[heads, part, :keys] - shift
            small = jnp.exp(-jnp.abs(first))
            soft = jnp.maximum(first, 0.0) + jnp.log(1.0 + small)
            strict = (seg_col_ref[whole] == seg_row) & (behind(base, keys) > 0)
            two_part(jnp.where(strict, soft, 0.0), part, keys)
            share = jnp.where(first >= 0.0, 1.0, small) / (1.0 + small)
            sig_ref[whole, :keys] = jnp.where(strict, share, 0.0).astype(BF16)

        by_rows(b, pick)
        raw_scr[heads, :, :keys] = dot(earlier, pick_scr[:, :keys], NN)
        before = carry_ref[0:1, window]
        last = [pick_scr[end - few : end, :keys].astype(F32)[few - 1 :] for end in (BLK, 2 * BLK)]
        carry_ref[0:1, window] = before + raw_scr[heads, BLK - 1 : BLK, :keys] + (last[0] + last[1])

        def soften(part, whole, base):
            allowed = (seg_col_ref[whole] == seg_row) & (behind(base, keys) >= 0)
            penalty = jnp.where(allowed, raw_scr[heads, part, :keys] + before, 1e30).astype(BF16)
            pen_ref[whole, :keys] = penalty
            penalty = penalty.astype(F32)
            for h in range(heads):
                logits = raw_scr[h, part, :keys] - penalty
                top = jnp.max(logits, axis=-1, keepdims=True)
                weights = jnp.exp(logits - top)
                total = jnp.sum(weights, axis=-1, keepdims=True)
                lse_ref[whole, h : h + 1] = top + jnp.log(total)
                probs_scr[h, part, :keys] = (weights * (1.0 / total)).astype(BF16)

        by_rows(b, soften)
        mixed = [dot(probs_scr[h, :, :keys], qkv_ref[2 * heads + h, window], NN) for h in range(heads)]
        o = jnp.concatenate(mixed, axis=1).astype(BF16)
        o_ref[rows] = o
        one.pack(b, o)
        one.send(b)

    outer.relay(0)

    def mlp(b):
        one.arrived(b)
        rows = rows_of(b)
        one.lay(b, o_all, pl.ds(0, BLK))
        resid = x_ref[rows].astype(F32) + dot(o_all[...], wo_all[...], NT)
        resid_ref[rows] = resid
        plain, _ = plain_norm(resid)
        cn = (plain * gain_two + bias_two).astype(BF16)
        cn_ref[rows] = cn
        u = dot(cn, w1_ref[...], NN)
        root = math.sqrt(2.0 / math.pi)
        square = u * u
        bent = jnp.tanh(root * u * (1.0 + 0.044715 * square))
        half = 0.5 * (1.0 + bent)
        s_ref[rows] = (u * half).astype(BF16)
        slope = half + 0.5 * u * (1.0 - bent * bent) * (root * (1.0 + 3 * 0.044715 * square))
        du = (dot(dy_ref[rows], w2_ref[...], NN) * slope).astype(BF16)
        du_ref[rows] = du
        x3_ref[rows] = dot(du, w1_ref[...], NT).astype(BF16)
        three.enter(b)

    lag, turned_from = 3, blocks - 3

    def mlp_and_send(b):
        mlp(b)

        def before():
            three.add(b - 1)
            three.cross(b - 1)

        if isinstance(b, int):
            if 0 < b <= turned_from:
                before()
        else:
            pl.when((b > 0) & (b <= turned_from))(before)

    def forward(b, start, keys):
        attend(b, start, keys)
        if isinstance(b, int):
            if b == lag - 1:
                outer.arrived(0)
                outer.lay(0, wo_all, pl.ds(0, width))
            if b >= lag - 1:
                one.relay(b - lag + 1)
            if b >= lag:
                mlp_and_send(b - lag)
        else:
            one.relay(b - lag + 1)
            mlp_and_send(b - lag)

    every_block(forward, False)

    def forward_last(i, _):
        b = blocks - lag + i

        @pl.when(i < lag - 1)
        def _():
            one.relay(b + 1)

        mlp_and_send(b)
        return 0

    lax.fori_loop(0, lag, forward_last, 0)
    for b in reversed(range(turned_from, blocks)):
        three.add(b)
        three.cross(b)

    def mlp_out(i, _):
        rows = wide_rows(i)
        out_ref[rows] = dot(s_ref[rows], w2_ref[...], NT).astype(BF16)
        return 0

    lax.fori_loop(0, length // wide, mlp_out, 0)
    mat_ref[:, cuts[3] : cuts[4]] = dot(dy_ref[...], s_ref[...], TN).astype(BF16)
    mat_ref[:, cuts[1] : cuts[2]] = dot(cn_ref[...], du_ref[...], TN).astype(BF16)
    mat_ref[:, cuts[4] :] = jnp.zeros((width, mat_ref.shape[1] - cuts[4]), BF16)

    for early in range(turned_from):
        three.relay(early)
    three.relay(blocks - 1)
    ng_ref[...] = jnp.zeros_like(ng_ref)
    carry_ref[...] = jnp.zeros_like(carry_ref)
    dkv_ref[...] = jnp.zeros_like(dkv_ref)

    def back(b, start, keys):
        def ahead():
            three.relay(b - 1)

        if not isinstance(b, int):
            pl.when(b > turned_from)(ahead)
        elif b > turned_from:
            ahead()
        three.arrived(b)
        rows, window = rows_of(b), pl.ds(start, keys)
        plain, inverse_std = plain_norm(resid_ref[rows])
        d_two = three.sums(b)
        ng_ref[0:1, :] += jnp.sum(d_two * plain, axis=0, keepdims=True)
        ng_ref[1:2, :] += jnp.sum(d_two, axis=0, keepdims=True)
        dres = dy_ref[rows].astype(F32) + norm_back(plain, inverse_std, d_two * gain_two)
        dhb = dres.astype(BF16)
        dhb_ref[rows] = dhb
        do = dot(dhb, wo_ref[...], NN).astype(BF16)
        do = [do[:, h * HD : (h + 1) * HD] for h in range(heads)]
        for h in range(heads):
            raw_scr[h, :, :keys] = dot(qkv_ref[h, rows], qkv_ref[heads + h, window], NT)
            back_scr[h, :, :keys] = dot(do[h], qkv_ref[2 * heads + h, window], NT)

        def harden(part, whole, base):
            penalty = pen_ref[whole, :keys].astype(F32)
            total = None
            for h in range(heads):
                probs = jnp.exp(raw_scr[h, part, :keys] - penalty - lse_ref[whole, h : h + 1])
                dprobs = back_scr[h, part, :keys]
                inner = jnp.sum(dprobs * probs, axis=-1, keepdims=True)
                dlogits = probs * (dprobs - inner)
                probs_scr[h, part, :keys] = probs.astype(BF16)
                draw_scr[h, part, :keys] = dlogits.astype(BF16)
                total = dlogits if total is None else total + dlogits
            two_part(total, part, keys)

        by_rows(b, harden)
        raw_scr[heads, :, :keys] = dot(later, pick_scr[:, :keys], NN)
        after = carry_ref[0:1, window]
        top = [pick_scr[start_ : start_ + few, :keys].astype(F32)[:1] for start_ in (0, BLK)]
        carry_ref[0:1, window] = after + raw_scr[heads, 0:1, :keys] + (top[0] + top[1])

        def select(part, whole, base):
            suffix = raw_scr[heads, part, :keys] + after
            draw_scr[heads, part, :keys] = (sig_ref[whole, :keys].astype(F32) * -suffix).astype(BF16)

        by_rows(b, select)
        dq = []
        for h in range(heads):
            draw = draw_scr[h, :, :keys]
            dq.append(dot(draw, qkv_ref[heads + h, window], NN) * 0.125)
            dkv_ref[h * HD : (h + 1) * HD, window] += dot(qkv_ref[h, rows], draw, TN)
            dkv_ref[attn + h * HD : attn + (h + 1) * HD, window] += dot(do[h], probs_scr[h, :, :keys], TN)
        draw = draw_scr[heads, :, :keys]
        dq.append(dot(draw, qkv_ref[3 * heads + 1, window], NN) * 0.125)
        dkv_ref[2 * attn : 2 * attn + HD, window] += dot(qkv_ref[3 * heads, rows], draw, TN)
        dproj_ref[rows, :attn] = jnp.concatenate(dq[:heads], axis=1).astype(BF16)
        dproj_ref[rows, 3 * attn : 3 * attn + HD] = dq[heads].astype(BF16)

    every_block(back, True)
    dproj_ref[:, 3 * attn + HD : 3 * attn + 2 * HD] = dkv_ref[2 * attn :].T.astype(BF16)

    def collect(src, dst, where, i):
        return remote(src, dst, collect_sem.at[i], collect_sem.at[i + 2], where)

    gf_ref[...] = dot(a_ref[...], dproj_ref[:, 3 * attn :], TN).astype(BF16)

    @pl.when(core == 1)
    def _():
        collect(gf_ref, gf_near, beside, 0).start()

    @pl.when(core == 0)
    def _():
        collect(gf_ref, gf_near, beside, 0).wait_recv()
        gf_ref[...] = (gf_ref[...].astype(F32) + gf_near[...].astype(F32)).astype(BF16)

    @pl.when(t == 2)
    def _():
        collect(gf_ref, gf_far, over, 1).start()

    dproj_ref[:, attn : 3 * attn] = dkv_ref[: 2 * attn].T.astype(BF16)
    mat_ref[:, cuts[2] : cuts[3]] = dot(dhb_ref[...], o_ref[...], TN).astype(BF16)
    grad = dot(a_ref[...], dproj_ref[:, : 3 * attn], TN)
    mat_ref[:, : cuts[1]] = grad.astype(BF16)

    @pl.when(t == 0)
    def _():
        collect(gf_ref, gf_far, over, 1).wait_recv()
        extra = gf_ref[...].astype(F32) + gf_far[...].astype(F32)
        mat_ref[:, :HD] = (mat_ref[:, :HD].astype(F32) + extra[:, :HD]).astype(BF16)
        mat_ref[:, attn : attn + HD] = (mat_ref[:, attn : attn + HD].astype(F32) + extra[:, HD:]).astype(BF16)
        give(over, 0).wait_send()

    @pl.when(core == 0)
    def _():
        give(beside, 1).wait_send()

    @pl.when(core == 1)
    def _():
        collect(gf_ref, gf_near, beside, 0).wait_send()

    @pl.when(t == 2)
    def _():
        collect(gf_ref, gf_far, over, 1).wait_send()

    def close(b, _):
        one.close(b)
        three.close(b)
        return 0

    lax.fori_loop(0, blocks, close, 0)
    outer.close(0)


def layer(inputs, segments, cotangent, wp, w1, wo, w2, norms, block):
    length, width = inputs.shape
    attn, hidden = wo.shape[1], w1.shape[1]
    heads = attn // HD
    rows, cols = width // block, 4 * attn // block + 2 * (hidden // block)
    cuts = piece_cuts(rows, cols, width // attn)
    blocks = length // BLK
    span = min(length // 2 + BLK, length)

    def low(*shape):
        return pltpu.VMEM(shape, BF16)

    half = length // 2
    total = [low(length, width)] + [low(half, width)] * 5 + [pltpu.SemaphoreType.DMA((8, blocks))]

    def out(shape, dtype):
        return jax.ShapeDtypeStruct(shape, dtype)

    return pl.pallas_call(
        functools.partial(layer_kernel, heads, shift_for(length), [cut * block for cut in cuts]),
        out_shape=[
            out((width, cols * block + 128), BF16),
            out((length, width), BF16),
            out((length, 3 * attn + 2 * HD), BF16),
            out((width, 2 * HD), BF16),
            out((length, width), BF16),
            out((length, width), F32),
            out((2, width), F32),
        ],
        in_specs=[VM] * 8,
        out_specs=[VM] * 7,
        scratch_shapes=[
            low(length, width),
            low(width, 2 * HD),
            low(3 * heads + 2, length, HD),
            low(length, span),
            low(length, span),
            pltpu.VMEM((length, 8), F32),
            low(length, attn),
            low(length, width),
            low(length, hidden),
            low(length, hidden),
            pltpu.VMEM((2 * attn + HD, length), F32),
            pltpu.VMEM((8, length), F32),
            pltpu.VMEM((heads + 1, BLK, span), F32),
            pltpu.VMEM((heads, BLK, span), F32),
            low(heads, BLK, span),
            low(heads + 1, BLK, span),
            low(2 * BLK, span),
        ]
        + [low(blocks, attn, BLK)] * 4
        + [pltpu.SemaphoreType.DMA((6, blocks)), low(BLK, width)]
        + [low(1, width + width // 2, BLK)] * 4
        + [pltpu.SemaphoreType.DMA((6, 1)), low(width, width)]
        + total
        + [low(width, 2 * HD)] * 3
        + [pltpu.SemaphoreType.DMA((3,)), pltpu.SemaphoreType.DMA((4,))]
        + [pltpu.VMEM((1, length), F32), pltpu.VMEM((length, 1), F32)],
        compiler_params=pltpu.CompilerParams(
            collective_id=3, has_side_effects=True, vmem_limit_bytes=LAYER_LIMIT
        ),
        name="layer",
        cost_estimate=pl.CostEstimate(flops=0, bytes_accessed=221000000, transcendentals=0),
    )(
        inputs,
        segments.reshape(1, length),
        cotangent,
        wp,
        w1,
        wo,
        w2,
        norms,
    )


def settle_kernel(
    n,
    count,
    inverse_ref,
    mat_ref,
    out_in,
    dproj_ref,
    wp_ref,
    wf_ref,
    dhb_ref,
    resid_ref,
    x_ref,
    norm_ref,
    ng_in,
    g_ref,
    output_ref,
    grad_ref,
    ng_ref,
    p_ref,
    u_scr,
    xin,
    lin,
    rin,
    x_send,
    x_recv,
    l_send,
    l_recv,
    r_send,
    r_recv,
    near4,
    mine4,
    far4,
    near_mine4,
    near_far4,
    sem4,
    near2,
    mine2,
    far2,
    near_mine2,
    near_far2,
    sem2,
    norm_held,
    norm_send,
    norm_recv,
    da_scr,
):
    m = n // 2
    dp, t = lax.axis_index("dp"), lax.axis_index("tensor")
    place, side = dp // 2, lax.rem(dp, 2)
    pair = (place * 2 + 1 - side, t)
    four = Total(dp, t, da_scr, near4, mine4, far4, near_mine4, near_far4, sem4)
    two = Total(dp, t, out_in, near2, mine2, far2, near_mine2, near_far2, sem2)
    blocks = four.blocks
    peers = [lax.rem(dp + hop, n) for hop in range(1, n)]
    size, wide = p_ref.shape[1:]
    cols = (mat_ref.shape[1] - 128) // size

    def chop(row, _):
        whole_row = mat_ref[pl.ds(pl.multiple_of(row * size, size), size), :]
        for c in range(cols):
            u_scr[row * cols + c] = whole_row[:, c * size : (c + 1) * size]
        return 0

    lax.fori_loop(0, mat_ref.shape[0] // size, chop, 0)
    greet([four.beside, four.over] + [(peer, t) for peer in peers])

    def across(q):
        return remote(p_ref.at[q * 2 + 1 - side], xin.at[q], x_send.at[q], x_recv.at[q], pair)

    def rightward(q):
        return remote(lin.at[q], lin.at[q], r_send.at[q], l_recv.at[q], (dp + 2, t))

    def leftward(q):
        return remote(rin.at[q], rin.at[q], l_send.at[q], r_recv.at[q], (dp - 2, t))

    def both(hop, one):
        @pl.when(place + hop < m)
        def _():
            one(place + hop, True)

        if hop > 0:
            @pl.when(place - hop >= 0)
            def _():
                one(place - hop, False)

    def work(q, right):
        lay(q * 2 + side)
        across(q).wait_recv()
        own = p_ref[q * 2 + side].astype(F32) + xin[q].astype(F32)
        if right:
            @pl.when(place > 0)
            def _():
                rightward(q).wait_recv()
                lin[q] = (own + lin[q].astype(F32)).astype(BF16)

            @pl.when(place == 0)
            def _():
                lin[q] = own.astype(BF16)

            rightward(q).start()
        else:
            @pl.when(place < m - 1)
            def _():
                leftward(q).wait_recv()
                rin[q] = (own + rin[q].astype(F32)).astype(BF16)

            @pl.when(place == m - 1)
            def _():
                rin[q] = own.astype(BF16)

            leftward(q).start()

    def keep():
        q = place
        lay(q * 2 + side)
        across(q).wait_recv()
        g_ref[...] = p_ref[q * 2 + side].astype(F32) + xin[q].astype(F32)

        @pl.when(place > 0)
        def _():
            rightward(q).wait_recv()
            g_ref[...] += lin[q].astype(F32)

        @pl.when(place < m - 1)
        def _():
            leftward(q).wait_recv()
            g_ref[...] += rin[q].astype(F32)

    def norm_copy(peer):
        return remote(ng_ref, norm_held.at[dp], norm_send.at[peer], norm_recv.at[dp], (peer, t))

    def norm_from(peer):
        return remote(ng_ref, norm_held.at[peer], norm_send.at[peer], norm_recv.at[peer], (peer, t))

    some = math.gcd(count, 8)
    room = tiles_up(some * size) // 128

    def strip(base):
        return jnp.concatenate([u_scr[inverse_ref[base + e]] for e in range(some)], axis=1)

    def lay(d):
        if some * size == room * 128:
            def one(g, _):
                place = pl.ds(pl.multiple_of(g * room * 128, 128), room * 128)
                p_ref[d, :, place] = strip(d * count + g * some)
                return 0

            lax.fori_loop(0, count // some, one, 0, unroll=3)
        else:
            parts = [strip(d * count + g * some)[:, : some * size] for g in range(count // some)]
            if wide > count * size:
                parts.append(jnp.zeros((size, wide - count * size), BF16))
            p_ref[d] = jnp.concatenate(parts, axis=1)

    def give(q, right):
        lay(q * 2 + 1 - side)
        across(q).start()

    cut = wp_ref.shape[1]

    def project_back(b):
        rows = pl.ds(b * four.size, four.size)
        da = dot(dproj_ref[rows, :cut], wp_ref[...], NT)
        da_scr[rows] = (da + dot(dproj_ref[rows, cut:], wf_ref[...], NT)).astype(BF16)
        four.enter(b)

    for step, hop in enumerate(reversed(range(m))):
        both(hop, give)
        if step == 0:
            for b in range(blocks):
                project_back(b)
        if step == 1:
            for b in range(blocks):
                four.add(b)
                four.cross(b)
                two.enter(b)
    for b in range(blocks):
        two.add(b)
        two.cross(b)

    ng_ref[...] = jnp.zeros_like(ng_ref)
    gain = norm_ref[0:1, :]

    def rows_of(b):
        return pl.ds(b * four.size, four.size)

    def grad_block(b):
        rows = rows_of(b)
        four.arrived(b)
        d_one = four.sums(b)
        plain, inverse_std = plain_norm(x_ref[rows].astype(F32))
        ng_ref[0:1, :] += jnp.sum(d_one * plain, axis=0, keepdims=True)
        ng_ref[1:2, :] += jnp.sum(d_one, axis=0, keepdims=True)
        grad_ref[rows] = dhb_ref[rows].astype(F32) + norm_back(plain, inverse_std, d_one * gain)

    def out_block(b):
        rows = rows_of(b)
        two.arrived(b)
        output_ref[rows] = (resid_ref[rows] + two.sums(b)).astype(BF16)

    def norms_out():
        ng_ref[2:4, :] = ng_in[...]
        for peer in peers:
            norm_copy(peer).start()

    def norms_in():
        for peer in peers:
            norm_from(peer).wait_recv()
        total = None
        for source in range(n):
            term = jnp.where(dp == source, ng_ref[...], norm_held[source])
            total = term if total is None else total + term
        for peer in peers:
            norm_copy(peer).wait_send()
        ng_ref[...] = total

    tasks = []
    for b in range(blocks):
        tasks.append(functools.partial(four.relay, b))
        if b > 0:
            tasks.append(functools.partial(grad_block, b - 1))
    tasks.append(functools.partial(grad_block, blocks - 1))
    tasks.append(norms_out)
    for b in range(blocks):
        tasks.append(functools.partial(two.relay, b))
        if b > 0:
            tasks.append(functools.partial(out_block, b - 1))
    tasks.append(functools.partial(out_block, blocks - 1))
    done = 0
    for step, hop in enumerate(reversed(range(1, m))):
        until = min((1, 10, 18, len(tasks))[min(step, 3)], len(tasks))
        while done < until:
            tasks[done]()
            done += 1
        both(hop, work)
    while done < len(tasks):
        tasks[done]()
        done += 1
    keep()
    norms_in()

    def finish(q, _):
        across(q).wait_send()

        @pl.when(q > place)
        def _():
            rightward(q).wait_send()

        @pl.when(q < place)
        def _():
            leftward(q).wait_send()

        return 0

    lax.fori_loop(0, m, finish, 0)
    for b in range(blocks):
        four.close(b)
        two.close(b)


def settle(inverse, matrix, block, out_part, dproj, wp, wf, dhb, resid, inputs, norms, ng, n):
    count = matrix.shape[0] // block * ((matrix.shape[1] - 128) // block) // n
    wide = tiles_up(count * block)
    m = n // 2
    length, width = inputs.shape
    blocks = 8

    def low(*shape):
        return pltpu.VMEM(shape, BF16)

    half = length // 2
    total = [low(half, width)] * 5 + [pltpu.SemaphoreType.DMA((8, blocks))]
    return pl.pallas_call(
        functools.partial(settle_kernel, n, count),
        out_shape=[
            jax.ShapeDtypeStruct((block, wide), F32),
            jax.ShapeDtypeStruct((length, width), BF16),
            jax.ShapeDtypeStruct((length, width), F32),
            jax.ShapeDtypeStruct((4, width), F32),
        ],
        in_specs=[pl.BlockSpec(memory_space=pltpu.SMEM)] + [VM] * 10,
        out_specs=[VM] * 4,
        scratch_shapes=[low(n, block, wide), low(n * count, block, block)]
        + [low(m, block, wide)] * 3
        + [pltpu.SemaphoreType.DMA((m,))] * 6
        + total
        + total
        + [pltpu.VMEM((n, 4, width), F32), pltpu.SemaphoreType.DMA((n,)), pltpu.SemaphoreType.DMA((n,))]
        + [low(length, width)],
        compiler_params=pltpu.CompilerParams(
            collective_id=2, has_side_effects=True, vmem_limit_bytes=SETTLE_LIMIT
        ),
        name="settle",
        cost_estimate=pl.CostEstimate(flops=0, bytes_accessed=187000000, transcendentals=0),
    )(inverse, matrix, out_part, dproj, wp, wf, dhb, resid, inputs, norms, ng)


def norm_update(grad, master, first, second):
    new_first = beta_one * first + (1.0 - beta_one) * grad
    new_second = beta_two * second + (1.0 - beta_two) * grad * grad
    direction = (
        new_first
        / (1.0 - beta_one**STEP)
        / (jnp.sqrt(new_second / (1.0 - beta_two**STEP)) + adam_eps)
    )
    return (new_first, new_second, master - norm_rate * direction)


def body(
    inputs,
    segments,
    cotangent,
    owner,
    masters,
    first_moment,
    second_moment,
    left_stats,
    right_stats,
    left_basis,
    right_basis,
    norm_master,
    norm_first,
    norm_second,
):
    length = inputs.shape[1]
    width = inputs.shape[2]
    n_dp = lax.axis_size("dp")
    parts = lax.axis_size("tensor")
    per_dev = masters.shape[1]
    block = masters.shape[-1]
    slots, inverse = lax.optimization_barrier(block_slots(owner, per_dev))
    pieces, norms = gather_masters(
        slots, masters[0], norm_master, n_dp, width // block, parts
    )
    grad_matrix, out_part, dproj, w_first, dhb, resid, norm_grads = layer(
        inputs[0], segments[0], cotangent[0], *pieces, norms, block
    )
    own_packed, output, input_grad, norm_grads = settle(
        inverse,
        grad_matrix,
        block,
        out_part,
        dproj,
        pieces[0],
        w_first,
        dhb,
        resid,
        inputs[0],
        norms,
        norm_grads,
        n_dp,
    )
    *updated, output, input_grad = soap(
        own_packed,
        output,
        input_grad,
        masters[0],
        first_moment[0],
        second_moment[0],
        left_stats[0],
        right_stats[0],
        left_basis[0],
        right_basis[0],
    )
    norm_grads, output = lax.optimization_barrier((norm_grads, output))
    norm_per = norm_master.shape[0]
    own_norm_grads = lax.dynamic_slice_in_dim(
        norm_grads.reshape(-1), lax.axis_index("dp") * norm_per, norm_per
    )
    norm_first_new, norm_second_new, norm_new = norm_update(
        own_norm_grads, norm_master, norm_first, norm_second
    )
    return (
        output[None],
        input_grad[None],
        *[item[None] for item in updated],
        norm_first_new,
        norm_second_new,
        norm_new,
    )


def solution(mesh):
    in_specs = (
        P("dp", None, None),
        P("dp", None),
        P("dp", None, None),
        P(),
        P("tensor", "dp", None, None),
        P("tensor", "dp", None, None),
        P("tensor", "dp", None, None),
        P("tensor", "dp", None, None),
        P("tensor", "dp", None, None),
        P("tensor", "dp", None, None),
        P("tensor", "dp", None, None),
        P("dp"),
        P("dp"),
        P("dp"),
    )
    out_specs = (
        P("dp", None, None),
        P("dp", None, None),
        P("tensor", "dp", None, None),
        P("tensor", "dp", None, None),
        P("tensor", "dp", None, None),
        P("tensor", "dp", None, None),
        P("tensor", "dp", None, None),
        P("tensor", "dp", None, None),
        P("tensor", "dp", None, None),
        P("dp"),
        P("dp"),
        P("dp"),
    )
    return jax.shard_map(body, mesh=mesh, in_specs=in_specs, out_specs=out_specs, check_vma=False)
```

```python
import functools
import math

import jax
import jax.numpy as jnp
from jax import lax
from jax.experimental import pallas as pl
from jax.experimental.pallas import tpu as pltpu
from jax.sharding import PartitionSpec as P

HD = 64
STEP = 10
F32 = jnp.float32
BF16 = jnp.bfloat16
LAYER_LIMIT = 35 * 2**20
GATHER_LIMIT = 35 * 2**20
SETTLE_LIMIT = 31 * 2**20

norm_eps = 1e-05
beta_one = 0.9
beta_two = 0.95
beta_stats = 0.95
learn_rate = 0.03
norm_rate = 0.4
weight_decay = 0.01
adam_eps = 1e-08


def shift_for(length):
    return math.log(length / 8.0)


def block_slots(owner, per_dev):
    count = owner.shape[0]
    index = jnp.arange(count, dtype=jnp.int32)
    earlier = (owner[:, None] == owner[None, :]) & (index[None, :] < index[:, None])
    rank = jnp.sum(earlier.astype(jnp.int32), axis=1)
    slots = owner * per_dev + rank
    inverse = jnp.sum(jnp.where(slots[None, :] == index[:, None], index[None, :], 0), axis=1)
    return (slots, inverse)


def norm_back(plain, inverse_std, grad):
    return inverse_std * (
        grad
        - jnp.mean(grad, axis=-1, keepdims=True)
        - plain * jnp.mean(grad * plain, axis=-1, keepdims=True)
    )


def piece_cuts(rows, cols, parts):
    attn = rows // parts
    hidden = (cols - 4 * attn) // 2
    return (0, 3 * attn, 3 * attn + hidden, 4 * attn + hidden, cols)


MESH = pl.DeviceIdType.MESH
VM = pl.BlockSpec(memory_space=pltpu.VMEM)
MIB = 2**20


def tiles_up(value):
    return -(-value // 128) * 128


def remote(src, dst, send, recv, where):
    return pltpu.make_async_remote_copy(
        src_ref=src, dst_ref=dst, send_sem=send, recv_sem=recv, device_id=where, device_id_type=MESH
    )


def greet(devices):
    barrier = pltpu.get_barrier_semaphore()
    for device in devices:
        pl.semaphore_signal(barrier, inc=1, device_id=device, device_id_type=MESH)
    pl.semaphore_wait(barrier, len(devices))


def line_greet(dp, t, m):
    place, side = dp // 2, lax.rem(dp, 2)
    barrier = pltpu.get_barrier_semaphore()
    pl.semaphore_signal(barrier, inc=1, device_id=(place * 2 + 1 - side, t), device_id_type=MESH)

    @pl.when(place > 0)
    def _():
        pl.semaphore_signal(barrier, inc=1, device_id=(dp - 2, t), device_id_type=MESH)

    @pl.when(place < m - 1)
    def _():
        pl.semaphore_signal(barrier, inc=1, device_id=(dp + 2, t), device_id_type=MESH)

    ends = (place == 0).astype(jnp.int32) + (place == m - 1).astype(jnp.int32)
    pl.semaphore_wait(barrier, 3 - ends)


def gather_kernel(
    n, count, block, wide, norm_rows, norm_per, rows, cuts, slot_ref, m_ref, norm_ref, *refs
):
    w_refs, (nout_ref, u_ref, held, send_sem, recv_sem, side_send, side_recv) = refs[:4], refs[4:]
    m = n // 2
    dp, t = lax.axis_index("dp"), lax.axis_index("tensor")
    place, side = dp // 2, lax.rem(dp, 2)
    pair = (place * 2 + 1 - side, t)
    for k in range(count):
        held[dp, :, k * block : (k + 1) * block] = m_ref[k].astype(BF16)
    if wide > count * block:
        held[dp, :, count * block : wide] = jnp.zeros((block, wide - count * block), BF16)
    held[dp, :, wide : wide + 128] = jnp.concatenate(
        [norm_ref[...], jnp.zeros((block - norm_rows, 128), F32)], axis=0
    ).astype(BF16)
    line_greet(dp, t, m)

    total = wide + 128
    less = total // 128 // 6 * 128

    middle = less + (total - less) // 256 * 128
    parts = ((less, middle), (middle, total))

    def send(source, way, where, part):
        first, last = parts[part]
        columns = held.at[source, :, first:last]
        return remote(columns, columns, send_sem.at[source, way, part], recv_sem.at[source, part], where)

    def side_send_to(source, way, where):
        part = held.at[source, :, :less]
        return remote(part, part, side_send.at[source, way], side_recv.at[source], where)

    def side_spread(source, left, right):
        @pl.when(left)
        def _():
            side_send_to(source, 0, (dp - 2, t)).start()

        @pl.when(right)
        def _():
            side_send_to(source, 1, (dp + 2, t)).start()

    def unpack(source):
        for k in range(count):
            u_ref[source * count + k] = held[source, :, k * block : (k + 1) * block]

    def spread(source, left, right, part):
        @pl.when(left)
        def _():
            send(source, 0, (dp - 2, t), part).start()

        @pl.when(right)
        def _():
            send(source, 1, (dp + 2, t), part).start()

        send(source, 2, pair, part).start()

    def spread_done(source, left, right):
        for part in (0, 1):
            send(source, 2, pair, part).wait_send()

            @pl.when(left)
            def _():
                send(source, 0, (dp - 2, t), part).wait_send()

            @pl.when(right)
            def _():
                send(source, 1, (dp + 2, t), part).wait_send()

    side_send_to(dp, 2, pair).start()
    side_spread(dp, place > 0, place < m - 1)
    for part in (0, 1):
        spread(dp, place > 0, place < m - 1, part)
    beside = place * 2 + 1 - side
    side_send_to(beside, 2, pair).wait_recv()
    side_spread(beside, place > 0, place < m - 1)
    unpack(dp)

    def one(hop, _):
        for part in (0, 1):
            @pl.when(place - hop >= 0)
            def _():
                source = dp - 2 * hop
                send(source, 2, pair, part).wait_recv()
                spread(source, False, place < m - 1, part)

            @pl.when(place + hop < m)
            def _():
                source = dp + 2 * hop
                send(source, 2, pair, part).wait_recv()
                spread(source, place > 0, False, part)

        @pl.when(place - hop >= 0)
        def _():
            for s in (0, 1):
                both = (place - hop) * 2 + s
                side_send_to(both, 2, pair).wait_recv()
                side_spread(both, False, place < m - 1)
            unpack(dp - 2 * hop)

        @pl.when(place + hop < m)
        def _():
            for s in (0, 1):
                both = (place + hop) * 2 + s
                side_send_to(both, 2, pair).wait_recv()
                side_spread(both, place > 0, False)
            unpack(dp + 2 * hop)

        return 0

    lax.fori_loop(1, m, one, 0)

    def other(step, _):
        source = step * 2 + 1 - side
        for part in (0, 1):
            send(source, 2, pair, part).wait_recv()
        unpack(source)
        return 0

    lax.fori_loop(0, m, other, 0)

    def strip(row, _):
        for first, last, w_ref in zip(cuts, cuts[1:], w_refs):
            w_ref[pl.ds(pl.multiple_of(row * block, block), block), :] = jnp.concatenate(
                [u_ref[slot_ref[row * cuts[-1] + c]] for c in range(first, last)], axis=1
            )
        return 0

    lax.fori_loop(0, rows, strip, 0)

    line = nout_ref.shape[1]
    for source in range(n):
        values = held[source, :16, wide : wide + 128].astype(F32)
        for r in range(norm_rows):
            spot = source * norm_per + r * 128
            size = min(128, norm_per - r * 128)
            nout_ref[spot // line : spot // line + 1, spot % line : spot % line + size] = values[
                r : r + 1, :size
            ]

    def finish(step, _):
        source = step * 2 + side
        spread_done(
            source,
            (place > 0) & (step >= place),
            (place < m - 1) & (step <= place),
        )
        for s in (0, 1):
            both = step * 2 + s

            @pl.when((place > 0) & (step >= place))
            def _():
                side_send_to(both, 0, (dp - 2, t)).wait_send()

            @pl.when((place < m - 1) & (step <= place))
            def _():
                side_send_to(both, 1, (dp + 2, t)).wait_send()

        return 0

    lax.fori_loop(0, m, finish, 0)
    side_send_to(dp, 2, pair).wait_send()


def gather_masters(slots, masters, norm, n, rows, parts):
    count, block = masters.shape[0], masters.shape[-1]
    wide = tiles_up(count * block)
    norm_rows = -(-norm.shape[0] // 128)
    norm_tile = jnp.pad(norm, (0, norm_rows * 128 - norm.shape[0])).reshape(norm_rows, 128)
    cuts = piece_cuts(rows, n * count // rows, parts)
    *pieces, norms = pl.pallas_call(
        functools.partial(gather_kernel, n, count, block, wide, norm_rows, norm.shape[0], rows, cuts),
        out_shape=[
            jax.ShapeDtypeStruct((rows * block, (last - first) * block), BF16)
            for first, last in zip(cuts, cuts[1:])
        ]
        + [jax.ShapeDtypeStruct((4, n * norm.shape[0] // 4), F32)],
        in_specs=[pl.BlockSpec(memory_space=pltpu.SMEM), VM, VM],
        out_specs=[VM] * 5,
        scratch_shapes=[
            pltpu.VMEM((n * count, block, block), BF16),
            pltpu.VMEM((n, block, wide + 128), BF16),
            pltpu.SemaphoreType.DMA((n, 3, 2)),
            pltpu.SemaphoreType.DMA((n, 2)),
            pltpu.SemaphoreType.DMA((n, 3)),
            pltpu.SemaphoreType.DMA((n,)),
        ],
        compiler_params=pltpu.CompilerParams(
            collective_id=1, has_side_effects=True, vmem_limit_bytes=GATHER_LIMIT
        ),
        name="gather_masters",
        cost_estimate=pl.CostEstimate(flops=0, bytes_accessed=163200000, transcendentals=0),
    )(slots, masters, norm_tile)
    return pieces, norms


NN = ((1,), (0,))
NT = ((1,), (1,))
TN = ((0,), (0,))


def lane_prod(n, lanes, left_row, right_tile, put, group=4):
    tiles = n // 8

    def some(step, _):
        base = step * group

        def one(k, acc):
            rights = [right_tile(k, j) for j in range(tiles)]
            out = []
            for r in range(group):
                row = jnp.broadcast_to(left_row(base + r, k), (8, lanes))
                out.append(tuple(acc[r][j] + row * rights[j] for j in range(tiles)))
            return tuple(out)

        zero = tuple(tuple(jnp.zeros((8, lanes), F32) for _ in range(tiles)) for _ in range(group))
        acc = lax.fori_loop(0, n, one, zero, unroll=8)
        for r in range(group):
            for j in range(tiles):
                put(base + r, j, acc[r][j])
        return 0

    lax.fori_loop(0, n // group, some, 0)


def lane_gram(n, lanes, row, tile, put, put_turned):
    tiles = n // 8
    for first in range(tiles):
        columns = range(first, tiles)

        def some(step, _):
            base = first * 8 + step * 4

            def one(k, acc):
                rights = [tile(k, j) for j in columns]
                out = []
                for r in range(4):
                    left = jnp.broadcast_to(row(base + r, k), (8, lanes))
                    out.append(tuple(a + left * right for a, right in zip(acc[r], rights)))
                return tuple(out)

            zero = tuple(tuple(jnp.zeros((8, lanes), F32) for _ in columns) for _ in range(4))
            acc = lax.fori_loop(0, n, one, zero, unroll=8)
            for r in range(4):
                for j in columns:
                    put(base + r, j, acc[r][j - first])
                    if j > first:
                        put_turned(base + r, j, acc[r][j - first])
            return 0

        lax.fori_loop(0, 2, some, 0)


def soap_kernel(
    n,
    count,
    packed_ref,
    y_ref,
    dx_ref,
    m_ref,
    f_ref,
    s_ref,
    l_ref,
    r_ref,
    ql_ref,
    qr_ref,
    nf_out,
    ns_out,
    nm_out,
    nl_out,
    nr_out,
    bl_out,
    br_out,
    y_out,
    dx_out,
    nf_ref,
    ns_ref,
    nm_ref,
    nl_ref,
    nr_ref,
    basis_ref,
    u_scr,
    g_ref,
    gt_ref,
    qt_ref,
    h_ref,
    d_ref,
    sems,
):
    tiles = n // 8

    def at(ref):
        def row(i, k):
            return ref[pl.ds(i * n + k, 1), :]

        return row

    def at_turned(ref):
        def row(i, k):
            return ref[pl.ds(k * n + i, 1), :]

        return row

    def tile(ref):
        def one(k, j):
            return ref[pl.ds(pl.multiple_of(k * n + 8 * j, 8), 8), :]

        return one

    def turned(i, j):
        return pl.ds(8 * j * n + i, 8, stride=n)

    def turn_into(dst, src):
        def one(k, _):
            for j in range(tiles):
                dst[here(k, j), :] = src[turned(k, j), :]
            return 0

        lax.fori_loop(0, n, one, 0, unroll=4)

    def here(i, j):
        return pl.ds(pl.multiple_of(i * n + 8 * j, 8), 8)

    def send(place, src, dst):
        return pltpu.make_async_copy(src, dst, sems.at[place])

    send(7, y_ref, y_out).start()
    send(8, dx_ref, dx_out).start()
    for c in range(count):
        u_scr[c] = packed_ref[:, c * n : (c + 1) * n]

    def turn(i, _):
        slab = u_scr[:, pl.ds(i, 1), :].reshape(count, n)
        g_ref[pl.ds(pl.multiple_of(i * n, 8), n), :] = slab.T
        return 0

    lax.fori_loop(0, n, turn, 0, unroll=4)

    turn_into(gt_ref, g_ref)
    turn_into(qt_ref, qr_ref)

    def blend(dst, old):
        def put(i, j, value):
            where = here(i, j)
            dst[where, :] = beta_stats * old[where, :] + (1.0 - beta_stats) * value

        def put_turned(i, j, value):
            where = turned(i, j)
            dst[where, :] = beta_stats * old[where, :] + (1.0 - beta_stats) * value

        return put, put_turned

    def store(ref, base=0):
        def put(i, j, value):
            ref[pl.ds(pl.multiple_of(base + i * n + 8 * j, 8), 8), :] = value

        return put

    lane_gram(n, count, at_turned(gt_ref), tile(gt_ref), *blend(nl_ref, l_ref))
    send(3, nl_ref, nl_out).start()
    lane_gram(n, count, at_turned(g_ref), tile(g_ref), *blend(nr_ref, r_ref))
    send(4, nr_ref, nr_out).start()
    lane_prod(n, count, at(nl_ref), tile(ql_ref), store(basis_ref))
    lane_prod(n, count, at(nr_ref), tile(qr_ref), store(basis_ref, n * n))

    sub = lax.broadcasted_iota(jnp.int32, (8, count), 0)
    for panel in range(tiles):
        def side(s, _):
            base = pl.multiple_of(s * n * n, 8)

            def spot(i, j):
                return pl.ds(pl.multiple_of(base + i * n + 8 * j, 8), 8)

            rows = [basis_ref[spot(i, panel), :] for i in range(n)]
            sizes = jnp.ones((8, count), F32)
            for k in range(8):
                heads = [jnp.broadcast_to(row[k : k + 1], (8, count)) for row in rows]
                terms = [head * row for head, row in zip(heads, rows)]
                while len(terms) > 1:
                    terms = [sum(terms[p : p + 2][1:], terms[p]) for p in range(0, len(terms), 2)]
                size = jnp.broadcast_to(terms[0][k : k + 1], (8, count))
                sizes = jnp.where(sub == k, size, sizes)
                factor = jnp.where(sub > k, terms[0] * (1.0 / size), 0.0)
                rows = [row - head * factor for head, row in zip(heads, rows)]
            scale = lax.rsqrt(sizes)
            for i in range(n):
                basis_ref[spot(i, panel), :] = rows[i] * scale
            for start in range(panel + 1, tiles, 3):
                columns = range(start, min(start + 3, tiles))

                def heads_of(i):
                    return [
                        jnp.broadcast_to(basis_ref[pl.ds(base + i * n + 8 * panel + k, 1), :], (8, count))
                        for k in range(8)
                    ]

                def project(i, acc):
                    heads = heads_of(i)
                    values = [basis_ref[spot(i, j), :] for j in columns]
                    return tuple(
                        tuple(a + head * value for a, value in zip(acc[k], values))
                        for k, head in enumerate(heads)
                    )

                zero = tuple(tuple(jnp.zeros((8, count), F32) for _ in columns) for _ in range(8))
                parts = lax.fori_loop(0, n, project, zero, unroll=4)

                def take(i, _):
                    heads = heads_of(i)
                    for c, j in enumerate(columns):
                        value = basis_ref[spot(i, j), :]
                        for k in range(8):
                            value = value - heads[k] * parts[k][c]
                        basis_ref[spot(i, j), :] = value
                    return 0

                lax.fori_loop(0, n, take, 0, unroll=4)
            return 0

        lax.fori_loop(0, 2, side, 0)
    left_basis, right_basis = basis_ref.at[: n * n], basis_ref.at[n * n :]
    send(5, left_basis, bl_out).start()
    send(6, right_basis, br_out).start()

    def put_moments(i, j, rot):
        first = beta_one * f_ref[here(i, j), :] + (1.0 - beta_one) * rot
        second = beta_two * s_ref[here(i, j), :] + (1.0 - beta_two) * rot * rot
        nf_ref[here(i, j), :] = first
        ns_ref[here(i, j), :] = second
        d_ref[here(i, j), :] = first / (1.0 - beta_one**STEP) / (
            jnp.sqrt(second / (1.0 - beta_two**STEP)) + adam_eps
        )

    def put_master(i, j, moved):
        master = m_ref[here(i, j), :]
        nm_ref[here(i, j), :] = master - learn_rate * (moved + weight_decay * master)

    lane_prod(n, count, at_turned(ql_ref), tile(g_ref), store(h_ref))
    lane_prod(n, count, at(h_ref), tile(qr_ref), put_moments)
    send(0, nf_ref, nf_out).start()
    send(1, ns_ref, ns_out).start()
    lane_prod(n, count, at(ql_ref), tile(d_ref), store(h_ref))
    lane_prod(n, count, at(h_ref), tile(qt_ref), put_master)
    send(2, nm_ref, nm_out).start()
    sources = (nf_ref, ns_ref, nm_ref, nl_ref, nr_ref, left_basis, right_basis, y_ref, dx_ref)
    targets = (nf_out, ns_out, nm_out, nl_out, nr_out, bl_out, br_out, y_out, dx_out)
    for place, (src, dst) in enumerate(zip(sources, targets)):
        send(place, src, dst).wait()


def soap(packed, output, input_grad, *state):
    count, n = state[0].shape[0], state[0].shape[-1]
    flat = [item.transpose(1, 2, 0).reshape(n * n, count) for item in state]
    shape = jax.ShapeDtypeStruct((n * n, count), F32)
    room = pltpu.VMEM((n * n, count), F32)
    outs = pl.pallas_call(
        functools.partial(soap_kernel, n, count),
        out_shape=[shape] * 7 + [jax.ShapeDtypeStruct(item.shape, item.dtype) for item in (output, input_grad)],
        in_specs=[VM] * 10,
        out_specs=[pl.BlockSpec(memory_space=pl.ANY)] * 9,
        scratch_shapes=[room] * 5
        + [pltpu.VMEM((2 * n * n, count), F32), pltpu.VMEM((count, n, n), F32)]
        + [room] * 5
        + [pltpu.SemaphoreType.DMA((9,))],
        compiler_params=pltpu.CompilerParams(vmem_limit_bytes=31 * MIB),
        name="soap",
    )(packed, output, input_grad, *flat)
    return [item.reshape(n, n, count).transpose(2, 0, 1) for item in outs[:7]] + list(outs[7:])


BLK = 128


def plain_norm(rows):
    centered = rows - jnp.mean(rows, axis=-1, keepdims=True)
    inverse_std = lax.rsqrt(jnp.mean(centered * centered, axis=-1, keepdims=True) + norm_eps)
    return centered * inverse_std, inverse_std


def dot(left, right, dims):
    return lax.dot_general(left, right, (dims, ((), ())), preferred_element_type=F32)


class Total:
    def __init__(self, dp, t, x, near, mine, far, near_mine, near_far, sems):
        up, core = t // 2, lax.rem(t, 2)
        self.up, self.core = up, core
        self.beside = (dp, up * 2 + 1 - core)
        self.over = (dp, (1 - up) * 2 + core)
        self.x, self.near, self.mine, self.far = x, near, mine, far
        self.near_mine, self.near_far, self.sems = near_mine, near_far, sems
        self.blocks = sems.shape[1]
        self.size = x.shape[0] // self.blocks
        self.half = self.size // 2

    def rows(self, b, core):
        return pl.ds(pl.multiple_of(b * self.size + core * self.half, self.half), self.half)

    def part(self, b):
        return pl.ds(pl.multiple_of(b * self.half, self.half), self.half)

    def copy(self, kind, b):
        here = self.part(b)
        src, dst, where = (
            (self.x.at[self.rows(b, 1 - self.core)], self.near, self.beside),
            (self.mine.at[here], self.far, self.over),
            (self.mine.at[here], self.near_mine, self.beside),
            (self.far.at[here], self.near_far, self.beside),
        )[kind]
        return remote(src, dst.at[here], self.sems.at[2 * kind, b], self.sems.at[2 * kind + 1, b], where)

    def enter(self, b):
        self.copy(0, b).start()

    def add(self, b):
        here = self.part(b)
        self.copy(0, b).wait_recv()
        self.mine[here] = (self.x[self.rows(b, self.core)].astype(F32) + self.near[here].astype(F32)).astype(BF16)

    def cross(self, b):
        self.copy(1, b).start()
        self.copy(2, b).start()

    def relay(self, b):
        self.copy(1, b).wait_recv()
        self.copy(3, b).start()

    def arrived(self, b):
        self.copy(2, b).wait_recv()
        self.copy(3, b).wait_recv()

    def sums(self, b):
        here = self.part(b)
        own = self.mine[here].astype(F32) + self.far[here].astype(F32)
        other = self.near_mine[here].astype(F32) + self.near_far[here].astype(F32)
        low = self.core == 0
        return jnp.concatenate([jnp.where(low, own, other), jnp.where(low, other, own)], axis=0)

    def close(self, b):
        for kind in range(4):
            self.copy(kind, b).wait_send()


class Packs:
    def __init__(self, total, own, beside, over, far, sems):
        self.beside, self.over = total.beside, total.over
        self.up, self.core = total.up, total.core
        self.own, self.from_beside, self.from_over, self.from_far, self.sems = own, beside, over, far, sems

    def copy(self, kind, b):
        src, dst, where = (
            (self.own, self.from_beside, self.beside),
            (self.own, self.from_over, self.over),
            (self.from_over, self.from_far, self.beside),
        )[kind]
        return remote(src.at[b], dst.at[b], self.sems.at[2 * kind, b], self.sems.at[2 * kind + 1, b], where)

    def send(self, b):
        self.copy(1, b).start()
        self.copy(0, b).start()

    def relay(self, b):
        self.copy(1, b).wait_recv()
        self.copy(2, b).start()

    def arrived(self, b):
        self.copy(0, b).wait_recv()
        self.copy(2, b).wait_recv()

    def close(self, b):
        for kind in range(3):
            self.copy(kind, b).wait_send()

    def lay(self, b, dst, rows):
        tall = rows.size
        pairs = ((self.up, self.own, self.from_beside), (1 - self.up, self.from_over, self.from_far))
        for up, same, other in pairs:
            for core, ref in ((self.core, same), (1 - self.core, other)):
                dst[rows, pl.ds(pl.multiple_of((up * 2 + core) * 128, 128), 128)] = ref[b, :tall]
            first, second = same[b, tall:], other[b, tall:]
            low = self.core == 0
            zero = jnp.where(low, first.astype(F32), second.astype(F32)).astype(BF16)
            one = jnp.where(low, second.astype(F32), first.astype(F32)).astype(BF16)
            tail = jnp.concatenate(
                [
                    jnp.concatenate([zero[:, :HD], one[:, :HD]], axis=1),
                    jnp.concatenate([zero[:, HD:], one[:, HD:]], axis=1),
                ],
                axis=0,
            )
            dst[rows, pl.ds(pl.multiple_of(512 + up * 128, 128), 128)] = tail

    def pack(self, b, value):
        tall = value.shape[0]
        self.own[b, :tall] = value[:, :128]
        self.own[b, tall:] = jnp.concatenate([value[: tall // 2, 128:], value[tall // 2 :, 128:]], axis=1)


def layer_kernel(
    heads,
    shift,
    cuts,
    x_ref,
    seg_in,
    dy_ref,
    wp_ref,
    w1_ref,
    wo_ref,
    w2_ref,
    norm_ref,
    mat_ref,
    out_ref,
    dproj_ref,
    wf_out,
    dhb_ref,
    resid_ref,
    ng_ref,
    a_ref,
    wf_ref,
    qkv_ref,
    pen_ref,
    sig_ref,
    lse_ref,
    o_ref,
    cn_ref,
    s_ref,
    du_ref,
    dkv_ref,
    carry_ref,
    raw_scr,
    back_scr,
    probs_scr,
    draw_scr,
    pick_scr,
    o_own,
    o_beside,
    o_over,
    o_far,
    o_sem,
    o_all,
    wo_own,
    wo_beside,
    wo_over,
    wo_far,
    wo_sem,
    wo_all,
    x3_ref,
    near3,
    mine3,
    far3,
    near_mine3,
    near_far3,
    sem3,
    gf_ref,
    gf_near,
    gf_far,
    share_sem,
    collect_sem,
    seg_row_ref,
    seg_col_ref,
):
    dp, t = lax.axis_index("dp"), lax.axis_index("tensor")
    up, core = t // 2, lax.rem(t, 2)
    beside, over = (dp, up * 2 + 1 - core), (dp, (1 - up) * 2 + core)
    length, width = x_ref.shape
    blocks = length // BLK
    span = min(length // 2 + BLK, length)
    attn = heads * HD
    three = Total(dp, t, x3_ref, near3, mine3, far3, near_mine3, near_far3, sem3)
    one = Packs(three, o_own, o_beside, o_over, o_far, o_sem)
    outer = Packs(three, wo_own, wo_beside, wo_over, wo_far, wo_sem)
    greet([beside, over])
    seg_row_ref[...] = seg_in[...].astype(F32)
    by_block = jnp.concatenate([seg_row_ref[:, b * BLK : (b + 1) * BLK] for b in range(blocks)], axis=0)
    turned_seg = by_block.T
    for b in range(blocks):
        seg_col_ref[b * BLK : (b + 1) * BLK] = turned_seg[:, b : b + 1]

    def give(where, i):
        return remote(wf_ref, wf_ref, share_sem.at[i], share_sem.at[2], where)

    @pl.when(t == 0)
    def _():
        wf_ref[:, :HD] = wp_ref[:, :HD]
        wf_ref[:, HD:] = wp_ref[:, attn : attn + HD]
        give(over, 0).start()
        give(beside, 1).start()

    outer.pack(0, wo_ref[...])
    outer.send(0)

    def rows_of(b):
        return pl.ds(pl.multiple_of(b * BLK, BLK), BLK)

    gain_one, bias_one = norm_ref[0:1, :], norm_ref[1:2, :]
    gain_two, bias_two = norm_ref[2:3, :], norm_ref[3:4, :]
    wide = 2 * BLK

    def wide_rows(i):
        return pl.ds(pl.multiple_of(i * wide, wide), wide)

    def project(i, _):
        rows = wide_rows(i)
        plain, _ = plain_norm(x_ref[rows].astype(F32))
        a = (plain * gain_one + bias_one).astype(BF16)
        a_ref[rows] = a
        projected = dot(a, wp_ref[...], NN)
        for h in range(heads):
            qkv_ref[h, rows] = projected[:, h * HD : (h + 1) * HD].astype(BF16) * 0.125
        for h in range(heads, 3 * heads):
            qkv_ref[h, rows] = projected[:, h * HD : (h + 1) * HD].astype(BF16)
        return 0

    lax.fori_loop(0, length // wide, project, 0)

    @pl.when(t == 2)
    def _():
        give(over, 0).wait_recv()
        give(beside, 1).start()

    @pl.when((t == 1) | (t == 3))
    def _():
        give(beside, 1).wait_recv()

    def project_first(i, _):
        rows = wide_rows(i)
        projected = dot(a_ref[rows], wf_ref[...], NN)
        qkv_ref[3 * heads, rows] = projected[:, :HD].astype(BF16) * 0.125
        qkv_ref[3 * heads + 1, rows] = projected[:, HD:].astype(BF16)
        return 0

    lax.fori_loop(0, length // wide, project_first, 0)
    wf_out[...] = wf_ref[...]

    square_row = lax.broadcasted_iota(jnp.int32, (BLK, 2 * BLK), 0)
    square_col = lax.rem(lax.broadcasted_iota(jnp.int32, (BLK, 2 * BLK), 1), BLK)
    earlier = (square_col < square_row).astype(F32).astype(BF16)
    later = (square_col > square_row).astype(F32).astype(BF16)
    few = 32

    def every_block(one, backward):
        low = span // BLK - 1

        def early():
            for b in range(low)[:: -1 if backward else 1]:
                one(b, 0, (b + 1) * BLK)

        def rest():
            def step(i, _):
                b = blocks - 1 - i if backward else low + i
                one(b, pl.multiple_of((b - low) * BLK, BLK), span)
                return 0

            lax.fori_loop(0, blocks - low, step, 0)

        for part in (rest, early) if backward else (early, rest):
            part()

    def by_rows(b, one):
        def step(i, _):
            base = pl.multiple_of(i * few, few)
            one(pl.ds(base, few), pl.ds(pl.multiple_of(b * BLK + base, few), few), base)
            return 0

        lax.fori_loop(0, BLK // few, step, 0, unroll=True)

    def two_part(values, part, keys):
        high = values.astype(BF16)
        pick_scr[part, :keys] = high
        pick_scr[pl.ds(pl.multiple_of(part.start + BLK, few), few), :keys] = (
            values - high.astype(F32)
        ).astype(BF16)

    def behind(base, keys):
        row = lax.broadcasted_iota(jnp.int32, (few, keys), 0) + (base + keys - BLK)
        return row - lax.broadcasted_iota(jnp.int32, (few, keys), 1)

    carry_ref[...] = jnp.zeros_like(carry_ref)

    def attend(b, start, keys):
        rows, window = rows_of(b), pl.ds(start, keys)
        raw_scr[heads, :, :keys] = dot(qkv_ref[3 * heads, rows], qkv_ref[3 * heads + 1, window], NT)
        for h in range(heads):
            raw_scr[h, :, :keys] = dot(qkv_ref[h, rows], qkv_ref[heads + h, window], NT)
        seg_row = seg_row_ref[:, window]

        def pick(part, whole, base):
            first = raw_scr[heads, part, :keys] - shift
            small = jnp.exp(-jnp.abs(first))
            soft = jnp.maximum(first, 0.0) + jnp.log(1.0 + small)
            strict = (seg_col_ref[whole] == seg_row) & (behind(base, keys) > 0)
            two_part(jnp.where(strict, soft, 0.0), part, keys)
            share = jnp.where(first >= 0.0, 1.0, small) / (1.0 + small)
            sig_ref[whole, :keys] = jnp.where(strict, share, 0.0).astype(BF16)

        by_rows(b, pick)
        raw_scr[heads, :, :keys] = dot(earlier, pick_scr[:, :keys], NN)
        before = carry_ref[0:1, window]
        last = [pick_scr[end - few : end, :keys].astype(F32)[few - 1 :] for end in (BLK, 2 * BLK)]
        carry_ref[0:1, window] = before + raw_scr[heads, BLK - 1 : BLK, :keys] + (last[0] + last[1])

        def soften(part, whole, base):
            allowed = (seg_col_ref[whole] == seg_row) & (behind(base, keys) >= 0)
            penalty = jnp.where(allowed, raw_scr[heads, part, :keys] + before, 1e30).astype(BF16)
            pen_ref[whole, :keys] = penalty
            penalty = penalty.astype(F32)
            for h in range(heads):
                logits = raw_scr[h, part, :keys] - penalty
                top = jnp.max(logits, axis=-1, keepdims=True)
                weights = jnp.exp(logits - top)
                total = jnp.sum(weights, axis=-1, keepdims=True)
                lse_ref[whole, h : h + 1] = top + jnp.log(total)
                probs_scr[h, part, :keys] = (weights * (1.0 / total)).astype(BF16)

        by_rows(b, soften)
        mixed = [dot(probs_scr[h, :, :keys], qkv_ref[2 * heads + h, window], NN) for h in range(heads)]
        o = jnp.concatenate(mixed, axis=1).astype(BF16)
        o_ref[rows] = o
        one.pack(b, o)
        one.send(b)

    outer.relay(0)

    def mlp(b):
        one.arrived(b)
        rows = rows_of(b)
        one.lay(b, o_all, pl.ds(0, BLK))
        resid = x_ref[rows].astype(F32) + dot(o_all[...], wo_all[...], NT)
        resid_ref[rows] = resid
        plain, _ = plain_norm(resid)
        cn = (plain * gain_two + bias_two).astype(BF16)
        cn_ref[rows] = cn
        u = dot(cn, w1_ref[...], NN)
        root = math.sqrt(2.0 / math.pi)
        square = u * u
        bent = jnp.tanh(root * u * (1.0 + 0.044715 * square))
        half = 0.5 * (1.0 + bent)
        s_ref[rows] = (u * half).astype(BF16)
        slope = half + 0.5 * u * (1.0 - bent * bent) * (root * (1.0 + 3 * 0.044715 * square))
        du = (dot(dy_ref[rows], w2_ref[...], NN) * slope).astype(BF16)
        du_ref[rows] = du
        x3_ref[rows] = dot(du, w1_ref[...], NT).astype(BF16)
        three.enter(b)

    lag, turned_from = 3, blocks - 3

    def mlp_and_send(b):
        mlp(b)

        def before():
            three.add(b - 1)
            three.cross(b - 1)

        if isinstance(b, int):
            if 0 < b <= turned_from:
                before()
        else:
            pl.when((b > 0) & (b <= turned_from))(before)

    def forward(b, start, keys):
        attend(b, start, keys)
        if isinstance(b, int):
            if b == lag - 1:
                outer.arrived(0)
                outer.lay(0, wo_all, pl.ds(0, width))
            if b >= lag - 1:
                one.relay(b - lag + 1)
            if b >= lag:
                mlp_and_send(b - lag)
        else:
            one.relay(b - lag + 1)
            mlp_and_send(b - lag)

    every_block(forward, False)

    def forward_last(i, _):
        b = blocks - lag + i

        @pl.when(i < lag - 1)
        def _():
            one.relay(b + 1)

        mlp_and_send(b)
        return 0

    lax.fori_loop(0, lag, forward_last, 0)
    for b in reversed(range(turned_from, blocks)):
        three.add(b)
        three.cross(b)

    def mlp_out(i, _):
        rows = wide_rows(i)
        out_ref[rows] = dot(s_ref[rows], w2_ref[...], NT).astype(BF16)
        return 0

    lax.fori_loop(0, length // wide, mlp_out, 0)
    mat_ref[:, cuts[3] : cuts[4]] = dot(dy_ref[...], s_ref[...], TN).astype(BF16)
    mat_ref[:, cuts[1] : cuts[2]] = dot(cn_ref[...], du_ref[...], TN).astype(BF16)
    mat_ref[:, cuts[4] :] = jnp.zeros((width, mat_ref.shape[1] - cuts[4]), BF16)

    for early in range(turned_from):
        three.relay(early)
    three.relay(blocks - 1)
    ng_ref[...] = jnp.zeros_like(ng_ref)
    carry_ref[...] = jnp.zeros_like(carry_ref)
    dkv_ref[...] = jnp.zeros_like(dkv_ref)

    def back(b, start, keys):
        def ahead():
            three.relay(b - 1)

        if not isinstance(b, int):
            pl.when(b > turned_from)(ahead)
        elif b > turned_from:
            ahead()
        three.arrived(b)
        rows, window = rows_of(b), pl.ds(start, keys)
        plain, inverse_std = plain_norm(resid_ref[rows])
        d_two = three.sums(b)
        ng_ref[0:1, :] += jnp.sum(d_two * plain, axis=0, keepdims=True)
        ng_ref[1:2, :] += jnp.sum(d_two, axis=0, keepdims=True)
        dres = dy_ref[rows].astype(F32) + norm_back(plain, inverse_std, d_two * gain_two)
        dhb = dres.astype(BF16)
        dhb_ref[rows] = dhb
        do = dot(dhb, wo_ref[...], NN).astype(BF16)
        do = [do[:, h * HD : (h + 1) * HD] for h in range(heads)]
        for h in range(heads):
            raw_scr[h, :, :keys] = dot(qkv_ref[h, rows], qkv_ref[heads + h, window], NT)
            back_scr[h, :, :keys] = dot(do[h], qkv_ref[2 * heads + h, window], NT)

        def harden(part, whole, base):
            penalty = pen_ref[whole, :keys].astype(F32)
            total = None
            for h in range(heads):
                probs = jnp.exp(raw_scr[h, part, :keys] - penalty - lse_ref[whole, h : h + 1])
                dprobs = back_scr[h, part, :keys]
                inner = jnp.sum(dprobs * probs, axis=-1, keepdims=True)
                dlogits = probs * (dprobs - inner)
                probs_scr[h, part, :keys] = probs.astype(BF16)
                draw_scr[h, part, :keys] = dlogits.astype(BF16)
                total = dlogits if total is None else total + dlogits
            two_part(total, part, keys)

        by_rows(b, harden)
        raw_scr[heads, :, :keys] = dot(later, pick_scr[:, :keys], NN)
        after = carry_ref[0:1, window]
        top = [pick_scr[start_ : start_ + few, :keys].astype(F32)[:1] for start_ in (0, BLK)]
        carry_ref[0:1, window] = after + raw_scr[heads, 0:1, :keys] + (top[0] + top[1])

        def select(part, whole, base):
            suffix = raw_scr[heads, part, :keys] + after
            draw_scr[heads, part, :keys] = (sig_ref[whole, :keys].astype(F32) * -suffix).astype(BF16)

        by_rows(b, select)
        dq = []
        for h in range(heads):
            draw = draw_scr[h, :, :keys]
            dq.append(dot(draw, qkv_ref[heads + h, window], NN) * 0.125)
            dkv_ref[h * HD : (h + 1) * HD, window] += dot(qkv_ref[h, rows], draw, TN)
            dkv_ref[attn + h * HD : attn + (h + 1) * HD, window] += dot(do[h], probs_scr[h, :, :keys], TN)
        draw = draw_scr[heads, :, :keys]
        dq.append(dot(draw, qkv_ref[3 * heads + 1, window], NN) * 0.125)
        dkv_ref[2 * attn : 2 * attn + HD, window] += dot(qkv_ref[3 * heads, rows], draw, TN)
        dproj_ref[rows, :attn] = jnp.concatenate(dq[:heads], axis=1).astype(BF16)
        dproj_ref[rows, 3 * attn : 3 * attn + HD] = dq[heads].astype(BF16)

    every_block(back, True)
    dproj_ref[:, 3 * attn + HD : 3 * attn + 2 * HD] = dkv_ref[2 * attn :].T.astype(BF16)

    def collect(src, dst, where, i):
        return remote(src, dst, collect_sem.at[i], collect_sem.at[i + 2], where)

    gf_ref[...] = dot(a_ref[...], dproj_ref[:, 3 * attn :], TN).astype(BF16)

    @pl.when(core == 1)
    def _():
        collect(gf_ref, gf_near, beside, 0).start()

    @pl.when(core == 0)
    def _():
        collect(gf_ref, gf_near, beside, 0).wait_recv()
        gf_ref[...] = (gf_ref[...].astype(F32) + gf_near[...].astype(F32)).astype(BF16)

    @pl.when(t == 2)
    def _():
        collect(gf_ref, gf_far, over, 1).start()

    dproj_ref[:, attn : 3 * attn] = dkv_ref[: 2 * attn].T.astype(BF16)
    mat_ref[:, cuts[2] : cuts[3]] = dot(dhb_ref[...], o_ref[...], TN).astype(BF16)
    grad = dot(a_ref[...], dproj_ref[:, : 3 * attn], TN)
    mat_ref[:, : cuts[1]] = grad.astype(BF16)

    @pl.when(t == 0)
    def _():
        collect(gf_ref, gf_far, over, 1).wait_recv()
        extra = gf_ref[...].astype(F32) + gf_far[...].astype(F32)
        mat_ref[:, :HD] = (mat_ref[:, :HD].astype(F32) + extra[:, :HD]).astype(BF16)
        mat_ref[:, attn : attn + HD] = (mat_ref[:, attn : attn + HD].astype(F32) + extra[:, HD:]).astype(BF16)
        give(over, 0).wait_send()

    @pl.when(core == 0)
    def _():
        give(beside, 1).wait_send()

    @pl.when(core == 1)
    def _():
        collect(gf_ref, gf_near, beside, 0).wait_send()

    @pl.when(t == 2)
    def _():
        collect(gf_ref, gf_far, over, 1).wait_send()

    def close(b, _):
        one.close(b)
        three.close(b)
        return 0

    lax.fori_loop(0, blocks, close, 0)
    outer.close(0)


def layer(inputs, segments, cotangent, wp, w1, wo, w2, norms, block):
    length, width = inputs.shape
    attn, hidden = wo.shape[1], w1.shape[1]
    heads = attn // HD
    rows, cols = width // block, 4 * attn // block + 2 * (hidden // block)
    cuts = piece_cuts(rows, cols, width // attn)
    blocks = length // BLK
    span = min(length // 2 + BLK, length)

    def low(*shape):
        return pltpu.VMEM(shape, BF16)

    half = length // 2
    total = [low(length, width)] + [low(half, width)] * 5 + [pltpu.SemaphoreType.DMA((8, blocks))]

    def out(shape, dtype):
        return jax.ShapeDtypeStruct(shape, dtype)

    return pl.pallas_call(
        functools.partial(layer_kernel, heads, shift_for(length), [cut * block for cut in cuts]),
        out_shape=[
            out((width, cols * block + 128), BF16),
            out((length, width), BF16),
            out((length, 3 * attn + 2 * HD), BF16),
            out((width, 2 * HD), BF16),
            out((length, width), BF16),
            out((length, width), F32),
            out((2, width), F32),
        ],
        in_specs=[VM] * 8,
        out_specs=[VM] * 7,
        scratch_shapes=[
            low(length, width),
            low(width, 2 * HD),
            low(3 * heads + 2, length, HD),
            low(length, span),
            low(length, span),
            pltpu.VMEM((length, 8), F32),
            low(length, attn),
            low(length, width),
            low(length, hidden),
            low(length, hidden),
            pltpu.VMEM((2 * attn + HD, length), F32),
            pltpu.VMEM((8, length), F32),
            pltpu.VMEM((heads + 1, BLK, span), F32),
            pltpu.VMEM((heads, BLK, span), F32),
            low(heads, BLK, span),
            low(heads + 1, BLK, span),
            low(2 * BLK, span),
        ]
        + [low(blocks, attn, BLK)] * 4
        + [pltpu.SemaphoreType.DMA((6, blocks)), low(BLK, width)]
        + [low(1, width + width // 2, BLK)] * 4
        + [pltpu.SemaphoreType.DMA((6, 1)), low(width, width)]
        + total
        + [low(width, 2 * HD)] * 3
        + [pltpu.SemaphoreType.DMA((3,)), pltpu.SemaphoreType.DMA((4,))]
        + [pltpu.VMEM((1, length), F32), pltpu.VMEM((length, 1), F32)],
        compiler_params=pltpu.CompilerParams(
            collective_id=3, has_side_effects=True, vmem_limit_bytes=LAYER_LIMIT
        ),
        name="layer",
        cost_estimate=pl.CostEstimate(flops=0, bytes_accessed=221000000, transcendentals=0),
    )(
        inputs,
        segments.reshape(1, length),
        cotangent,
        wp,
        w1,
        wo,
        w2,
        norms,
    )


def settle_kernel(
    n,
    count,
    inverse_ref,
    mat_ref,
    out_in,
    dproj_ref,
    wp_ref,
    wf_ref,
    dhb_ref,
    resid_ref,
    x_ref,
    norm_ref,
    ng_in,
    g_ref,
    output_ref,
    grad_ref,
    ng_ref,
    p_ref,
    u_scr,
    xin,
    lin,
    rin,
    x_send,
    x_recv,
    l_send,
    l_recv,
    r_send,
    r_recv,
    near4,
    mine4,
    far4,
    near_mine4,
    near_far4,
    sem4,
    near2,
    mine2,
    far2,
    near_mine2,
    near_far2,
    sem2,
    norm_held,
    norm_send,
    norm_recv,
    da_scr,
):
    m = n // 2
    dp, t = lax.axis_index("dp"), lax.axis_index("tensor")
    place, side = dp // 2, lax.rem(dp, 2)
    pair = (place * 2 + 1 - side, t)
    four = Total(dp, t, da_scr, near4, mine4, far4, near_mine4, near_far4, sem4)
    two = Total(dp, t, out_in, near2, mine2, far2, near_mine2, near_far2, sem2)
    blocks = four.blocks
    peers = [lax.rem(dp + hop, n) for hop in range(1, n)]
    size, wide = p_ref.shape[1:]
    cols = (mat_ref.shape[1] - 128) // size

    def chop(row, _):
        whole_row = mat_ref[pl.ds(pl.multiple_of(row * size, size), size), :]
        for c in range(cols):
            u_scr[row * cols + c] = whole_row[:, c * size : (c + 1) * size]
        return 0

    lax.fori_loop(0, mat_ref.shape[0] // size, chop, 0)
    greet([four.beside, four.over] + [(peer, t) for peer in peers])

    middle = wide // 256 * 128
    parts = ((0, middle), (middle, wide))

    def piece(ref, part):
        first, last = parts[part]
        return ref.at[:, first:last]

    def across(q, part):
        src, dst = p_ref.at[q * 2 + 1 - side], xin.at[q]
        return remote(piece(src, part), piece(dst, part), x_send.at[q, part], x_recv.at[q, part], pair)

    def rightward(q, part):
        ref = piece(lin.at[q], part)
        return remote(ref, ref, r_send.at[q, part], l_recv.at[q, part], (dp + 2, t))

    def leftward(q, part):
        ref = piece(rin.at[q], part)
        return remote(ref, ref, l_send.at[q, part], r_recv.at[q, part], (dp - 2, t))

    def both(hop, one):
        @pl.when(place + hop < m)
        def _():
            one(place + hop, True)

        if hop > 0:
            @pl.when(place - hop >= 0)
            def _():
                one(place - hop, False)

    def work(q, right):
        lay(q * 2 + side)
        for part in (0, 1):
            first, last = parts[part]
            across(q, part).wait_recv()
            own = p_ref[q * 2 + side, :, first:last].astype(F32) + xin[q, :, first:last].astype(F32)
            line, pass_on, is_end = (lin, rightward, place == 0) if right else (rin, leftward, place == m - 1)

            @pl.when(jnp.logical_not(is_end))
            def _():
                pass_on(q, part).wait_recv()
                line[q, :, first:last] = (own + line[q, :, first:last].astype(F32)).astype(BF16)

            @pl.when(is_end)
            def _():
                line[q, :, first:last] = own.astype(BF16)

            pass_on(q, part).start()

    def keep():
        q = place
        lay(q * 2 + side)
        for part in (0, 1):
            first, last = parts[part]
            across(q, part).wait_recv()
            g_ref[:, first:last] = p_ref[q * 2 + side, :, first:last].astype(F32) + xin[q, :, first:last].astype(F32)

            @pl.when(place > 0)
            def _():
                rightward(q, part).wait_recv()
                g_ref[:, first:last] += lin[q, :, first:last].astype(F32)

            @pl.when(place < m - 1)
            def _():
                leftward(q, part).wait_recv()
                g_ref[:, first:last] += rin[q, :, first:last].astype(F32)

    def norm_copy(peer):
        return remote(ng_ref, norm_held.at[dp], norm_send.at[peer], norm_recv.at[dp], (peer, t))

    def norm_from(peer):
        return remote(ng_ref, norm_held.at[peer], norm_send.at[peer], norm_recv.at[peer], (peer, t))

    some = math.gcd(count, 8)
    room = tiles_up(some * size) // 128

    def strip(base):
        return jnp.concatenate([u_scr[inverse_ref[base + e]] for e in range(some)], axis=1)

    def lay(d):
        if some * size == room * 128:
            def one(g, _):
                place = pl.ds(pl.multiple_of(g * room * 128, 128), room * 128)
                p_ref[d, :, place] = strip(d * count + g * some)
                return 0

            lax.fori_loop(0, count // some, one, 0, unroll=3)
        else:
            parts = [strip(d * count + g * some)[:, : some * size] for g in range(count // some)]
            if wide > count * size:
                parts.append(jnp.zeros((size, wide - count * size), BF16))
            p_ref[d] = jnp.concatenate(parts, axis=1)

    def give(q, right):
        lay(q * 2 + 1 - side)
        across(q, 0).start()
        across(q, 1).start()

    cut = wp_ref.shape[1]

    def project_back(b):
        rows = pl.ds(b * four.size, four.size)
        da = dot(dproj_ref[rows, :cut], wp_ref[...], NT)
        da_scr[rows] = (da + dot(dproj_ref[rows, cut:], wf_ref[...], NT)).astype(BF16)
        four.enter(b)

    for step, hop in enumerate(reversed(range(m))):
        both(hop, give)
        if step == 0:
            for b in range(blocks):
                project_back(b)
        if step == 1:
            for b in range(blocks):
                four.add(b)
                four.cross(b)
                two.enter(b)
    for b in range(blocks):
        two.add(b)
        two.cross(b)

    ng_ref[...] = jnp.zeros_like(ng_ref)
    gain = norm_ref[0:1, :]

    def rows_of(b):
        return pl.ds(b * four.size, four.size)

    def grad_block(b):
        rows = rows_of(b)
        four.arrived(b)
        d_one = four.sums(b)
        plain, inverse_std = plain_norm(x_ref[rows].astype(F32))
        ng_ref[0:1, :] += jnp.sum(d_one * plain, axis=0, keepdims=True)
        ng_ref[1:2, :] += jnp.sum(d_one, axis=0, keepdims=True)
        grad_ref[rows] = dhb_ref[rows].astype(F32) + norm_back(plain, inverse_std, d_one * gain)

    def out_block(b):
        rows = rows_of(b)
        two.arrived(b)
        output_ref[rows] = (resid_ref[rows] + two.sums(b)).astype(BF16)

    def norms_out():
        ng_ref[2:4, :] = ng_in[...]
        for peer in peers:
            norm_copy(peer).start()

    def norms_in():
        for peer in peers:
            norm_from(peer).wait_recv()
        total = None
        for source in range(n):
            term = jnp.where(dp == source, ng_ref[...], norm_held[source])
            total = term if total is None else total + term
        for peer in peers:
            norm_copy(peer).wait_send()
        ng_ref[...] = total

    tasks = []
    for b in range(blocks):
        tasks.append(functools.partial(four.relay, b))
        if b > 0:
            tasks.append(functools.partial(grad_block, b - 1))
    tasks.append(functools.partial(grad_block, blocks - 1))
    tasks.append(norms_out)
    for b in range(blocks):
        tasks.append(functools.partial(two.relay, b))
        if b > 0:
            tasks.append(functools.partial(out_block, b - 1))
    tasks.append(functools.partial(out_block, blocks - 1))
    done = 0
    for step, hop in enumerate(reversed(range(1, m))):
        until = min((1, 10, 18, len(tasks))[min(step, 3)], len(tasks))
        while done < until:
            tasks[done]()
            done += 1
        both(hop, work)
    while done < len(tasks):
        tasks[done]()
        done += 1
    keep()
    norms_in()

    def finish(q, _):
        for part in (0, 1):
            across(q, part).wait_send()

            @pl.when(q > place)
            def _():
                rightward(q, part).wait_send()

            @pl.when(q < place)
            def _():
                leftward(q, part).wait_send()

        return 0

    lax.fori_loop(0, m, finish, 0)
    for b in range(blocks):
        four.close(b)
        two.close(b)


def settle(inverse, matrix, block, out_part, dproj, wp, wf, dhb, resid, inputs, norms, ng, n):
    count = matrix.shape[0] // block * ((matrix.shape[1] - 128) // block) // n
    wide = tiles_up(count * block)
    m = n // 2
    length, width = inputs.shape
    blocks = 8

    def low(*shape):
        return pltpu.VMEM(shape, BF16)

    half = length // 2
    total = [low(half, width)] * 5 + [pltpu.SemaphoreType.DMA((8, blocks))]
    return pl.pallas_call(
        functools.partial(settle_kernel, n, count),
        out_shape=[
            jax.ShapeDtypeStruct((block, wide), F32),
            jax.ShapeDtypeStruct((length, width), BF16),
            jax.ShapeDtypeStruct((length, width), F32),
            jax.ShapeDtypeStruct((4, width), F32),
        ],
        in_specs=[pl.BlockSpec(memory_space=pltpu.SMEM)] + [VM] * 10,
        out_specs=[VM] * 4,
        scratch_shapes=[low(n, block, wide), low(n * count, block, block)]
        + [low(m, block, wide)] * 3
        + [pltpu.SemaphoreType.DMA((m, 2))] * 6
        + total
        + total
        + [pltpu.VMEM((n, 4, width), F32), pltpu.SemaphoreType.DMA((n,)), pltpu.SemaphoreType.DMA((n,))]
        + [low(length, width)],
        compiler_params=pltpu.CompilerParams(
            collective_id=2, has_side_effects=True, vmem_limit_bytes=SETTLE_LIMIT
        ),
        name="settle",
        cost_estimate=pl.CostEstimate(flops=0, bytes_accessed=187000000, transcendentals=0),
    )(inverse, matrix, out_part, dproj, wp, wf, dhb, resid, inputs, norms, ng)


def norm_update(grad, master, first, second):
    new_first = beta_one * first + (1.0 - beta_one) * grad
    new_second = beta_two * second + (1.0 - beta_two) * grad * grad
    direction = (
        new_first
        / (1.0 - beta_one**STEP)
        / (jnp.sqrt(new_second / (1.0 - beta_two**STEP)) + adam_eps)
    )
    return (new_first, new_second, master - norm_rate * direction)


def body(
    inputs,
    segments,
    cotangent,
    owner,
    masters,
    first_moment,
    second_moment,
    left_stats,
    right_stats,
    left_basis,
    right_basis,
    norm_master,
    norm_first,
    norm_second,
):
    length = inputs.shape[1]
    width = inputs.shape[2]
    n_dp = lax.axis_size("dp")
    parts = lax.axis_size("tensor")
    per_dev = masters.shape[1]
    block = masters.shape[-1]
    slots, inverse = lax.optimization_barrier(block_slots(owner, per_dev))
    pieces, norms = gather_masters(
        slots, masters[0], norm_master, n_dp, width // block, parts
    )
    grad_matrix, out_part, dproj, w_first, dhb, resid, norm_grads = layer(
        inputs[0], segments[0], cotangent[0], *pieces, norms, block
    )
    own_packed, output, input_grad, norm_grads = settle(
        inverse,
        grad_matrix,
        block,
        out_part,
        dproj,
        pieces[0],
        w_first,
        dhb,
        resid,
        inputs[0],
        norms,
        norm_grads,
        n_dp,
    )
    *updated, output, input_grad = soap(
        own_packed,
        output,
        input_grad,
        masters[0],
        first_moment[0],
        second_moment[0],
        left_stats[0],
        right_stats[0],
        left_basis[0],
        right_basis[0],
    )
    norm_grads, output = lax.optimization_barrier((norm_grads, output))
    norm_per = norm_master.shape[0]
    own_norm_grads = lax.dynamic_slice_in_dim(
        norm_grads.reshape(-1), lax.axis_index("dp") * norm_per, norm_per
    )
    norm_first_new, norm_second_new, norm_new = norm_update(
        own_norm_grads, norm_master, norm_first, norm_second
    )
    return (
        output[None],
        input_grad[None],
        *[item[None] for item in updated],
        norm_first_new,
        norm_second_new,
        norm_new,
    )


def solution(mesh):
    in_specs = (
        P("dp", None, None),
        P("dp", None),
        P("dp", None, None),
        P(),
        P("tensor", "dp", None, None),
        P("tensor", "dp", None, None),
        P("tensor", "dp", None, None),
        P("tensor", "dp", None, None),
        P("tensor", "dp", None, None),
        P("tensor", "dp", None, None),
        P("tensor", "dp", None, None),
        P("dp"),
        P("dp"),
        P("dp"),
    )
    out_specs = (
        P("dp", None, None),
        P("dp", None, None),
        P("tensor", "dp", None, None),
        P("tensor", "dp", None, None),
        P("tensor", "dp", None, None),
        P("tensor", "dp", None, None),
        P("tensor", "dp", None, None),
        P("tensor", "dp", None, None),
        P("tensor", "dp", None, None),
        P("dp"),
        P("dp"),
        P("dp"),
    )
    return jax.shard_map(body, mesh=mesh, in_specs=in_specs, out_specs=out_specs, check_vma=False)
```

```python
import functools
import math

import jax
import jax.numpy as jnp
from jax import lax
from jax.experimental import pallas as pl
from jax.experimental.pallas import tpu as pltpu
from jax.sharding import PartitionSpec as P

HD = 64
STEP = 10
F32 = jnp.float32
BF16 = jnp.bfloat16
LAYER_LIMIT = 35 * 2**20
GATHER_LIMIT = 35 * 2**20
SETTLE_LIMIT = 31 * 2**20

norm_eps = 1e-05
beta_one = 0.9
beta_two = 0.95
beta_stats = 0.95
learn_rate = 0.03
norm_rate = 0.4
weight_decay = 0.01
adam_eps = 1e-08


def shift_for(length):
    return math.log(length / 8.0)


def block_slots(owner):
    count = owner.shape[0]
    index = jnp.arange(count, dtype=jnp.int32)
    earlier = (owner[:, None] == owner[None, :]) & (index[None, :] < index[:, None])
    lower = owner[None, :] < owner[:, None]
    slots = jnp.sum((earlier | lower).astype(jnp.int32), axis=1)
    inverse = jnp.sum(jnp.where(slots[None, :] == index[:, None], index[None, :], 0), axis=1)
    return (slots, inverse)


def norm_back(plain, inverse_std, grad):
    return inverse_std * (
        grad
        - jnp.mean(grad, axis=-1, keepdims=True)
        - plain * jnp.mean(grad * plain, axis=-1, keepdims=True)
    )


def piece_cuts(rows, cols, parts):
    attn = rows // parts
    hidden = (cols - 4 * attn) // 2
    return (0, 3 * attn, 3 * attn + hidden, 4 * attn + hidden, cols)


MESH = pl.DeviceIdType.MESH
VM = pl.BlockSpec(memory_space=pltpu.VMEM)
MIB = 2**20


def tiles_up(value):
    return -(-value // 128) * 128


def remote(src, dst, send, recv, where):
    return pltpu.make_async_remote_copy(
        src_ref=src, dst_ref=dst, send_sem=send, recv_sem=recv, device_id=where, device_id_type=MESH
    )


def greet(devices):
    barrier = pltpu.get_barrier_semaphore()
    for device in devices:
        pl.semaphore_signal(barrier, inc=1, device_id=device, device_id_type=MESH)
    pl.semaphore_wait(barrier, len(devices))


def line_greet(dp, t, m):
    place, side = dp // 2, lax.rem(dp, 2)
    barrier = pltpu.get_barrier_semaphore()
    pl.semaphore_signal(barrier, inc=1, device_id=(place * 2 + 1 - side, t), device_id_type=MESH)

    @pl.when(place > 0)
    def _():
        pl.semaphore_signal(barrier, inc=1, device_id=(dp - 2, t), device_id_type=MESH)

    @pl.when(place < m - 1)
    def _():
        pl.semaphore_signal(barrier, inc=1, device_id=(dp + 2, t), device_id_type=MESH)

    ends = (place == 0).astype(jnp.int32) + (place == m - 1).astype(jnp.int32)
    pl.semaphore_wait(barrier, 3 - ends)


def gather_kernel(
    n, count, block, wide, norm_rows, norm_per, rows, cuts, slot_ref, m_ref, norm_ref, *refs
):
    w_refs, (nout_ref, u_ref, held, send_sem, recv_sem, side_send, side_recv) = refs[:4], refs[4:]
    m = n // 2
    dp, t = lax.axis_index("dp"), lax.axis_index("tensor")
    place, side = dp // 2, lax.rem(dp, 2)
    pair = (place * 2 + 1 - side, t)
    for k in range(count):
        held[dp, :, k * block : (k + 1) * block] = m_ref[k].astype(BF16)
    if wide > count * block:
        held[dp, :, count * block : wide] = jnp.zeros((block, wide - count * block), BF16)
    held[dp, :, wide : wide + 128] = jnp.concatenate(
        [norm_ref[...], jnp.zeros((block - norm_rows, 128), F32)], axis=0
    ).astype(BF16)
    line_greet(dp, t, m)

    total = wide + 128
    less = total // 128 // 6 * 128

    middle = less + (total - less) // 256 * 128
    parts = ((less, middle), (middle, total))

    def send(source, way, where, part):
        first, last = parts[part]
        columns = held.at[source, :, first:last]
        return remote(columns, columns, send_sem.at[source, way, part], recv_sem.at[source, part], where)

    def side_send_to(source, way, where):
        part = held.at[source, :, :less]
        return remote(part, part, side_send.at[source, way], side_recv.at[source], where)

    def side_spread(source, left, right):
        @pl.when(left)
        def _():
            side_send_to(source, 0, (dp - 2, t)).start()

        @pl.when(right)
        def _():
            side_send_to(source, 1, (dp + 2, t)).start()

    def unpack(source):
        for k in range(count):
            u_ref[source * count + k] = held[source, :, k * block : (k + 1) * block]

    def spread(source, left, right, part):
        @pl.when(left)
        def _():
            send(source, 0, (dp - 2, t), part).start()

        @pl.when(right)
        def _():
            send(source, 1, (dp + 2, t), part).start()

        send(source, 2, pair, part).start()

    def spread_done(source, left, right):
        for part in (0, 1):
            send(source, 2, pair, part).wait_send()

            @pl.when(left)
            def _():
                send(source, 0, (dp - 2, t), part).wait_send()

            @pl.when(right)
            def _():
                send(source, 1, (dp + 2, t), part).wait_send()

    side_send_to(dp, 2, pair).start()
    side_spread(dp, place > 0, place < m - 1)
    for part in (0, 1):
        spread(dp, place > 0, place < m - 1, part)
    beside = place * 2 + 1 - side
    side_send_to(beside, 2, pair).wait_recv()
    side_spread(beside, place > 0, place < m - 1)
    unpack(dp)

    def one(hop, _):
        for part in (0, 1):
            @pl.when(place - hop >= 0)
            def _():
                source = dp - 2 * hop
                send(source, 2, pair, part).wait_recv()
                spread(source, False, place < m - 1, part)

            @pl.when(place + hop < m)
            def _():
                source = dp + 2 * hop
                send(source, 2, pair, part).wait_recv()
                spread(source, place > 0, False, part)

        @pl.when(place - hop >= 0)
        def _():
            for s in (0, 1):
                both = (place - hop) * 2 + s
                side_send_to(both, 2, pair).wait_recv()
                side_spread(both, False, place < m - 1)
            unpack(dp - 2 * hop)

        @pl.when(place + hop < m)
        def _():
            for s in (0, 1):
                both = (place + hop) * 2 + s
                side_send_to(both, 2, pair).wait_recv()
                side_spread(both, place > 0, False)
            unpack(dp + 2 * hop)

        return 0

    lax.fori_loop(1, m, one, 0)

    def other(step, _):
        source = step * 2 + 1 - side
        for part in (0, 1):
            send(source, 2, pair, part).wait_recv()
        unpack(source)
        return 0

    lax.fori_loop(0, m, other, 0)

    def strip(row, _):
        for first, last, w_ref in zip(cuts, cuts[1:], w_refs):
            w_ref[pl.ds(pl.multiple_of(row * block, block), block), :] = jnp.concatenate(
                [u_ref[slot_ref[row * cuts[-1] + c]] for c in range(first, last)], axis=1
            )
        return 0

    lax.fori_loop(0, rows, strip, 0, unroll=2)

    line = nout_ref.shape[1]
    for source in range(n):
        values = held[source, :16, wide : wide + 128].astype(F32)
        for r in range(norm_rows):
            spot = source * norm_per + r * 128
            size = min(128, norm_per - r * 128)
            nout_ref[spot // line : spot // line + 1, spot % line : spot % line + size] = values[
                r : r + 1, :size
            ]

    def finish(step, _):
        source = step * 2 + side
        spread_done(
            source,
            (place > 0) & (step >= place),
            (place < m - 1) & (step <= place),
        )
        for s in (0, 1):
            both = step * 2 + s

            @pl.when((place > 0) & (step >= place))
            def _():
                side_send_to(both, 0, (dp - 2, t)).wait_send()

            @pl.when((place < m - 1) & (step <= place))
            def _():
                side_send_to(both, 1, (dp + 2, t)).wait_send()

        return 0

    lax.fori_loop(0, m, finish, 0)
    side_send_to(dp, 2, pair).wait_send()


def gather_masters(slots, masters, norm, n, rows, parts):
    count, block = masters.shape[0], masters.shape[-1]
    wide = tiles_up(count * block)
    norm_rows = -(-norm.shape[0] // 128)
    norm_tile = jnp.pad(norm, (0, norm_rows * 128 - norm.shape[0])).reshape(norm_rows, 128)
    cuts = piece_cuts(rows, n * count // rows, parts)
    *pieces, norms = pl.pallas_call(
        functools.partial(gather_kernel, n, count, block, wide, norm_rows, norm.shape[0], rows, cuts),
        out_shape=[
            jax.ShapeDtypeStruct((rows * block, (last - first) * block), BF16)
            for first, last in zip(cuts, cuts[1:])
        ]
        + [jax.ShapeDtypeStruct((4, n * norm.shape[0] // 4), F32)],
        in_specs=[pl.BlockSpec(memory_space=pltpu.SMEM), VM, VM],
        out_specs=[VM] * 5,
        scratch_shapes=[
            pltpu.VMEM((n * count, block, block), BF16),
            pltpu.VMEM((n, block, wide + 128), BF16),
            pltpu.SemaphoreType.DMA((n, 3, 2)),
            pltpu.SemaphoreType.DMA((n, 2)),
            pltpu.SemaphoreType.DMA((n, 3)),
            pltpu.SemaphoreType.DMA((n,)),
        ],
        compiler_params=pltpu.CompilerParams(
            collective_id=1, has_side_effects=True, vmem_limit_bytes=GATHER_LIMIT
        ),
        name="gather_masters",
        cost_estimate=pl.CostEstimate(flops=0, bytes_accessed=163200000, transcendentals=0),
    )(slots, masters, norm_tile)
    return pieces, norms


NN = ((1,), (0,))
NT = ((1,), (1,))
TN = ((0,), (0,))


def lane_prod(n, lanes, left_row, right_tile, put, group=4):
    tiles = n // 8

    def some(step, _):
        base = step * group

        def one(k, acc):
            rights = [right_tile(k, j) for j in range(tiles)]
            out = []
            for r in range(group):
                row = jnp.broadcast_to(left_row(base + r, k), (8, lanes))
                out.append(tuple(acc[r][j] + row * rights[j] for j in range(tiles)))
            return tuple(out)

        zero = tuple(tuple(jnp.zeros((8, lanes), F32) for _ in range(tiles)) for _ in range(group))
        acc = lax.fori_loop(0, n, one, zero, unroll=8)
        for r in range(group):
            for j in range(tiles):
                put(base + r, j, acc[r][j])
        return 0

    lax.fori_loop(0, n // group, some, 0)


def lane_gram(n, lanes, row, tile, put, put_turned):
    tiles = n // 8
    for first in range(tiles):
        columns = range(first, tiles)

        def some(step, _):
            base = first * 8 + step * 4

            def one(k, acc):
                rights = [tile(k, j) for j in columns]
                out = []
                for r in range(4):
                    left = jnp.broadcast_to(row(base + r, k), (8, lanes))
                    out.append(tuple(a + left * right for a, right in zip(acc[r], rights)))
                return tuple(out)

            zero = tuple(tuple(jnp.zeros((8, lanes), F32) for _ in columns) for _ in range(4))
            acc = lax.fori_loop(0, n, one, zero, unroll=8)
            for r in range(4):
                for j in columns:
                    put(base + r, j, acc[r][j - first])
                    if j > first:
                        put_turned(base + r, j, acc[r][j - first])
            return 0

        lax.fori_loop(0, 2, some, 0)


def soap_kernel(
    n,
    count,
    packed_ref,
    y_ref,
    dx_ref,
    m_ref,
    f_ref,
    s_ref,
    l_ref,
    r_ref,
    ql_ref,
    qr_ref,
    nf_out,
    ns_out,
    nm_out,
    nl_out,
    nr_out,
    bl_out,
    br_out,
    y_out,
    dx_out,
    nf_ref,
    ns_ref,
    nm_ref,
    nl_ref,
    nr_ref,
    basis_ref,
    u_scr,
    g_ref,
    gt_ref,
    qt_ref,
    h_ref,
    d_ref,
    sems,
):
    tiles = n // 8

    def at(ref):
        def row(i, k):
            return ref[pl.ds(i * n + k, 1), :]

        return row

    def at_turned(ref):
        def row(i, k):
            return ref[pl.ds(k * n + i, 1), :]

        return row

    def tile(ref):
        def one(k, j):
            return ref[pl.ds(pl.multiple_of(k * n + 8 * j, 8), 8), :]

        return one

    def turned(i, j):
        return pl.ds(8 * j * n + i, 8, stride=n)

    def turn_into(dst, src):
        def one(k, _):
            for j in range(tiles):
                dst[here(k, j), :] = src[turned(k, j), :]
            return 0

        lax.fori_loop(0, n, one, 0, unroll=4)

    def here(i, j):
        return pl.ds(pl.multiple_of(i * n + 8 * j, 8), 8)

    def send(place, src, dst):
        return pltpu.make_async_copy(src, dst, sems.at[place])

    send(7, y_ref, y_out).start()
    send(8, dx_ref, dx_out).start()
    for c in range(count):
        u_scr[c] = packed_ref[:, c * n : (c + 1) * n]

    def turn(i, _):
        slab = u_scr[:, pl.ds(i, 1), :].reshape(count, n)
        g_ref[pl.ds(pl.multiple_of(i * n, 8), n), :] = slab.T
        return 0

    lax.fori_loop(0, n, turn, 0, unroll=4)

    turn_into(gt_ref, g_ref)
    turn_into(qt_ref, qr_ref)

    def blend(dst, old):
        def put(i, j, value):
            where = here(i, j)
            dst[where, :] = beta_stats * old[where, :] + (1.0 - beta_stats) * value

        def put_turned(i, j, value):
            where = turned(i, j)
            dst[where, :] = beta_stats * old[where, :] + (1.0 - beta_stats) * value

        return put, put_turned

    def store(ref, base=0):
        def put(i, j, value):
            ref[pl.ds(pl.multiple_of(base + i * n + 8 * j, 8), 8), :] = value

        return put

    lane_gram(n, count, at_turned(gt_ref), tile(gt_ref), *blend(nl_ref, l_ref))
    send(3, nl_ref, nl_out).start()
    lane_gram(n, count, at_turned(g_ref), tile(g_ref), *blend(nr_ref, r_ref))
    send(4, nr_ref, nr_out).start()
    lane_prod(n, count, at(nl_ref), tile(ql_ref), store(basis_ref))
    lane_prod(n, count, at(nr_ref), tile(qr_ref), store(basis_ref, n * n))

    sub = lax.broadcasted_iota(jnp.int32, (8, count), 0)
    for panel in range(tiles):
        def side(s, _):
            base = pl.multiple_of(s * n * n, 8)

            def spot(i, j):
                return pl.ds(pl.multiple_of(base + i * n + 8 * j, 8), 8)

            rows = [basis_ref[spot(i, panel), :] for i in range(n)]
            sizes = jnp.ones((8, count), F32)
            for k in range(8):
                heads = [jnp.broadcast_to(row[k : k + 1], (8, count)) for row in rows]
                terms = [head * row for head, row in zip(heads, rows)]
                while len(terms) > 1:
                    terms = [sum(terms[p : p + 2][1:], terms[p]) for p in range(0, len(terms), 2)]
                size = jnp.broadcast_to(terms[0][k : k + 1], (8, count))
                sizes = jnp.where(sub == k, size, sizes)
                factor = jnp.where(sub > k, terms[0] * (1.0 / size), 0.0)
                rows = [row - head * factor for head, row in zip(heads, rows)]
            scale = lax.rsqrt(sizes)
            for i in range(n):
                basis_ref[spot(i, panel), :] = rows[i] * scale
            for start in range(panel + 1, tiles, 3):
                columns = range(start, min(start + 3, tiles))

                def heads_of(i):
                    return [
                        jnp.broadcast_to(basis_ref[pl.ds(base + i * n + 8 * panel + k, 1), :], (8, count))
                        for k in range(8)
                    ]

                def project(i, acc):
                    heads = heads_of(i)
                    values = [basis_ref[spot(i, j), :] for j in columns]
                    return tuple(
                        tuple(a + head * value for a, value in zip(acc[k], values))
                        for k, head in enumerate(heads)
                    )

                zero = tuple(tuple(jnp.zeros((8, count), F32) for _ in columns) for _ in range(8))
                parts = lax.fori_loop(0, n, project, zero, unroll=4)

                def take(i, _):
                    heads = heads_of(i)
                    for c, j in enumerate(columns):
                        value = basis_ref[spot(i, j), :]
                        for k in range(8):
                            value = value - heads[k] * parts[k][c]
                        basis_ref[spot(i, j), :] = value
                    return 0

                lax.fori_loop(0, n, take, 0, unroll=4)
            return 0

        lax.fori_loop(0, 2, side, 0)
    left_basis, right_basis = basis_ref.at[: n * n], basis_ref.at[n * n :]
    send(5, left_basis, bl_out).start()
    send(6, right_basis, br_out).start()

    def put_moments(i, j, rot):
        first = beta_one * f_ref[here(i, j), :] + (1.0 - beta_one) * rot
        second = beta_two * s_ref[here(i, j), :] + (1.0 - beta_two) * rot * rot
        nf_ref[here(i, j), :] = first
        ns_ref[here(i, j), :] = second
        d_ref[here(i, j), :] = first / (1.0 - beta_one**STEP) / (
            jnp.sqrt(second / (1.0 - beta_two**STEP)) + adam_eps
        )

    def put_master(i, j, moved):
        master = m_ref[here(i, j), :]
        nm_ref[here(i, j), :] = master - learn_rate * (moved + weight_decay * master)

    lane_prod(n, count, at_turned(ql_ref), tile(g_ref), store(h_ref))
    lane_prod(n, count, at(h_ref), tile(qr_ref), put_moments)
    send(0, nf_ref, nf_out).start()
    send(1, ns_ref, ns_out).start()
    lane_prod(n, count, at(ql_ref), tile(d_ref), store(h_ref))
    lane_prod(n, count, at(h_ref), tile(qt_ref), put_master)
    send(2, nm_ref, nm_out).start()
    sources = (nf_ref, ns_ref, nm_ref, nl_ref, nr_ref, left_basis, right_basis, y_ref, dx_ref)
    targets = (nf_out, ns_out, nm_out, nl_out, nr_out, bl_out, br_out, y_out, dx_out)
    for place, (src, dst) in enumerate(zip(sources, targets)):
        send(place, src, dst).wait()


def soap(packed, output, input_grad, *state):
    count, n = state[0].shape[0], state[0].shape[-1]
    flat = [item.transpose(1, 2, 0).reshape(n * n, count) for item in state]
    shape = jax.ShapeDtypeStruct((n * n, count), F32)
    room = pltpu.VMEM((n * n, count), F32)
    outs = pl.pallas_call(
        functools.partial(soap_kernel, n, count),
        out_shape=[shape] * 7 + [jax.ShapeDtypeStruct(item.shape, item.dtype) for item in (output, input_grad)],
        in_specs=[VM] * 10,
        out_specs=[pl.BlockSpec(memory_space=pl.ANY)] * 9,
        scratch_shapes=[room] * 5
        + [pltpu.VMEM((2 * n * n, count), F32), pltpu.VMEM((count, n, n), F32)]
        + [room] * 5
        + [pltpu.SemaphoreType.DMA((9,))],
        compiler_params=pltpu.CompilerParams(vmem_limit_bytes=31 * MIB),
        name="soap",
    )(packed, output, input_grad, *flat)
    return [item.reshape(n, n, count).transpose(2, 0, 1) for item in outs[:7]] + list(outs[7:])


BLK = 128


def plain_norm(rows):
    centered = rows - jnp.mean(rows, axis=-1, keepdims=True)
    inverse_std = lax.rsqrt(jnp.mean(centered * centered, axis=-1, keepdims=True) + norm_eps)
    return centered * inverse_std, inverse_std


def dot(left, right, dims):
    return lax.dot_general(left, right, (dims, ((), ())), preferred_element_type=F32)


class Total:
    def __init__(self, dp, t, x, near, mine, far, near_mine, near_far, sems):
        up, core = t // 2, lax.rem(t, 2)
        self.up, self.core = up, core
        self.beside = (dp, up * 2 + 1 - core)
        self.over = (dp, (1 - up) * 2 + core)
        self.x, self.near, self.mine, self.far = x, near, mine, far
        self.near_mine, self.near_far, self.sems = near_mine, near_far, sems
        self.blocks = sems.shape[1]
        self.size = x.shape[0] // self.blocks
        self.half = self.size // 2

    def rows(self, b, core):
        return pl.ds(pl.multiple_of(b * self.size + core * self.half, self.half), self.half)

    def part(self, b):
        return pl.ds(pl.multiple_of(b * self.half, self.half), self.half)

    def copy(self, kind, b):
        here = self.part(b)
        src, dst, where = (
            (self.x.at[self.rows(b, 1 - self.core)], self.near, self.beside),
            (self.mine.at[here], self.far, self.over),
            (self.mine.at[here], self.near_mine, self.beside),
            (self.far.at[here], self.near_far, self.beside),
        )[kind]
        return remote(src, dst.at[here], self.sems.at[2 * kind, b], self.sems.at[2 * kind + 1, b], where)

    def enter(self, b):
        self.copy(0, b).start()

    def add(self, b):
        here = self.part(b)
        self.copy(0, b).wait_recv()
        self.mine[here] = (self.x[self.rows(b, self.core)].astype(F32) + self.near[here].astype(F32)).astype(BF16)

    def cross(self, b):
        self.copy(1, b).start()
        self.copy(2, b).start()

    def relay(self, b):
        self.copy(1, b).wait_recv()
        self.copy(3, b).start()

    def arrived(self, b):
        self.copy(2, b).wait_recv()
        self.copy(3, b).wait_recv()

    def sums(self, b):
        here = self.part(b)
        own = self.mine[here].astype(F32) + self.far[here].astype(F32)
        other = self.near_mine[here].astype(F32) + self.near_far[here].astype(F32)
        low = self.core == 0
        return jnp.concatenate([jnp.where(low, own, other), jnp.where(low, other, own)], axis=0)

    def close(self, b):
        for kind in range(4):
            self.copy(kind, b).wait_send()


class Packs:
    def __init__(self, total, own, beside, over, far, sems):
        self.beside, self.over = total.beside, total.over
        self.up, self.core = total.up, total.core
        self.own, self.from_beside, self.from_over, self.from_far, self.sems = own, beside, over, far, sems

    def copy(self, kind, b):
        src, dst, where = (
            (self.own, self.from_beside, self.beside),
            (self.own, self.from_over, self.over),
            (self.from_over, self.from_far, self.beside),
        )[kind]
        return remote(src.at[b], dst.at[b], self.sems.at[2 * kind, b], self.sems.at[2 * kind + 1, b], where)

    def send(self, b):
        self.copy(1, b).start()
        self.copy(0, b).start()

    def relay(self, b):
        self.copy(1, b).wait_recv()
        self.copy(2, b).start()

    def arrived(self, b):
        self.copy(0, b).wait_recv()
        self.copy(2, b).wait_recv()

    def close(self, b):
        for kind in range(3):
            self.copy(kind, b).wait_send()

    def lay(self, b, dst, rows):
        tall = rows.size
        pairs = ((self.up, self.own, self.from_beside), (1 - self.up, self.from_over, self.from_far))
        for up, same, other in pairs:
            for core, ref in ((self.core, same), (1 - self.core, other)):
                dst[rows, pl.ds(pl.multiple_of((up * 2 + core) * 128, 128), 128)] = ref[b, :tall]
            first, second = same[b, tall:], other[b, tall:]
            low = self.core == 0
            zero = jnp.where(low, first.astype(F32), second.astype(F32)).astype(BF16)
            one = jnp.where(low, second.astype(F32), first.astype(F32)).astype(BF16)
            tail = jnp.concatenate(
                [
                    jnp.concatenate([zero[:, :HD], one[:, :HD]], axis=1),
                    jnp.concatenate([zero[:, HD:], one[:, HD:]], axis=1),
                ],
                axis=0,
            )
            dst[rows, pl.ds(pl.multiple_of(512 + up * 128, 128), 128)] = tail

    def pack(self, b, value):
        tall = value.shape[0]
        self.own[b, :tall] = value[:, :128]
        self.own[b, tall:] = jnp.concatenate([value[: tall // 2, 128:], value[tall // 2 :, 128:]], axis=1)


def layer_kernel(
    heads,
    shift,
    cuts,
    x_ref,
    seg_in,
    dy_ref,
    wp_ref,
    w1_ref,
    wo_ref,
    w2_ref,
    norm_ref,
    mat_ref,
    out_ref,
    dproj_ref,
    wf_out,
    dhb_ref,
    resid_ref,
    ng_ref,
    a_ref,
    wf_ref,
    qkv_ref,
    pen_ref,
    sig_ref,
    lse_ref,
    o_ref,
    cn_ref,
    s_ref,
    du_ref,
    dkv_ref,
    carry_ref,
    raw_scr,
    back_scr,
    probs_scr,
    draw_scr,
    pick_scr,
    o_own,
    o_beside,
    o_over,
    o_far,
    o_sem,
    o_all,
    wo_own,
    wo_beside,
    wo_over,
    wo_far,
    wo_sem,
    wo_all,
    x3_ref,
    near3,
    mine3,
    far3,
    near_mine3,
    near_far3,
    sem3,
    gf_ref,
    gf_near,
    gf_far,
    share_sem,
    collect_sem,
    seg_row_ref,
    seg_col_ref,
):
    dp, t = lax.axis_index("dp"), lax.axis_index("tensor")
    up, core = t // 2, lax.rem(t, 2)
    beside, over = (dp, up * 2 + 1 - core), (dp, (1 - up) * 2 + core)
    length, width = x_ref.shape
    blocks = length // BLK
    span = min(length // 2 + BLK, length)
    attn = heads * HD
    three = Total(dp, t, x3_ref, near3, mine3, far3, near_mine3, near_far3, sem3)
    one = Packs(three, o_own, o_beside, o_over, o_far, o_sem)
    outer = Packs(three, wo_own, wo_beside, wo_over, wo_far, wo_sem)
    greet([beside, over])
    seg_row_ref[...] = seg_in[...].astype(F32)
    by_block = jnp.concatenate([seg_row_ref[:, b * BLK : (b + 1) * BLK] for b in range(blocks)], axis=0)
    turned_seg = by_block.T
    for b in range(blocks):
        seg_col_ref[b * BLK : (b + 1) * BLK] = turned_seg[:, b : b + 1]

    def give(where, i):
        return remote(wf_ref, wf_ref, share_sem.at[i], share_sem.at[2], where)

    @pl.when(t == 0)
    def _():
        wf_ref[:, :HD] = wp_ref[:, :HD]
        wf_ref[:, HD:] = wp_ref[:, attn : attn + HD]
        give(over, 0).start()
        give(beside, 1).start()

    outer.pack(0, wo_ref[...])
    outer.send(0)

    def rows_of(b):
        return pl.ds(pl.multiple_of(b * BLK, BLK), BLK)

    gain_one, bias_one = norm_ref[0:1, :], norm_ref[1:2, :]
    gain_two, bias_two = norm_ref[2:3, :], norm_ref[3:4, :]
    wide = 2 * BLK

    def wide_rows(i):
        return pl.ds(pl.multiple_of(i * wide, wide), wide)

    def project(i, _):
        rows = wide_rows(i)
        plain, _ = plain_norm(x_ref[rows].astype(F32))
        a = (plain * gain_one + bias_one).astype(BF16)
        a_ref[rows] = a
        projected = dot(a, wp_ref[...], NN)
        for h in range(heads):
            qkv_ref[h, rows] = projected[:, h * HD : (h + 1) * HD].astype(BF16) * 0.125
        for h in range(heads, 3 * heads):
            qkv_ref[h, rows] = projected[:, h * HD : (h + 1) * HD].astype(BF16)
        return 0

    lax.fori_loop(0, length // wide, project, 0)

    @pl.when(t == 2)
    def _():
        give(over, 0).wait_recv()
        give(beside, 1).start()

    @pl.when((t == 1) | (t == 3))
    def _():
        give(beside, 1).wait_recv()

    def project_first(i, _):
        rows = wide_rows(i)
        projected = dot(a_ref[rows], wf_ref[...], NN)
        qkv_ref[3 * heads, rows] = projected[:, :HD].astype(BF16) * 0.125
        qkv_ref[3 * heads + 1, rows] = projected[:, HD:].astype(BF16)
        return 0

    lax.fori_loop(0, length // wide, project_first, 0)
    wf_out[...] = wf_ref[...]

    square_row = lax.broadcasted_iota(jnp.int32, (BLK, 2 * BLK), 0)
    square_col = lax.rem(lax.broadcasted_iota(jnp.int32, (BLK, 2 * BLK), 1), BLK)
    earlier = (square_col < square_row).astype(F32).astype(BF16)
    later = (square_col > square_row).astype(F32).astype(BF16)
    few = 32

    def every_block(one, backward):
        low = span // BLK - 1

        def early():
            for b in range(low)[:: -1 if backward else 1]:
                one(b, 0, (b + 1) * BLK)

        def rest():
            def step(i, _):
                b = blocks - 1 - i if backward else low + i
                one(b, pl.multiple_of((b - low) * BLK, BLK), span)
                return 0

            lax.fori_loop(0, blocks - low, step, 0)

        for part in (rest, early) if backward else (early, rest):
            part()

    def by_rows(b, one):
        def step(i, _):
            base = pl.multiple_of(i * few, few)
            one(pl.ds(base, few), pl.ds(pl.multiple_of(b * BLK + base, few), few), base)
            return 0

        lax.fori_loop(0, BLK // few, step, 0, unroll=True)

    def two_part(values, part, keys):
        high = values.astype(BF16)
        pick_scr[part, :keys] = high
        pick_scr[pl.ds(pl.multiple_of(part.start + BLK, few), few), :keys] = (
            values - high.astype(F32)
        ).astype(BF16)

    def behind(base, keys):
        row = lax.broadcasted_iota(jnp.int32, (few, keys), 0) + (base + keys - BLK)
        return row - lax.broadcasted_iota(jnp.int32, (few, keys), 1)

    carry_ref[...] = jnp.zeros_like(carry_ref)

    def attend(b, start, keys):
        rows, window = rows_of(b), pl.ds(start, keys)
        raw_scr[heads, :, :keys] = dot(qkv_ref[3 * heads, rows], qkv_ref[3 * heads + 1, window], NT)
        for h in range(heads):
            raw_scr[h, :, :keys] = dot(qkv_ref[h, rows], qkv_ref[heads + h, window], NT)
        seg_row = seg_row_ref[:, window]

        def pick(part, whole, base):
            first = raw_scr[heads, part, :keys] - shift
            small = jnp.exp(-jnp.abs(first))
            soft = jnp.maximum(first, 0.0) + jnp.log(1.0 + small)
            strict = (seg_col_ref[whole] == seg_row) & (behind(base, keys) > 0)
            two_part(jnp.where(strict, soft, 0.0), part, keys)
            share = jnp.where(first >= 0.0, 1.0, small) / (1.0 + small)
            sig_ref[whole, :keys] = jnp.where(strict, share, 0.0).astype(BF16)

        by_rows(b, pick)
        raw_scr[heads, :, :keys] = dot(earlier, pick_scr[:, :keys], NN)
        before = carry_ref[0:1, window]
        last = [pick_scr[end - few : end, :keys].astype(F32)[few - 1 :] for end in (BLK, 2 * BLK)]
        carry_ref[0:1, window] = before + raw_scr[heads, BLK - 1 : BLK, :keys] + (last[0] + last[1])

        def soften(part, whole, base):
            allowed = (seg_col_ref[whole] == seg_row) & (behind(base, keys) >= 0)
            penalty = jnp.where(allowed, raw_scr[heads, part, :keys] + before, 1e30).astype(BF16)
            pen_ref[whole, :keys] = penalty
            penalty = penalty.astype(F32)
            for h in range(heads):
                logits = raw_scr[h, part, :keys] - penalty
                top = jnp.max(logits, axis=-1, keepdims=True)
                weights = jnp.exp(logits - top)
                total = jnp.sum(weights, axis=-1, keepdims=True)
                lse_ref[whole, h : h + 1] = top + jnp.log(total)
                probs_scr[h, part, :keys] = (weights * (1.0 / total)).astype(BF16)

        by_rows(b, soften)
        mixed = [dot(probs_scr[h, :, :keys], qkv_ref[2 * heads + h, window], NN) for h in range(heads)]
        o = jnp.concatenate(mixed, axis=1).astype(BF16)
        o_ref[rows] = o
        one.pack(b, o)
        one.send(b)

    outer.relay(0)

    def mlp(b):
        one.arrived(b)
        rows = rows_of(b)
        one.lay(b, o_all, pl.ds(0, BLK))
        resid = x_ref[rows].astype(F32) + dot(o_all[...], wo_all[...], NT)
        resid_ref[rows] = resid
        plain, _ = plain_norm(resid)
        cn = (plain * gain_two + bias_two).astype(BF16)
        cn_ref[rows] = cn
        u = dot(cn, w1_ref[...], NN)
        root = math.sqrt(2.0 / math.pi)
        square = u * u
        bent = jnp.tanh(root * u * (1.0 + 0.044715 * square))
        half = 0.5 * (1.0 + bent)
        s_ref[rows] = (u * half).astype(BF16)
        slope = half + 0.5 * u * (1.0 - bent * bent) * (root * (1.0 + 3 * 0.044715 * square))
        du = (dot(dy_ref[rows], w2_ref[...], NN) * slope).astype(BF16)
        du_ref[rows] = du
        x3_ref[rows] = dot(du, w1_ref[...], NT).astype(BF16)
        three.enter(b)

    lag, turned_from = 3, blocks - 3

    def mlp_and_send(b):
        mlp(b)

        def before():
            three.add(b - 1)
            three.cross(b - 1)

        if isinstance(b, int):
            if 0 < b <= turned_from:
                before()
        else:
            pl.when((b > 0) & (b <= turned_from))(before)

    def forward(b, start, keys):
        attend(b, start, keys)
        if isinstance(b, int):
            if b == lag - 1:
                outer.arrived(0)
                outer.lay(0, wo_all, pl.ds(0, width))
            if b >= lag - 1:
                one.relay(b - lag + 1)
            if b >= lag:
                mlp_and_send(b - lag)
        else:
            one.relay(b - lag + 1)
            mlp_and_send(b - lag)

    every_block(forward, False)

    def forward_last(i, _):
        b = blocks - lag + i

        @pl.when(i < lag - 1)
        def _():
            one.relay(b + 1)

        mlp_and_send(b)
        return 0

    lax.fori_loop(0, lag, forward_last, 0)
    for b in reversed(range(turned_from, blocks)):
        three.add(b)
        three.cross(b)

    def mlp_out(i, _):
        rows = wide_rows(i)
        out_ref[rows] = dot(s_ref[rows], w2_ref[...], NT).astype(BF16)
        return 0

    lax.fori_loop(0, length // wide, mlp_out, 0)
    mat_ref[:, cuts[3] : cuts[4]] = dot(dy_ref[...], s_ref[...], TN).astype(BF16)
    mat_ref[:, cuts[1] : cuts[2]] = dot(cn_ref[...], du_ref[...], TN).astype(BF16)
    mat_ref[:, cuts[4] :] = jnp.zeros((width, mat_ref.shape[1] - cuts[4]), BF16)

    for early in range(turned_from):
        three.relay(early)
    three.relay(blocks - 1)
    ng_ref[...] = jnp.zeros_like(ng_ref)
    carry_ref[...] = jnp.zeros_like(carry_ref)
    dkv_ref[...] = jnp.zeros_like(dkv_ref)

    def back(b, start, keys):
        def ahead():
            three.relay(b - 1)

        if not isinstance(b, int):
            pl.when(b > turned_from)(ahead)
        elif b > turned_from:
            ahead()
        three.arrived(b)
        rows, window = rows_of(b), pl.ds(start, keys)
        plain, inverse_std = plain_norm(resid_ref[rows])
        d_two = three.sums(b)
        ng_ref[0:1, :] += jnp.sum(d_two * plain, axis=0, keepdims=True)
        ng_ref[1:2, :] += jnp.sum(d_two, axis=0, keepdims=True)
        dres = dy_ref[rows].astype(F32) + norm_back(plain, inverse_std, d_two * gain_two)
        dhb = dres.astype(BF16)
        dhb_ref[rows] = dhb
        do = dot(dhb, wo_ref[...], NN).astype(BF16)
        do = [do[:, h * HD : (h + 1) * HD] for h in range(heads)]
        for h in range(heads):
            raw_scr[h, :, :keys] = dot(qkv_ref[h, rows], qkv_ref[heads + h, window], NT)
            back_scr[h, :, :keys] = dot(do[h], qkv_ref[2 * heads + h, window], NT)

        def harden(part, whole, base):
            penalty = pen_ref[whole, :keys].astype(F32)
            total = None
            for h in range(heads):
                probs = jnp.exp(raw_scr[h, part, :keys] - penalty - lse_ref[whole, h : h + 1])
                dprobs = back_scr[h, part, :keys]
                inner = jnp.sum(dprobs * probs, axis=-1, keepdims=True)
                dlogits = probs * (dprobs - inner)
                probs_scr[h, part, :keys] = probs.astype(BF16)
                draw_scr[h, part, :keys] = dlogits.astype(BF16)
                total = dlogits if total is None else total + dlogits
            two_part(total, part, keys)

        by_rows(b, harden)
        raw_scr[heads, :, :keys] = dot(later, pick_scr[:, :keys], NN)
        after = carry_ref[0:1, window]
        top = [pick_scr[start_ : start_ + few, :keys].astype(F32)[:1] for start_ in (0, BLK)]
        carry_ref[0:1, window] = after + raw_scr[heads, 0:1, :keys] + (top[0] + top[1])

        def select(part, whole, base):
            suffix = raw_scr[heads, part, :keys] + after
            draw_scr[heads, part, :keys] = (sig_ref[whole, :keys].astype(F32) * -suffix).astype(BF16)

        by_rows(b, select)
        dq = []
        for h in range(heads):
            draw = draw_scr[h, :, :keys]
            dq.append(dot(draw, qkv_ref[heads + h, window], NN) * 0.125)
            dkv_ref[h * HD : (h + 1) * HD, window] += dot(qkv_ref[h, rows], draw, TN)
            dkv_ref[attn + h * HD : attn + (h + 1) * HD, window] += dot(do[h], probs_scr[h, :, :keys], TN)
        draw = draw_scr[heads, :, :keys]
        dq.append(dot(draw, qkv_ref[3 * heads + 1, window], NN) * 0.125)
        dkv_ref[2 * attn : 2 * attn + HD, window] += dot(qkv_ref[3 * heads, rows], draw, TN)
        dproj_ref[rows, :attn] = jnp.concatenate(dq[:heads], axis=1).astype(BF16)
        dproj_ref[rows, 3 * attn : 3 * attn + HD] = dq[heads].astype(BF16)

    every_block(back, True)
    dproj_ref[:, 3 * attn + HD : 3 * attn + 2 * HD] = dkv_ref[2 * attn :].T.astype(BF16)

    def collect(src, dst, where, i):
        return remote(src, dst, collect_sem.at[i], collect_sem.at[i + 2], where)

    gf_ref[...] = dot(a_ref[...], dproj_ref[:, 3 * attn :], TN).astype(BF16)

    @pl.when(core == 1)
    def _():
        collect(gf_ref, gf_near, beside, 0).start()

    @pl.when(core == 0)
    def _():
        collect(gf_ref, gf_near, beside, 0).wait_recv()
        gf_ref[...] = (gf_ref[...].astype(F32) + gf_near[...].astype(F32)).astype(BF16)

    @pl.when(t == 2)
    def _():
        collect(gf_ref, gf_far, over, 1).start()

    dproj_ref[:, attn : 3 * attn] = dkv_ref[: 2 * attn].T.astype(BF16)
    mat_ref[:, cuts[2] : cuts[3]] = dot(dhb_ref[...], o_ref[...], TN).astype(BF16)
    grad = dot(a_ref[...], dproj_ref[:, : 3 * attn], TN)
    mat_ref[:, : cuts[1]] = grad.astype(BF16)

    @pl.when(t == 0)
    def _():
        collect(gf_ref, gf_far, over, 1).wait_recv()
        extra = gf_ref[...].astype(F32) + gf_far[...].astype(F32)
        mat_ref[:, :HD] = (mat_ref[:, :HD].astype(F32) + extra[:, :HD]).astype(BF16)
        mat_ref[:, attn : attn + HD] = (mat_ref[:, attn : attn + HD].astype(F32) + extra[:, HD:]).astype(BF16)
        give(over, 0).wait_send()

    @pl.when(core == 0)
    def _():
        give(beside, 1).wait_send()

    @pl.when(core == 1)
    def _():
        collect(gf_ref, gf_near, beside, 0).wait_send()

    @pl.when(t == 2)
    def _():
        collect(gf_ref, gf_far, over, 1).wait_send()

    def close(b, _):
        one.close(b)
        three.close(b)
        return 0

    lax.fori_loop(0, blocks, close, 0)
    outer.close(0)


def layer(inputs, segments, cotangent, wp, w1, wo, w2, norms, block):
    length, width = inputs.shape
    attn, hidden = wo.shape[1], w1.shape[1]
    heads = attn // HD
    rows, cols = width // block, 4 * attn // block + 2 * (hidden // block)
    cuts = piece_cuts(rows, cols, width // attn)
    blocks = length // BLK
    span = min(length // 2 + BLK, length)

    def low(*shape):
        return pltpu.VMEM(shape, BF16)

    half = length // 2
    total = [low(length, width)] + [low(half, width)] * 5 + [pltpu.SemaphoreType.DMA((8, blocks))]

    def out(shape, dtype):
        return jax.ShapeDtypeStruct(shape, dtype)

    return pl.pallas_call(
        functools.partial(layer_kernel, heads, shift_for(length), [cut * block for cut in cuts]),
        out_shape=[
            out((width, cols * block + 128), BF16),
            out((length, width), BF16),
            out((length, 3 * attn + 2 * HD), BF16),
            out((width, 2 * HD), BF16),
            out((length, width), BF16),
            out((length, width), F32),
            out((2, width), F32),
        ],
        in_specs=[VM] * 8,
        out_specs=[VM] * 7,
        scratch_shapes=[
            low(length, width),
            low(width, 2 * HD),
            low(3 * heads + 2, length, HD),
            low(length, span),
            low(length, span),
            pltpu.VMEM((length, 8), F32),
            low(length, attn),
            low(length, width),
            low(length, hidden),
            low(length, hidden),
            pltpu.VMEM((2 * attn + HD, length), F32),
            pltpu.VMEM((8, length), F32),
            pltpu.VMEM((heads + 1, BLK, span), F32),
            pltpu.VMEM((heads, BLK, span), F32),
            low(heads, BLK, span),
            low(heads + 1, BLK, span),
            low(2 * BLK, span),
        ]
        + [low(blocks, attn, BLK)] * 4
        + [pltpu.SemaphoreType.DMA((6, blocks)), low(BLK, width)]
        + [low(1, width + width // 2, BLK)] * 4
        + [pltpu.SemaphoreType.DMA((6, 1)), low(width, width)]
        + total
        + [low(width, 2 * HD)] * 3
        + [pltpu.SemaphoreType.DMA((3,)), pltpu.SemaphoreType.DMA((4,))]
        + [pltpu.VMEM((1, length), F32), pltpu.VMEM((length, 1), F32)],
        compiler_params=pltpu.CompilerParams(
            collective_id=3, has_side_effects=True, vmem_limit_bytes=LAYER_LIMIT
        ),
        name="layer",
        cost_estimate=pl.CostEstimate(flops=0, bytes_accessed=221000000, transcendentals=0),
    )(
        inputs,
        segments.reshape(1, length),
        cotangent,
        wp,
        w1,
        wo,
        w2,
        norms,
    )


def settle_kernel(
    n,
    count,
    inverse_ref,
    mat_ref,
    out_in,
    dproj_ref,
    wp_ref,
    wf_ref,
    dhb_ref,
    resid_ref,
    x_ref,
    norm_ref,
    ng_in,
    g_ref,
    output_ref,
    grad_ref,
    ng_ref,
    p_ref,
    u_scr,
    xin,
    lin,
    rin,
    x_send,
    x_recv,
    l_send,
    l_recv,
    r_send,
    r_recv,
    near4,
    mine4,
    far4,
    near_mine4,
    near_far4,
    sem4,
    near2,
    mine2,
    far2,
    near_mine2,
    near_far2,
    sem2,
    norm_held,
    norm_send,
    norm_recv,
    da_scr,
):
    m = n // 2
    dp, t = lax.axis_index("dp"), lax.axis_index("tensor")
    place, side = dp // 2, lax.rem(dp, 2)
    pair = (place * 2 + 1 - side, t)
    four = Total(dp, t, da_scr, near4, mine4, far4, near_mine4, near_far4, sem4)
    two = Total(dp, t, out_in, near2, mine2, far2, near_mine2, near_far2, sem2)
    blocks = four.blocks
    peers = [lax.rem(dp + hop, n) for hop in range(1, n)]
    size, wide = p_ref.shape[1:]
    cols = (mat_ref.shape[1] - 128) // size

    def chop(row, _):
        whole_row = mat_ref[pl.ds(pl.multiple_of(row * size, size), size), :]
        for c in range(cols):
            u_scr[row * cols + c] = whole_row[:, c * size : (c + 1) * size]
        return 0

    lax.fori_loop(0, mat_ref.shape[0] // size, chop, 0, unroll=2)
    greet([four.beside, four.over] + [(peer, t) for peer in peers])

    middle = wide // 256 * 128
    parts = ((0, middle), (middle, wide))

    def piece(ref, part):
        first, last = parts[part]
        return ref.at[:, first:last]

    def across(q, part):
        src, dst = p_ref.at[q * 2 + 1 - side], xin.at[q]
        return remote(piece(src, part), piece(dst, part), x_send.at[q, part], x_recv.at[q, part], pair)

    def rightward(q, part):
        ref = piece(lin.at[q], part)
        return remote(ref, ref, r_send.at[q, part], l_recv.at[q, part], (dp + 2, t))

    def leftward(q, part):
        ref = piece(rin.at[q], part)
        return remote(ref, ref, l_send.at[q, part], r_recv.at[q, part], (dp - 2, t))

    def both(hop, one):
        @pl.when(place + hop < m)
        def _():
            one(place + hop, True)

        if hop > 0:
            @pl.when(place - hop >= 0)
            def _():
                one(place - hop, False)

    def work(q, right):
        lay(q * 2 + side)
        for part in (0, 1):
            first, last = parts[part]
            across(q, part).wait_recv()
            own = p_ref[q * 2 + side, :, first:last].astype(F32) + xin[q, :, first:last].astype(F32)
            line, pass_on, is_end = (lin, rightward, place == 0) if right else (rin, leftward, place == m - 1)

            @pl.when(jnp.logical_not(is_end))
            def _():
                pass_on(q, part).wait_recv()
                line[q, :, first:last] = (own + line[q, :, first:last].astype(F32)).astype(BF16)

            @pl.when(is_end)
            def _():
                line[q, :, first:last] = own.astype(BF16)

            pass_on(q, part).start()

    def keep():
        q = place
        lay(q * 2 + side)
        for part in (0, 1):
            first, last = parts[part]
            across(q, part).wait_recv()
            g_ref[:, first:last] = p_ref[q * 2 + side, :, first:last].astype(F32) + xin[q, :, first:last].astype(F32)

            @pl.when(place > 0)
            def _():
                rightward(q, part).wait_recv()
                g_ref[:, first:last] += lin[q, :, first:last].astype(F32)

            @pl.when(place < m - 1)
            def _():
                leftward(q, part).wait_recv()
                g_ref[:, first:last] += rin[q, :, first:last].astype(F32)

    def norm_copy(peer):
        return remote(ng_ref, norm_held.at[dp], norm_send.at[peer], norm_recv.at[dp], (peer, t))

    def norm_from(peer):
        return remote(ng_ref, norm_held.at[peer], norm_send.at[peer], norm_recv.at[peer], (peer, t))

    some = math.gcd(count, 8)
    room = tiles_up(some * size) // 128

    def strip(base):
        return jnp.concatenate([u_scr[inverse_ref[base + e]] for e in range(some)], axis=1)

    def lay(d):
        if some * size == room * 128:
            def one(g, _):
                place = pl.ds(pl.multiple_of(g * room * 128, 128), room * 128)
                p_ref[d, :, place] = strip(d * count + g * some)
                return 0

            lax.fori_loop(0, count // some, one, 0, unroll=6)
        else:
            parts = [strip(d * count + g * some)[:, : some * size] for g in range(count // some)]
            if wide > count * size:
                parts.append(jnp.zeros((size, wide - count * size), BF16))
            p_ref[d] = jnp.concatenate(parts, axis=1)

    def give(q, right):
        lay(q * 2 + 1 - side)
        across(q, 0).start()
        across(q, 1).start()

    cut = wp_ref.shape[1]

    def project_back(b):
        rows = pl.ds(b * four.size, four.size)
        da = dot(dproj_ref[rows, :cut], wp_ref[...], NT)
        da_scr[rows] = (da + dot(dproj_ref[rows, cut:], wf_ref[...], NT)).astype(BF16)
        four.enter(b)

    for step, hop in enumerate(reversed(range(m))):
        both(hop, give)
        if step == 0:
            for b in range(blocks):
                project_back(b)
        if step == 1:
            for b in range(blocks):
                four.add(b)
                four.cross(b)
                two.enter(b)
    for b in range(blocks):
        two.add(b)
        two.cross(b)

    ng_ref[...] = jnp.zeros_like(ng_ref)
    gain = norm_ref[0:1, :]

    def rows_of(b):
        return pl.ds(b * four.size, four.size)

    def grad_block(b):
        rows = rows_of(b)
        four.arrived(b)
        d_one = four.sums(b)
        plain, inverse_std = plain_norm(x_ref[rows].astype(F32))
        ng_ref[0:1, :] += jnp.sum(d_one * plain, axis=0, keepdims=True)
        ng_ref[1:2, :] += jnp.sum(d_one, axis=0, keepdims=True)
        grad_ref[rows] = dhb_ref[rows].astype(F32) + norm_back(plain, inverse_std, d_one * gain)

    def out_block(b):
        rows = rows_of(b)
        two.arrived(b)
        output_ref[rows] = (resid_ref[rows] + two.sums(b)).astype(BF16)

    def norms_out():
        ng_ref[2:4, :] = ng_in[...]
        for peer in peers:
            norm_copy(peer).start()

    def norms_in():
        for peer in peers:
            norm_from(peer).wait_recv()
        total = None
        for source in range(n):
            term = jnp.where(dp == source, ng_ref[...], norm_held[source])
            total = term if total is None else total + term
        for peer in peers:
            norm_copy(peer).wait_send()
        ng_ref[...] = total

    tasks = []
    for b in range(blocks):
        tasks.append(functools.partial(four.relay, b))
        if b > 0:
            tasks.append(functools.partial(grad_block, b - 1))
    tasks.append(functools.partial(grad_block, blocks - 1))
    tasks.append(norms_out)
    for b in range(blocks):
        tasks.append(functools.partial(two.relay, b))
        if b > 0:
            tasks.append(functools.partial(out_block, b - 1))
    tasks.append(functools.partial(out_block, blocks - 1))
    done = 0
    for step, hop in enumerate(reversed(range(1, m))):
        until = min((1, 10, 18, len(tasks))[min(step, 3)], len(tasks))
        while done < until:
            tasks[done]()
            done += 1
        both(hop, work)
    while done < len(tasks):
        tasks[done]()
        done += 1
    keep()
    norms_in()

    def finish(q, _):
        for part in (0, 1):
            across(q, part).wait_send()

            @pl.when(q > place)
            def _():
                rightward(q, part).wait_send()

            @pl.when(q < place)
            def _():
                leftward(q, part).wait_send()

        return 0

    lax.fori_loop(0, m, finish, 0)
    for b in range(blocks):
        four.close(b)
        two.close(b)


def settle(inverse, matrix, block, out_part, dproj, wp, wf, dhb, resid, inputs, norms, ng, n):
    count = matrix.shape[0] // block * ((matrix.shape[1] - 128) // block) // n
    wide = tiles_up(count * block)
    m = n // 2
    length, width = inputs.shape
    blocks = 8

    def low(*shape):
        return pltpu.VMEM(shape, BF16)

    half = length // 2
    total = [low(half, width)] * 5 + [pltpu.SemaphoreType.DMA((8, blocks))]
    return pl.pallas_call(
        functools.partial(settle_kernel, n, count),
        out_shape=[
            jax.ShapeDtypeStruct((block, wide), F32),
            jax.ShapeDtypeStruct((length, width), BF16),
            jax.ShapeDtypeStruct((length, width), F32),
            jax.ShapeDtypeStruct((4, width), F32),
        ],
        in_specs=[pl.BlockSpec(memory_space=pltpu.SMEM)] + [VM] * 10,
        out_specs=[VM] * 4,
        scratch_shapes=[low(n, block, wide), low(n * count, block, block)]
        + [low(m, block, wide)] * 3
        + [pltpu.SemaphoreType.DMA((m, 2))] * 6
        + total
        + total
        + [pltpu.VMEM((n, 4, width), F32), pltpu.SemaphoreType.DMA((n,)), pltpu.SemaphoreType.DMA((n,))]
        + [low(length, width)],
        compiler_params=pltpu.CompilerParams(
            collective_id=2, has_side_effects=True, vmem_limit_bytes=SETTLE_LIMIT
        ),
        name="settle",
        cost_estimate=pl.CostEstimate(flops=0, bytes_accessed=187000000, transcendentals=0),
    )(inverse, matrix, out_part, dproj, wp, wf, dhb, resid, inputs, norms, ng)


def norm_update(grad, master, first, second):
    new_first = beta_one * first + (1.0 - beta_one) * grad
    new_second = beta_two * second + (1.0 - beta_two) * grad * grad
    direction = (
        new_first
        / (1.0 - beta_one**STEP)
        / (jnp.sqrt(new_second / (1.0 - beta_two**STEP)) + adam_eps)
    )
    return (new_first, new_second, master - norm_rate * direction)


def body(
    inputs,
    segments,
    cotangent,
    owner,
    masters,
    first_moment,
    second_moment,
    left_stats,
    right_stats,
    left_basis,
    right_basis,
    norm_master,
    norm_first,
    norm_second,
):
    length = inputs.shape[1]
    width = inputs.shape[2]
    n_dp = lax.axis_size("dp")
    parts = lax.axis_size("tensor")
    block = masters.shape[-1]
    slots, inverse = lax.optimization_barrier(block_slots(owner))
    pieces, norms = gather_masters(
        slots, masters[0], norm_master, n_dp, width // block, parts
    )
    grad_matrix, out_part, dproj, w_first, dhb, resid, norm_grads = layer(
        inputs[0], segments[0], cotangent[0], *pieces, norms, block
    )
    own_packed, output, input_grad, norm_grads = settle(
        inverse,
        grad_matrix,
        block,
        out_part,
        dproj,
        pieces[0],
        w_first,
        dhb,
        resid,
        inputs[0],
        norms,
        norm_grads,
        n_dp,
    )
    *updated, output, input_grad = soap(
        own_packed,
        output,
        input_grad,
        masters[0],
        first_moment[0],
        second_moment[0],
        left_stats[0],
        right_stats[0],
        left_basis[0],
        right_basis[0],
    )
    norm_grads, output = lax.optimization_barrier((norm_grads, output))
    norm_per = norm_master.shape[0]
    own_norm_grads = lax.dynamic_slice_in_dim(
        norm_grads.reshape(-1), lax.axis_index("dp") * norm_per, norm_per
    )
    norm_first_new, norm_second_new, norm_new = norm_update(
        own_norm_grads, norm_master, norm_first, norm_second
    )
    return (
        output[None],
        input_grad[None],
        *[item[None] for item in updated],
        norm_first_new,
        norm_second_new,
        norm_new,
    )


def solution(mesh):
    in_specs = (
        P("dp", None, None),
        P("dp", None),
        P("dp", None, None),
        P(),
        P("tensor", "dp", None, None),
        P("tensor", "dp", None, None),
        P("tensor", "dp", None, None),
        P("tensor", "dp", None, None),
        P("tensor", "dp", None, None),
        P("tensor", "dp", None, None),
        P("tensor", "dp", None, None),
        P("dp"),
        P("dp"),
        P("dp"),
    )
    out_specs = (
        P("dp", None, None),
        P("dp", None, None),
        P("tensor", "dp", None, None),
        P("tensor", "dp", None, None),
        P("tensor", "dp", None, None),
        P("tensor", "dp", None, None),
        P("tensor", "dp", None, None),
        P("tensor", "dp", None, None),
        P("tensor", "dp", None, None),
        P("dp"),
        P("dp"),
        P("dp"),
    )
    return jax.shard_map(body, mesh=mesh, in_specs=in_specs, out_specs=out_specs, check_vma=False)
```
